32 devices in a mesh: dp: 4 (over z), seq: 8 (over y, x, core).
Axes of the slice: x: 2, y: 2, z: 4, core: 2. Of those that a mesh axis runs over, the one named last changes fastest.
Arguments:
- inputs: bfloat16 [32, 1024, 512], P('dp', 'seq'), may hold values from -6 to 6
- doc_start: int32 [32, 1024], P('dp', 'seq'), may hold values from 0 to 1, as said below
- norm1_gain: float32 [512], replicated, may hold values from 0.5 to 1.5
- conv_weight: float32 [512, 4], replicated, may hold values from -3 to 3
- gate_bias: float32 [1024], replicated, may hold values from -20 to -2
- w_in: bfloat16 [512, 2048], replicated, may hold values from -0.25 to 0.25
- w_out: bfloat16 [1024, 512], replicated, may hold values from -3 to 3
- norm2_gain: float32 [512], replicated, may hold values from 0.5 to 1.5
- w_up: bfloat16 [512, 2048], replicated, may hold values from -0.25 to 0.25
- w_down: bfloat16 [2048, 512], replicated, may hold values from -0.125 to 0.125
- out_grad: bfloat16 [32, 1024, 512], P('dp', 'seq'), may hold values from -6 to 6
Outputs:
- result: bfloat16 [32, 1024, 512], P('dp', 'seq')
- grad_inputs: float32 [32, 1024, 512], P('dp', 'seq')
- grad_norm1: float32 [512], P('seq')
- grad_conv: float32 [512, 4], P('seq')
- grad_bias: float32 [1024], P('seq')
- grad_w_in: float32 [512, 2048], P('seq')
- grad_w_out: float32 [1024, 512], P('seq')
- grad_norm2: float32 [512], P('seq')
- grad_w_up: float32 [512, 2048], P('seq')
- grad_w_down: float32 [2048, 512], P('seq')
The draws below stay inside these ranges and needn't reach their ends.
Inputs may be any that keep to these rules, and one draw needn't show every extreme that they name: `doc_start`: each row's first token is 1. In every aligned block of 8 rows, one row drawn from the seed holds a single document over all 1024 tokens. In the other rows every later token begins a document independently with chance 1 / 384, so such a row holds documents of random, uneven lengths, or now and then a single one.
All inputs are finite; a program needn't handle non-finite values.
Results may differ from the reference program's by a relative error of at most 0.0085.
Values may be sent and summed in bfloat16 or wider, within the bound.
No kernel may reach another device: no remote copies, remote signals or barrier semaphores. Data moves between devices by JAX's collectives and lax.ppermute only.
A program may use at most 192 MiB of HBM per device.

```python
import jax
import jax.numpy as jnp
from jax import lax

D = 512
H = 1024
FF = 2048
KW = 4
SPAN = 128
ROWS_DEV = 8
L = 1024
ROWS = 32


def draw_doc_start(key, part):
    key_marks = jax.random.fold_in(key, 11)
    key_whole = jax.random.fold_in(key, 12)
    marks = (jax.random.randint(key_marks, (ROWS, L), 0, 3 * SPAN) == 0).astype(jnp.int32)
    chosen = jax.random.randint(key_whole, (ROWS // ROWS_DEV,), 0, ROWS_DEV)
    row_ids = jnp.arange(ROWS)
    whole_row = row_ids % ROWS_DEV == chosen[row_ids // ROWS_DEV]
    marks = jnp.where(whole_row[:, None], 0, marks)
    first_col = (jnp.arange(L) == 0).astype(jnp.int32)
    return jnp.maximum(marks, first_col[None, :])


def draw_gate_bias(key, part):
    key_pick = jax.random.fold_in(key, 21)
    key_slow = jax.random.fold_in(key, 22)
    key_fast = jax.random.fold_in(key, 23)
    share = 0.5
    slow_pick = jax.random.uniform(key_pick, (H,), jnp.float32) < share
    slow_rate = jnp.exp(jax.random.uniform(key_slow, (H,), jnp.float32, jnp.log(0.05), jnp.log(1.5))) / L
    fast_rate = jnp.exp(jax.random.uniform(key_fast, (H,), jnp.float32, jnp.log(2.0), jnp.log(L / 30.0))) / L
    rate_val = jnp.where(slow_pick, slow_rate, fast_rate)
    return jnp.log(rate_val / (1.0 - rate_val))


def block_scale(key, dims, shards, smallest, high):
    factor_of = 1.0
    for axis_at, parts in shards:
        steps = jax.random.uniform(jax.random.fold_in(jax.random.fold_in(key, 6), axis_at), (parts,), jnp.float32, smallest / len(shards), high / len(shards))
        factor_of = factor_of * jnp.repeat(jnp.exp(steps), dims[axis_at] // parts).reshape((-1,) + (1,) * (len(dims) - 1 - axis_at))
    return factor_of


def bell_draw(key, dims, scale, most, split=(), kind=jnp.bfloat16):
    result = scale * jax.random.normal(key, dims, jnp.float32)
    if split:
        result = result * block_scale(key, dims, split, -0.22, 0.18)
    return jnp.clip(result, -most, most).astype(kind)


def setup_inputs(seed: int = 0) -> dict:
    seeds = jax.random.split(jax.random.key(seed), 12)
    inputs = bell_draw(seeds[0], (ROWS, L, D), 1.0, 6.0, ((0, 4), (1, 8)))
    doc_start = draw_doc_start(jax.random.fold_in(seeds[11], 71), 0)
    norm1_gain = jnp.clip(1.0 + 0.1 * jax.random.normal(seeds[2], (D,), jnp.float32), 0.5, 1.5)
    conv_weight = bell_draw(seeds[3], (D, KW), KW ** -0.5, 3.0, (), jnp.float32)
    gate_bias = draw_gate_bias(jax.random.fold_in(seeds[11], 71), 0)
    w_in = bell_draw(seeds[5], (D, 2 * H), D ** -0.5, 0.25)
    w_out = bell_draw(seeds[6], (H, D), 4 ** -0.5, 3.0)
    norm2_gain = jnp.clip(1.0 + 0.1 * jax.random.normal(seeds[7], (D,), jnp.float32), 0.5, 1.5)
    w_up = bell_draw(seeds[8], (D, FF), D ** -0.5, 0.25)
    w_down = bell_draw(seeds[9], (FF, D), FF ** -0.5, 0.125)
    out_grad = bell_draw(seeds[10], (ROWS, L, D), 1.0, 6.0, ((0, 4), (1, 8)))
    return {"inputs": inputs, "doc_start": doc_start, "norm1_gain": norm1_gain, "conv_weight": conv_weight, "gate_bias": gate_bias, "w_in": w_in, "w_out": w_out, "norm2_gain": norm2_gain, "w_up": w_up, "w_down": w_down, "out_grad": out_grad}


@jax.custom_vjp
def low(v):
    return lax.optimization_barrier(v.astype(jnp.bfloat16)).astype(jnp.float32)

@jax.custom_vjp
def low_back(v):
    return v

def low_keep(v):
    return (low(v), None)

def low_pass(kept, grad):
    return (grad,)

def back_keep(v):
    return (v, None)

def back_low(kept, grad):
    return (low(grad),)
low.defvjp(low_keep, low_pass)
low_back.defvjp(back_keep, back_low)
epsilon = 1e-05

def product(left_side, right_side):
    return jnp.dot(left_side, right_side, precision=lax.Precision.HIGHEST, preferred_element_type=jnp.float32)

def rms_scale(values, gain):
    return values * lax.rsqrt(lax.optimization_barrier(jnp.mean(values * values, axis=-1, keepdims=True)) + epsilon) * gain

def block_row(input_row, keep_mask, norm1_gain, conv_weight, gate_bias, w_in, w_out, norm2_gain, w_up, w_down):
    normed = low(rms_scale(input_row, norm1_gain))
    padded = jnp.concatenate([jnp.zeros((KW - 1, D), jnp.float32), normed], 0)
    mixing = padded[KW - 1:] * conv_weight[:, 0]
    for tap in range(1, KW):
        mixing = mixing + padded[KW - 1 - tap:KW - 1 - tap + L] * conv_weight[:, tap]
    conv_out = low(low_back(mixing))
    projected = low_back(product(conv_out, w_in))
    gate_val = jax.nn.sigmoid(projected[:, :H] + gate_bias)
    candidate = projected[:, H:]
    decay_rate = (1.0 - gate_val) * keep_mask[:, None]
    drive_term = gate_val * candidate

    def advance(hidden, step_pair):
        hidden = step_pair[0] * hidden + step_pair[1]
        return (hidden, hidden)
    last_state, states = lax.scan(advance, jnp.zeros((H,), jnp.float32), (decay_rate, drive_term))
    branch = low_back(product(low(states), w_out))
    middle = input_row + branch
    normed_mid = low(rms_scale(middle, norm2_gain))
    up_proj = low_back(product(normed_mid, w_up))
    activated = low(jax.nn.gelu(up_proj, approximate=True))
    return middle + low_back(product(activated, w_down))

def reference(inputs, doc_start, norm1_gain, conv_weight, gate_bias, w_in, w_out, norm2_gain, w_up, w_down, out_grad):
    weights = (norm1_gain, conv_weight, gate_bias, w_in.astype(jnp.float32), w_out.astype(jnp.float32), norm2_gain, w_up.astype(jnp.float32), w_down.astype(jnp.float32))

    def one_row(totals, row_item):
        input_row, start_row, grad_row = row_item
        keep_mask = 1.0 - start_row.astype(jnp.float32)

        def forward(values_in, *params):
            return block_row(values_in, keep_mask, *params)
        primal, pull_back = jax.vjp(forward, input_row.astype(jnp.float32), *weights)
        gradients = pull_back(grad_row.astype(jnp.float32))
        totals = tuple((total + added for total, added in zip(totals, gradients[1:])))
        return (totals, (primal.astype(jnp.bfloat16), gradients[0]))
    zero_grads = tuple((jnp.zeros(weight.shape, jnp.float32) for weight in weights))
    totals, outputs = lax.scan(one_row, zero_grads, (inputs, doc_start, out_grad))
    return (outputs[0], outputs[1], totals[0], totals[1], totals[2], totals[3], totals[4], totals[5], totals[6], totals[7])
```

```python
import functools

import jax
import jax.numpy as jnp
from jax import lax
from jax.experimental import pallas as pl
from jax.experimental.pallas import tpu as pltpu
from jax.sharding import PartitionSpec as P

KW = 4
EPS = 1e-05
EDGE = 8
LANES = 128
LIMITS = (16, 30, 16, 16, 24)
F32 = jnp.float32
BF16 = jnp.bfloat16
GELU_C = 0.7978845608028654
GELU_A = 0.044715

VMEM_SPEC = pl.BlockSpec(memory_space=pltpu.VMEM)
SMEM_SPEC = pl.BlockSpec(memory_space=pltpu.SMEM)


def dot(left, right):
    return jnp.dot(left, right, preferred_element_type=F32)


def dot_nt(left, right):
    return lax.dot_general(left, right, (((1,), (1,)), ((), ())), preferred_element_type=F32)


def dot_tn(left, right):
    return lax.dot_general(left, right, (((0,), (0,)), ((), ())), preferred_element_type=F32)


def widen(column, lanes):
    return jnp.concatenate([column] * (lanes // column.shape[1]), axis=1)


def rms(values):
    return lax.rsqrt(jnp.mean(values * values, axis=-1, keepdims=True) + EPS)


def rows_of(index, count):
    return pl.ds(pl.multiple_of(index * count, count), count)


def interleave(buf, row, batch, values):
    for lane in range(buf.shape[0]):
        cols = slice(lane * LANES, (lane + 1) * LANES)
        buf[lane, pl.ds(row, values.shape[0], stride=batch), :] = values[:, cols].astype(F32)


def deinterleave(buf, row, batch, span):
    parts = [buf[lane, pl.ds(row, span, stride=batch), :] for lane in range(buf.shape[0])]
    return jnp.concatenate(parts, axis=1)


def read(buf, rows):
    return jnp.concatenate([buf[lane, rows, :] for lane in range(buf.shape[0])], axis=1)


def write(buf, rows, values):
    for lane in range(buf.shape[0]):
        buf[lane, rows, :] = values[:, lane * LANES : (lane + 1) * LANES]


def front_kernel(
    x_ref, halo_ref, keep_ref, gain_ref, taps_ref, bias_ref, w_ref,
    xt_ref, conv_ref, gate_ref, cand_ref, total_ref, norm_buf,
    *, steps,
):
    batch, span, width = x_ref.shape
    hidden = gate_ref.shape[1]
    size = steps * batch
    lead = EDGE * batch
    for row in range(batch):
        interleave(norm_buf, row, batch, halo_ref[row])
        interleave(xt_ref, row, batch, x_ref[row])
    gain = gain_ref[...]

    def normed_of(values):
        return (values * rms(values) * gain).astype(BF16).astype(F32)

    write(norm_buf, slice(0, lead), normed_of(read(norm_buf, slice(0, lead))))

    def chunk(index, carry):
        rows = rows_of(index, size)
        here = normed_of(read(xt_ref, rows))
        write(norm_buf, pl.ds(pl.multiple_of(index * size + lead, 8), size), here)
        mixing = here * taps_ref[0:1, :]
        for tap in range(1, KW):
            start = pl.multiple_of(index * size + lead - tap * batch, 8)
            mixing = mixing + read(norm_buf, pl.ds(start, size)) * taps_ref[tap : tap + 1, :]
        conv_low = mixing.astype(BF16)
        conv_ref[rows, :] = conv_low
        gate_ref[rows, :] = jax.nn.sigmoid(dot(conv_low, w_ref[:, :hidden]) + bias_ref[...])
        cand_ref[rows, :] = dot(conv_low, w_ref[:, hidden:])

        def step(offset, carry):
            prod, state = carry
            here = rows_of(index * steps + offset, batch)
            gate = gate_ref[here, :]
            decay = (1.0 - gate) * widen(keep_ref[here, :], hidden)
            return decay * prod, decay * state + gate * cand_ref[here, :]

        return lax.fori_loop(0, steps, step, carry, unroll=8)

    first = (jnp.ones((batch, hidden), F32), jnp.zeros((batch, hidden), F32))
    prod, state = lax.fori_loop(0, span // steps, chunk, first)
    total_ref[0] = prod
    total_ref[1] = state


def middle_kernel(
    place_ref, totals_ref, g_ref, xt_ref, keep_ref, gate_ref, cand_ref, gain_ref,
    w_out_ref, w_up_ref, w_down_ref,
    result_ref, gt_ref, prev_ref, held_ref, nmid_ref, act_ref, gup_ref, gmid_ref, gbranch_ref, gheld_ref,
    outgoing_ref, gnorm2_ref, wide_buf,
    *, steps, block,
):
    batch, span, width = g_ref.shape
    hidden = gate_ref.shape[1]
    inner = w_up_ref.shape[1]
    size = steps * batch
    place = place_ref[0]
    for row in range(batch):
        interleave(wide_buf, row, batch, g_ref[row])

    def fold(source, state):
        return jnp.where(source < place, totals_ref[source, 0] * state + totals_ref[source, 1], state)

    carry_in = lax.fori_loop(0, totals_ref.shape[0], fold, jnp.zeros((batch, hidden), F32))
    gain = gain_ref[...]

    def chunk(index, carry):
        state, gnorm2 = carry
        rows = rows_of(index, size)

        def two_steps(pair, state):
            out = []
            for side in range(2):
                here = pl.ds(pl.multiple_of((index * steps + 2 * pair + side) * batch, batch), batch)
                gate = gate_ref[here, :]
                prev_ref[here, :] = state
                decay = (1.0 - gate) * widen(keep_ref[here, :], hidden)
                state = decay * state + gate * cand_ref[here, :]
                out.append(state)
            both = rows_of(index * (steps // 2) + pair, 2 * batch)
            held_ref[both, :] = jnp.concatenate(out, axis=0).astype(BF16)
            return state

        state = lax.fori_loop(0, steps // 2, two_steps, state, unroll=4)
        middle = read(xt_ref, rows) + dot(held_ref[rows, :], w_out_ref[...])
        scale = rms(middle)
        unit = middle * scale
        nmid = (unit * gain).astype(BF16)
        nmid_ref[rows, :] = nmid
        g_wide = read(wide_buf, rows)
        g_low = g_wide.astype(BF16)
        gt_ref[rows, :] = g_low
        result = middle
        gnmid = jnp.zeros((size, width), F32)
        for part in range(inner // block):
            cols = slice(part * block, (part + 1) * block)
            up = dot(nmid, w_up_ref[:, cols])
            gact = dot_nt(g_low, w_down_ref[cols, :])
            square = up * up
            half = 0.5 + 0.5 * jnp.tanh(up * (GELU_C + (GELU_C * GELU_A) * square))
            act = up * half
            slope = half + act * (1.0 - half) * (2.0 * GELU_C + (6.0 * GELU_C * GELU_A) * square)
            act_low = act.astype(BF16)
            gup = (slope * gact).astype(BF16)
            act_ref[rows, cols] = act_low
            gup_ref[rows, cols] = gup
            result = result + dot(act_low, w_down_ref[cols, :])
            gnmid = gnmid + dot_nt(gup, w_up_ref[:, cols])
        write(wide_buf, rows, result)
        gnorm2 = gnorm2 + jnp.sum(gnmid * unit, axis=0, keepdims=True)
        pulled = gnmid * gain
        gmid = g_wide + scale * (pulled - unit * jnp.mean(pulled * unit, axis=-1, keepdims=True))
        gmid_ref[rows, :] = gmid
        gbranch = gmid.astype(BF16)
        gbranch_ref[rows, :] = gbranch
        gheld_ref[rows, :] = dot_nt(gbranch, w_out_ref[...])
        return state, gnorm2

    _, gnorm2 = lax.fori_loop(0, span // steps, chunk, (carry_in, jnp.zeros((1, width), F32)))
    gnorm2_ref[...] = gnorm2

    def back(offset, carry):
        here = rows_of(span - 1 - offset, batch)
        decay = (1.0 - gate_ref[here, :]) * widen(keep_ref[here, :], hidden)
        return decay * (gheld_ref[here, :] + carry)

    outgoing_ref[...] = lax.fori_loop(0, span, back, jnp.zeros((batch, hidden), F32), unroll=8)
    for row in range(batch):
        result_ref[row] = deinterleave(wide_buf, row, batch, span).astype(BF16)


def back_kernel(
    place_ref, totals_ref, outs_ref, keep_ref, gate_ref, cand_ref, prev_ref, gheld_ref, conv_ref,
    gproj_ref, gbias_ref, stay_ref, send_ref,
):
    count, batch, hidden = outs_ref.shape
    span = gate_ref.shape[0] // batch
    place = place_ref[0]

    def fold(offset, state):
        source = count - 1 - offset
        return jnp.where(source > place, totals_ref[source, 0] * state + outs_ref[source], state)

    carry_in = lax.fori_loop(0, count, fold, jnp.zeros((batch, hidden), F32))

    def two_steps(offset, carry):
        arriving, gbias = carry
        pair = span // 2 - 1 - offset
        logits = [None, None]
        cands = [None, None]
        for side in (1, 0):
            here = pl.ds(pl.multiple_of((2 * pair + side) * batch, batch), batch)
            gate = gate_ref[here, :]
            keep = widen(keep_ref[here, :], hidden)
            gstate = gheld_ref[here, :] + arriving
            rest = 1.0 - gate
            cands[side] = gstate * gate
            logits[side] = cands[side] * (cand_ref[here, :] - prev_ref[here, :] * keep) * rest
            arriving = rest * keep * gstate
            gbias = gbias + logits[side]
        both = rows_of(pair, 2 * batch)
        gproj_ref[both, :hidden] = jnp.concatenate(logits, axis=0).astype(BF16)
        gproj_ref[both, hidden:] = jnp.concatenate(cands, axis=0).astype(BF16)
        return arriving, gbias

    _, gbias = lax.fori_loop(
        0, span // 2, two_steps, (carry_in, jnp.zeros((batch, hidden), F32)), unroll=4
    )
    gbias_ref[...] = jnp.sum(gbias, axis=0, keepdims=True)
    odd = place_ref[0] % 2 == 1
    wide_gradient(conv_ref, gproj_ref, stay_ref, send_ref, 0, odd)


def deal(tile, shards, first, stay_ref, send_ref, row, odd):
    size = tile.shape[0] // shards
    for even in range(0, shards, 2):
        pair = [tile[(even + k) * size : (even + k + 1) * size].astype(BF16) for k in range(2)]
        index = (first + even) // 2
        stay_ref[index, row : row + size, :] = jnp.where(odd, pair[1], pair[0])
        send_ref[index, row : row + size, :] = jnp.where(odd, pair[0], pair[1])


def wide_gradient(left_ref, right_ref, stay_ref, send_ref, row, odd):
    shards = 2 * stay_ref.shape[0]
    width = stay_ref.shape[2]
    size = left_ref.shape[1] // shards
    for part in range(right_ref.shape[1] // width):
        tile = dot_tn(left_ref[...], right_ref[:, part * width : (part + 1) * width])
        deal(tile, shards, 0, stay_ref, send_ref, row + part * size, odd)


def tall_gradient(left_ref, right_ref, stay_ref, send_ref, row, odd, block=512):
    shards = 2 * stay_ref.shape[0]
    count = left_ref.shape[1] // block
    for part in range(count):
        tile = dot_tn(left_ref[:, part * block : (part + 1) * block], right_ref[...])
        deal(tile, shards // count, part * (shards // count), stay_ref, send_ref, row, odd)


def weights_kernel(
    place_ref, nmid_ref, gup_ref, act_ref, gt_ref, held_ref, gbranch_ref, stay_ref, send_ref
):
    odd = place_ref[0] % 2 == 1
    shards = 2 * stay_ref.shape[0]
    wide_gradient(nmid_ref, gup_ref, stay_ref, send_ref, 0, odd)
    row = nmid_ref.shape[1] // shards * (gup_ref.shape[1] // stay_ref.shape[2])
    tall_gradient(act_ref, gt_ref, stay_ref, send_ref, row, odd)
    row = row + act_ref.shape[1] // shards
    tall_gradient(held_ref, gbranch_ref, stay_ref, send_ref, row, odd)


def chunks(count, size, body):
    def step(index, carry):
        body(pl.ds(pl.multiple_of(index * size, size), size))
        return carry

    lax.fori_loop(0, count // size, step, 0)


def core_sum_kernel(bits_ref, stay_ref, come_ref, stay_a, send_a, stay_b, send_b, *, plan):
    half = stay_a.shape[1]
    for out_stay, out_send, base, axis in ((stay_a, send_a, 0, plan[0]), (stay_b, send_b, half, plan[1])):
        low = 1 << axis
        for group in range(out_stay.shape[0]):
            fixed = (group >> axis) * 2 * low + (group & (low - 1))
            mine = fixed + low * bits_ref[axis]
            other = fixed + low * (1 - bits_ref[axis])

            def body(rows):
                source = pl.ds(pl.multiple_of(rows.start + base, 16), rows.size)
                out_stay[group, rows, :] = stay_ref[mine, source, :].astype(F32) + come_ref[
                    mine, source, :
                ].astype(F32)
                out_send[group, rows, :] = (
                    stay_ref[other, source, :].astype(F32) + come_ref[other, source, :].astype(F32)
                ).astype(BF16)

            chunks(half, 16, body)


def split_sum_kernel(bits_ref, *refs, plan):
    for part, (which, axis) in enumerate(plan):
        stay_ref, come_ref = refs[2 * part], refs[2 * part + 1]
        out_stay, out_send = refs[2 * len(plan) + 2 * part], refs[2 * len(plan) + 2 * part + 1]
        low = 1 << axis
        for group in range(out_stay.shape[0]):
            fixed = (group >> axis) * 2 * low + (group & (low - 1))
            mine = fixed + low * bits_ref[which]
            other = fixed + low * (1 - bits_ref[which])

            def body(rows):
                out_stay[group, rows, :] = stay_ref[mine, rows, :] + come_ref[mine, rows, :].astype(F32)
                out_send[group, rows, :] = (
                    stay_ref[other, rows, :] + come_ref[other, rows, :].astype(F32)
                ).astype(BF16)

            chunks(out_stay.shape[1], 16, body)


def join_sum_kernel(bits_ref, stay_a, come_a, stay_b, come_b, out_stay, out_send):
    half = stay_a.shape[1]
    width = out_stay.shape[1]
    here = pl.ds(pl.multiple_of(bits_ref[0] * width, width), width)
    there = pl.ds(pl.multiple_of((1 - bits_ref[0]) * width, width), width)
    for stay_ref, come_ref, base in ((stay_a, come_a, 0), (stay_b, come_b, half)):

        def body(rows):
            goal = pl.ds(pl.multiple_of(rows.start + base, 16), rows.size)
            out_stay[goal, :] = stay_ref[0, rows, here] + come_ref[0, rows, here].astype(F32)
            out_send[goal, :] = (
                stay_ref[0, rows, there] + come_ref[0, rows, there].astype(F32)
            ).astype(BF16)

        chunks(half, 16, body)


def column_sum_kernel(bits_ref, stay_ref, come_ref, out_stay, out_send, *, bit):
    width = out_stay.shape[1]
    here = pl.ds(pl.multiple_of(bits_ref[bit] * width, width), width)
    there = pl.ds(pl.multiple_of((1 - bits_ref[bit]) * width, width), width)

    def body(rows):
        out_stay[rows, :] = stay_ref[rows, here] + come_ref[rows, here].astype(F32)
        out_send[rows, :] = (stay_ref[rows, there] + come_ref[rows, there].astype(F32)).astype(BF16)

    chunks(out_stay.shape[0], 16, body)


def round_sum_kernel(stay_ref, come_ref, out_ref):
    def body(rows):
        out_ref[rows, :] = (stay_ref[rows, :].astype(F32) + come_ref[rows, :].astype(F32)).astype(BF16)

    chunks(out_ref.shape[0], 16, body)


def tail_kernel(
    gconv_ref, after_ref, xt_ref, halo_ref, gmid_ref, gain_ref, taps_ref,
    ginput_ref, gnorm1_ref, gtaps_ref, norm_buf, gconv_buf, wide_buf,
    *, steps,
):
    batch, span, width = ginput_ref.shape
    size = steps * batch
    lead = EDGE * batch
    gain = gain_ref[...]
    for row in range(batch):
        interleave(norm_buf, row, batch, halo_ref[row])
    edge = read(norm_buf, slice(0, lead))
    write(norm_buf, slice(0, lead), (edge * rms(edge) * gain).astype(BF16).astype(F32))
    gconv_buf[pl.ds(span * batch, after_ref.shape[0]), :] = after_ref[...].astype(F32)

    def spread(index, carry):
        rows = rows_of(index, size)
        values = read(xt_ref, rows)
        normed = (values * rms(values) * gain).astype(BF16).astype(F32)
        write(norm_buf, pl.ds(pl.multiple_of(index * size + lead, 8), size), normed)
        gconv_buf[rows, :] = gconv_ref[rows, :].astype(F32)
        return carry

    lax.fori_loop(0, span // steps, spread, 0)

    def chunk(index, carry):
        gnorm1, gtaps = carry
        rows = rows_of(index, size)
        here = gconv_buf[rows, :]
        gnormed = here * taps_ref[0:1, :]
        sums = []
        for tap in range(KW):
            if tap:
                later = pl.ds(pl.multiple_of(index * size + tap * batch, 8), size)
                gnormed = gnormed + gconv_buf[later, :] * taps_ref[tap : tap + 1, :]
            earlier = pl.ds(pl.multiple_of(index * size + lead - tap * batch, 8), size)
            sums.append(gtaps[tap] + jnp.sum(read(norm_buf, earlier) * here, axis=0, keepdims=True))
        values = read(xt_ref, rows)
        scale = rms(values)
        unit = values * scale
        gnorm1 = gnorm1 + jnp.sum(gnormed * unit, axis=0, keepdims=True)
        pulled = gnormed * gain
        ginput = gmid_ref[rows, :] + scale * (
            pulled - unit * jnp.mean(pulled * unit, axis=-1, keepdims=True)
        )
        write(wide_buf, rows, ginput)
        return gnorm1, tuple(sums)

    zero = jnp.zeros((1, width), F32)
    gnorm1, gtaps = lax.fori_loop(0, span // steps, chunk, (zero, (zero,) * KW))
    gnorm1_ref[...] = gnorm1
    for tap in range(KW):
        gtaps_ref[tap : tap + 1, :] = gtaps[tap]
    for row in range(batch):
        ginput_ref[row] = deinterleave(wide_buf, row, batch, span)


def call(kernel, name, out_shapes, in_specs, args, scratch=(), limit=16, flops=0, moved=0):
    return pl.pallas_call(
        kernel,
        name=name,
        out_shape=[jax.ShapeDtypeStruct(shape, kind) for shape, kind in out_shapes],
        in_specs=in_specs,
        out_specs=[VMEM_SPEC] * len(out_shapes),
        scratch_shapes=list(scratch),
        compiler_params=pltpu.CompilerParams(vmem_limit_bytes=limit * 2**20),
        cost_estimate=pl.CostEstimate(flops=flops, bytes_accessed=moved, transcendentals=0),
    )(*args)


def shifted(block, axis, distance):
    devices = range(lax.axis_size(axis))
    route = [(i - distance, i) for i in devices if i - distance in devices]
    return lax.ppermute(block, axis, route)


def swap(block, axis, bit):
    return lax.ppermute(block, axis, [(i, i ^ (1 << bit)) for i in range(lax.axis_size(axis))])


def spread_sum(name, stay, come, seq_bits, dp_bits):
    places, rows, width = stay.shape
    levels = places.bit_length() - 1
    order_a = list(range(levels))
    order_b = order_a[::-1]
    half = rows // 2

    def shapes(count):
        return [((count, half, width), F32), ((count, half, width), BF16)] * 2

    stay_a, send_a, stay_b, send_b = call(
        functools.partial(core_sum_kernel, plan=(order_a[0], order_b[0])), name + "_core",
        shapes(places // 2), [SMEM_SPEC] + [VMEM_SPEC] * 2, (seq_bits, stay, come),
    )
    for level in range(levels):
        come_a = swap(send_a, "seq", order_a[level] + 1)
        come_b = swap(send_b, "seq", order_b[level] + 1)
        if level + 1 == levels:
            break
        plan = []
        for order in (order_a, order_b):
            bit = order[level + 1]
            plan.append((bit, bit - sum(done < bit for done in order[: level + 1])))
        stay_a, send_a, stay_b, send_b = call(
            functools.partial(split_sum_kernel, plan=tuple(plan)), name + "_seq",
            shapes(places // 4 >> level), [SMEM_SPEC] + [VMEM_SPEC] * 4,
            (seq_bits, stay_a, come_a, stay_b, come_b),
        )
    depth = lax.axis_size("dp").bit_length() - 1
    wide = width // 2
    stay, send = call(
        join_sum_kernel, name + "_join", [((rows, wide), F32), ((rows, wide), BF16)],
        [SMEM_SPEC] + [VMEM_SPEC] * 4, (dp_bits, stay_a, come_a, stay_b, come_b),
    )
    for bit in range(1, depth - 1):
        wide = wide // 2
        come = swap(send, "dp", bit - 1)
        stay, send = call(
            functools.partial(column_sum_kernel, bit=bit), name + "_dp",
            [((rows, wide), F32), ((rows, wide), BF16)], [SMEM_SPEC] + [VMEM_SPEC] * 2,
            (dp_bits, stay, come),
        )
    come = swap(send, "dp", depth - 2)
    (low,) = call(
        round_sum_kernel, name + "_last", [((rows, wide), BF16)], [VMEM_SPEC] * 2, (stay, come)
    )
    come = swap(low, "dp", depth - 1)
    (total,) = call(
        round_sum_kernel, name + "_total", [((rows, wide), BF16)], [VMEM_SPEC] * 2, (low, come)
    )
    for bit in range(depth - 2, -1, -1):
        come = swap(total, "dp", bit)
        upper = dp_bits[bit] == 1
        total = jnp.concatenate(
            [jnp.where(upper, come, total), jnp.where(upper, total, come)], axis=1
        )
    return total.astype(F32)


def on_device(
    inputs, doc_start, norm1_gain, conv_weight, gate_bias, w_in, w_out, norm2_gain, w_up, w_down, out_grad
):
    batch, span, width = inputs.shape
    hidden = w_out.shape[0]
    inner = w_up.shape[1]
    tokens = batch * span
    lanes = width // LANES
    seq_count, dp_count = lax.axis_size("seq"), lax.axis_size("dp")
    pairs = seq_count // 2
    seq_at = lax.axis_index("seq").astype(jnp.int32)
    dp_at = lax.axis_index("dp").astype(jnp.int32)
    place = seq_at[None]
    seq_bits = jnp.stack([(seq_at >> bit) & 1 for bit in range(1, seq_count.bit_length() - 1)])
    dp_bits = jnp.stack([(dp_at >> bit) & 1 for bit in range(dp_count.bit_length() - 1)])
    halo = shifted(inputs[:, span - EDGE :, :], "seq", 1)
    keep = 1.0 - jnp.transpose(doc_start).astype(F32)
    keep = jnp.broadcast_to(keep[:, :, None], (span, batch, 128)).reshape(tokens, 128)
    taps = jnp.transpose(conv_weight)
    gain1, gain2, bias = norm1_gain[None], norm2_gain[None], gate_bias[None]

    xt, conv_out, gate, cand, totals = call(
        functools.partial(front_kernel, steps=16), "front",
        [
            ((lanes, tokens, LANES), F32), ((tokens, width), BF16), ((tokens, hidden), F32),
            ((tokens, hidden), F32), ((2, batch, hidden), F32),
        ],
        [VMEM_SPEC] * 7,
        (inputs, halo, keep, gain1, taps, bias, w_in),
        [pltpu.VMEM((lanes, tokens + EDGE * batch, LANES), F32)],
        limit=LIMITS[0], flops=2 * tokens * width * 2 * hidden, moved=10 * 2**20,
    )
    all_totals = lax.all_gather(totals[None], "seq", axis=0, tiled=True)
    (
        result, gt, prev, held, nmid, act, gup, gmid, gbranch, gheld, outgoing, gnorm2,
    ) = call(
        functools.partial(middle_kernel, steps=32, block=512), "middle",
        [
            ((batch, span, width), BF16), ((tokens, width), BF16), ((tokens, hidden), F32),
            ((tokens, hidden), BF16), ((tokens, width), BF16), ((tokens, inner), BF16),
            ((tokens, inner), BF16), ((tokens, width), F32), ((tokens, width), BF16),
            ((tokens, hidden), F32), ((batch, hidden), F32), ((1, width), F32),
        ],
        [SMEM_SPEC] + [VMEM_SPEC] * 10,
        (place, all_totals, out_grad, xt, keep, gate, cand, gain2, w_out, w_up, w_down),
        [pltpu.VMEM((lanes, tokens, LANES), F32)],
        limit=LIMITS[1], flops=10 * tokens * width * inner, moved=40 * 2**20,
    )
    all_outs = lax.all_gather(outgoing[None], "seq", axis=0, tiled=True)
    up_rows = inner // seq_count
    rows = up_rows + inner // seq_count + hidden // seq_count
    stay1, send1 = call(
        weights_kernel, "weights", [((pairs, rows, width), BF16)] * 2,
        [SMEM_SPEC] + [VMEM_SPEC] * 6,
        (place, nmid, gup, act, gt, held, gbranch),
        limit=LIMITS[2], flops=5 * tokens * width * inner, moved=10 * 2**20,
    )
    come1 = swap(send1, "seq", 0)
    gproj, gbias, stay2, send2 = call(
        back_kernel, "back",
        [((tokens, 2 * hidden), BF16), ((1, hidden), F32)]
        + [((pairs, 2 * hidden // seq_count, width), BF16)] * 2,
        [SMEM_SPEC] + [VMEM_SPEC] * 8,
        (place, all_totals, all_outs, keep, gate, cand, prev, gheld, conv_out),
        limit=LIMITS[3], flops=2 * tokens * width * inner, moved=20 * 2**20,
    )
    come2 = swap(send2, "seq", 0)
    total1 = spread_sum("first", stay1, come1, seq_bits, dp_bits)
    total2 = spread_sum("second", stay2, come2, seq_bits, dp_bits)
    gconv = dot_nt(gproj, w_in).astype(BF16)
    after = shifted(gconv[: EDGE * batch], "seq", -1)
    ginput, gnorm1, gtaps = call(
        functools.partial(tail_kernel, steps=16), "tail",
        [((batch, span, width), F32), ((1, width), F32), ((KW, width), F32)],
        [VMEM_SPEC] * 7,
        (gconv, after, xt, halo, gmid, gain1, taps),
        [
            pltpu.VMEM((lanes, tokens + EDGE * batch, LANES), F32),
            pltpu.VMEM((tokens + EDGE * batch, width), F32),
            pltpu.VMEM((lanes, tokens, LANES), F32),
        ],
        limit=LIMITS[4], flops=0, moved=10 * 2**20,
    )
    small = lax.psum(
        jnp.concatenate([gnorm1[0], gnorm2[0], gbias[0], jnp.transpose(gtaps).reshape(-1)]),
        ("dp", "seq"),
    )

    def own(values):
        size = values.shape[0] // seq_count
        return lax.dynamic_slice_in_dim(values, seq_at * size, size, 0)

    def sides(block):
        blocks = block.reshape(inner // width, -1, width)
        return jnp.concatenate([blocks[k] for k in range(inner // width)], axis=1)

    return (
        result, ginput, own(small[:width]), own(small[2 * width + hidden :].reshape(width, KW)),
        own(small[2 * width : 2 * width + hidden]), sides(total2),
        total1[2 * up_rows :], own(small[width : 2 * width]), sides(total1[:up_rows]),
        total1[up_rows : 2 * up_rows],
    )


def solution(mesh):
    rows, flat = P("dp", "seq", None), P()
    in_specs = (rows, P("dp", "seq")) + (flat,) * 8 + (rows,)
    vec, mat = P("seq"), P("seq", None)
    out_specs = (rows, rows, vec, mat, vec, mat, mat, vec, mat, mat)
    return jax.shard_map(
        on_device, mesh=mesh, in_specs=in_specs, out_specs=out_specs, check_vma=False
    )
```

```python
import functools

import jax
import jax.numpy as jnp
from jax import lax
from jax.experimental import pallas as pl
from jax.experimental.pallas import tpu as pltpu
from jax.sharding import PartitionSpec as P

KW = 4
EPS = 1e-05
EDGE = 8
LANES = 128
WORK = {"first_seq": 10**10, "back": 10**10}
LIMITS = {"ingest": 2, "prepare": 3, "prepare_rest": 1, "front": 4, "forward": 3, "weights": 3, "reverse": 2, "back": 3, "gconv": 1, "tail": 10, "result": 4}
F32 = jnp.float32
BF16 = jnp.bfloat16
GELU_C = 0.7978845608028654
GELU_A = 0.044715

VMEM_SPEC = pl.BlockSpec(memory_space=pltpu.VMEM)


def dot(left, right):
    return jnp.dot(left, right, preferred_element_type=F32)


def dot_nt(left, right):
    return lax.dot_general(left, right, (((1,), (1,)), ((), ())), preferred_element_type=F32)


def dot_tn(left, right):
    return lax.dot_general(left, right, (((0,), (0,)), ((), ())), preferred_element_type=F32)


def widen(column, lanes):
    return jnp.concatenate([column] * (lanes // column.shape[1]), axis=1)


def rms(values):
    return lax.rsqrt(jnp.mean(values * values, axis=-1, keepdims=True) + EPS)


def rows_of(index, count):
    return pl.ds(pl.multiple_of(index * count, count), count)


def interleave(buf, row, batch, values):
    for lane in range(buf.shape[0]):
        cols = slice(lane * LANES, (lane + 1) * LANES)
        buf[lane, pl.ds(row, values.shape[0], stride=batch), :] = values[:, cols].astype(F32)


def deinterleave(buf, row, batch, span):
    parts = [buf[lane, pl.ds(row, span, stride=batch), :] for lane in range(buf.shape[0])]
    return jnp.concatenate(parts, axis=1)


def read(buf, rows):
    return jnp.concatenate([buf[lane, rows, :] for lane in range(buf.shape[0])], axis=1)


def write(buf, rows, values):
    for lane in range(buf.shape[0]):
        buf[lane, rows, :] = values[:, lane * LANES : (lane + 1) * LANES]


def ingest_kernel(x_ref, start_ref, gain_ref, xt_ref, normed_ref, edge_ref, keep_ref, x_buf, sems, *, steps):
    batch, span, width = x_ref.shape
    size = steps * batch
    copies = [pltpu.make_async_copy(x_ref.at[row], x_buf.at[row], sems.at[row]) for row in range(batch)]
    for copy in copies:
        copy.start()
    keep = 1.0 - start_ref[...].astype(F32)
    for token in range(span):
        keep_ref[token * batch : (token + 1) * batch, :] = jnp.broadcast_to(
            keep[:, token : token + 1], (batch, LANES)
        )
    for row, copy in enumerate(copies):
        copy.wait()
        interleave(xt_ref, row, batch, x_buf[row])

    def chunk(index, carry):
        rows = rows_of(index, size)
        values = read(xt_ref, rows)
        normed_ref[rows, :] = (values * rms(values) * gain_ref[...]).astype(BF16)
        return carry

    lax.fori_loop(0, span // steps, chunk, 0)
    edge_ref[...] = normed_ref[(span - EDGE) * batch :, :]


def prepare_kernel(g_ref, w_down_ref, gt_ref, gact_ref, wide_buf, *, steps, block):
    batch, span, width = g_ref.shape
    size = steps * batch
    for row in range(batch):
        interleave(wide_buf, row, batch, g_ref[row])

    def chunk(index, carry):
        rows = rows_of(index, size)
        g_low = read(wide_buf, rows).astype(BF16)
        gt_ref[rows, :] = g_low
        for part in range(gact_ref.shape[1] // block):
            cols = slice(part * block, (part + 1) * block)
            gact_ref[rows, cols] = dot_nt(g_low, w_down_ref[cols, :]).astype(BF16)
        return carry

    lax.fori_loop(0, span // steps, chunk, 0)


def prepare_rest_kernel(gt_ref, w_down_ref, gact_ref, *, size, block):
    first = w_down_ref.shape[0] - gact_ref.shape[1]

    def chunk(index, carry):
        rows = rows_of(index, size)
        for part in range(gact_ref.shape[1] // block):
            cols = slice(part * block, (part + 1) * block)
            weights = w_down_ref[first + part * block : first + (part + 1) * block, :]
            gact_ref[rows, cols] = dot_nt(gt_ref[rows, :], weights).astype(BF16)
        return carry

    lax.fori_loop(0, gt_ref.shape[0] // size, chunk, 0)


def chip_totals_kernel(mine_ref, mate_ref, chip_ref):
    odd = bit_of("seq", 0) == 1
    prod, state = mine_ref[0], mine_ref[1]
    mate_prod, mate_state = mate_ref[0], mate_ref[1]
    chip_ref[0] = prod * mate_prod
    chip_ref[1] = jnp.where(odd, prod * mate_state + state, mate_prod * state + mate_state)


def chip_outgoing_kernel(mine_ref, mate_ref, totals_ref, mate_totals_ref, chip_ref):
    odd = bit_of("seq", 0) == 1
    mine, mate = mine_ref[...], mate_ref[...]
    chip_ref[...] = jnp.where(odd, mate_totals_ref[0] * mine + mate, totals_ref[0] * mate + mine)


def from_chip(refs, source, chip, part):
    value = refs[0][part]
    for mask in range(2, len(refs) + 1):
        value = jnp.where((source ^ chip) == mask, refs[mask - 1][part], value)
    return value


def front_kernel(
    normed_ref, halo_ref, keep_ref, taps_ref, bias_ref, w_ref,
    conv_ref, gate_ref, cand_ref, total_ref, norm_buf,
    *, steps, block,
):
    batch, hidden = total_ref.shape[1:]
    tokens, width = normed_ref.shape
    span = tokens // batch
    size = steps * batch
    lead = EDGE * batch
    norm_buf[:lead, :] = halo_ref[...].astype(F32)

    def chunk(index, carry):
        rows = rows_of(index, size)
        here = normed_ref[rows, :].astype(F32)
        norm_buf[pl.ds(pl.multiple_of(index * size + lead, 8), size), :] = here
        mixing = here * taps_ref[0:1, :]
        for tap in range(1, KW):
            start = pl.multiple_of(index * size + lead - tap * batch, 8)
            mixing = mixing + norm_buf[pl.ds(start, size), :] * taps_ref[tap : tap + 1, :]
        conv_low = mixing.astype(BF16)
        conv_ref[rows, :] = conv_low
        for part in range(hidden // block):
            cols = slice(part * block, (part + 1) * block)
            more = slice(hidden + part * block, hidden + (part + 1) * block)
            gate_ref[rows, cols] = jax.nn.sigmoid(dot(conv_low, w_ref[:, cols]) + bias_ref[:, cols])
            cand_ref[rows, cols] = dot(conv_low, w_ref[:, more])

        def step(offset, carry):
            prod, state = carry
            here = rows_of(index * steps + offset, batch)
            gate = gate_ref[here, :]
            decay = (1.0 - gate) * widen(keep_ref[here, :], hidden)
            return decay * prod, decay * state + gate * cand_ref[here, :]

        return lax.fori_loop(0, steps, step, carry, unroll=8)

    first = (jnp.ones((batch, hidden), F32), jnp.zeros((batch, hidden), F32))
    prod, state = lax.fori_loop(0, span // steps, chunk, first)
    total_ref[0] = prod
    total_ref[1] = state


def forward_kernel(
    mate_ref, *refs, chips, steps, block,
):
    chip_refs = refs[: chips - 1]
    (
        xt_ref, keep_ref, gate_ref, cand_ref, gact_ref, more_ref, gain_ref, w_out_ref, w_up_ref,
        prev_ref, held_ref, mid_ref, nmid_ref, act_ref, gup_ref,
    ) = refs[chips - 1 :]
    batch, hidden = mate_ref.shape[1:]
    inner = w_up_ref.shape[1]
    span = gate_ref.shape[0] // batch
    size = steps * batch
    chip = lax.shift_right_logical(lax.axis_index("seq"), 1)
    carry_in = jnp.zeros((batch, hidden), F32)
    for source in range(chips - 1):
        prod = from_chip(chip_refs, source, chip, 0)
        state = from_chip(chip_refs, source, chip, 1)
        carry_in = jnp.where(source < chip, prod * carry_in + state, carry_in)
    carry_in = jnp.where(bit_of("seq", 0) == 1, mate_ref[0] * carry_in + mate_ref[1], carry_in)
    gain = gain_ref[...]

    def chunk(index, state):
        rows = rows_of(index, size)

        def two_steps(pair, state):
            out = []
            for side in range(2):
                here = pl.ds(pl.multiple_of((index * steps + 2 * pair + side) * batch, batch), batch)
                gate = gate_ref[here, :]
                prev_ref[here, :] = state
                decay = (1.0 - gate) * widen(keep_ref[here, :], hidden)
                state = decay * state + gate * cand_ref[here, :]
                out.append(state)
            both = rows_of(index * (steps // 2) + pair, 2 * batch)
            held_ref[both, :] = jnp.concatenate(out, axis=0).astype(BF16)
            return state

        state = lax.fori_loop(0, steps // 2, two_steps, state, unroll=4)
        middle = read(xt_ref, rows) + dot(held_ref[rows, :], w_out_ref[...])
        mid_ref[rows, :] = middle
        nmid = (middle * rms(middle) * gain).astype(BF16)
        nmid_ref[rows, :] = nmid
        for part in range(inner // block):
            cols = slice(part * block, (part + 1) * block)
            up = dot(nmid, w_up_ref[:, cols])
            square = up * up
            half = 0.5 + 0.5 * jnp.tanh(up * (GELU_C + (GELU_C * GELU_A) * square))
            act = up * half
            slope = half + act * (1.0 - half) * (2.0 * GELU_C + (6.0 * GELU_C * GELU_A) * square)
            act_ref[rows, cols] = act.astype(BF16)
            start = part * block
            source, start = (gact_ref, start) if start < gact_ref.shape[1] else (more_ref, start - gact_ref.shape[1])
            gact = source[rows, start : start + block].astype(F32)
            gup_ref[rows, cols] = (slope * gact).astype(BF16)
        return state

    lax.fori_loop(0, span // steps, chunk, carry_in)


def result_kernel(act_ref, mid_ref, w_down_ref, result_ref, wide_buf, *, steps):
    batch, span, width = result_ref.shape

    def chunk(index, carry):
        rows = rows_of(index, steps * batch)
        write(wide_buf, rows, mid_ref[rows, :] + dot(act_ref[rows, :], w_down_ref[...]))
        return carry

    lax.fori_loop(0, span // steps, chunk, 0)
    for row in range(batch):
        result_ref[row] = deinterleave(wide_buf, row, batch, span).astype(BF16)


def gconv_kernel(gproj_ref, w_in_ref, gconv_ref, *, steps):
    size = steps * 8

    def chunk(index, carry):
        rows = rows_of(index, size)
        gconv_ref[rows, :] = dot_nt(gproj_ref[rows, :], w_in_ref[...]).astype(BF16)
        return carry

    lax.fori_loop(0, gproj_ref.shape[0] // size, chunk, 0)


def reverse_kernel(
    gup_ref, mid_ref, gt_ref, gain_ref, keep_ref, gate_ref, w_out_ref, w_up_ref,
    gmid_ref, gbranch_ref, gheld_ref, outgoing_ref, gnorm2_ref,
    *, steps,
):
    tokens, width = mid_ref.shape
    batch, hidden = outgoing_ref.shape
    span = tokens // batch
    size = steps * batch
    gain = gain_ref[...]

    def chunk(offset, carry):
        arriving, gnorm2 = carry
        index = span // steps - 1 - offset
        rows = rows_of(index, size)
        gnmid = dot_nt(gup_ref[rows, :], w_up_ref[...])
        middle = mid_ref[rows, :]
        scale = rms(middle)
        unit = middle * scale
        gnorm2 = gnorm2 + jnp.sum(gnmid * unit, axis=0, keepdims=True)
        pulled = gnmid * gain
        gmid = gt_ref[rows, :].astype(F32) + scale * (
            pulled - unit * jnp.mean(pulled * unit, axis=-1, keepdims=True)
        )
        gmid_ref[rows, :] = gmid
        gbranch = gmid.astype(BF16)
        gbranch_ref[rows, :] = gbranch
        gheld_ref[rows, :] = dot_nt(gbranch, w_out_ref[...])

        def back(offset, arriving):
            here = rows_of(index * steps + steps - 1 - offset, batch)
            decay = (1.0 - gate_ref[here, :]) * widen(keep_ref[here, :], hidden)
            return decay * (gheld_ref[here, :] + arriving)

        return lax.fori_loop(0, steps, back, arriving, unroll=8), gnorm2

    first = (jnp.zeros((batch, hidden), F32), jnp.zeros((1, width), F32))
    outgoing, gnorm2 = lax.fori_loop(0, span // steps, chunk, first)
    outgoing_ref[...] = outgoing
    gnorm2_ref[...] = gnorm2


def back_kernel(*refs, chips):
    chip_refs, out_refs = refs[: chips - 1], refs[chips - 1 : 2 * chips - 2]
    (
        mate_ref, mate_out_ref, keep_ref, gate_ref, cand_ref, prev_ref, gheld_ref, conv_ref,
        gproj_ref, gbias_ref, stay_ref, send_ref,
    ) = refs[2 * chips - 2 :]
    batch, hidden = mate_out_ref.shape
    span = gate_ref.shape[0] // batch
    chip = lax.shift_right_logical(lax.axis_index("seq"), 1)
    carry_in = jnp.zeros((batch, hidden), F32)
    for source in range(chips - 1, 0, -1):
        prod = from_chip(chip_refs, source, chip, 0)
        state = from_chip(out_refs, source, chip, slice(None))
        carry_in = jnp.where(source > chip, prod * carry_in + state, carry_in)
    carry_in = jnp.where(bit_of("seq", 0) == 0, mate_ref[0] * carry_in + mate_out_ref[...], carry_in)

    def two_steps(offset, carry):
        arriving, gbias = carry
        pair = span // 2 - 1 - offset
        logits = [None, None]
        cands = [None, None]
        for side in (1, 0):
            here = pl.ds(pl.multiple_of((2 * pair + side) * batch, batch), batch)
            gate = gate_ref[here, :]
            keep = widen(keep_ref[here, :], hidden)
            gstate = gheld_ref[here, :] + arriving
            rest = 1.0 - gate
            cands[side] = gstate * gate
            logits[side] = cands[side] * (cand_ref[here, :] - prev_ref[here, :] * keep) * rest
            arriving = rest * keep * gstate
            gbias = gbias + logits[side]
        both = rows_of(pair, 2 * batch)
        gproj_ref[both, :hidden] = jnp.concatenate(logits, axis=0).astype(BF16)
        gproj_ref[both, hidden:] = jnp.concatenate(cands, axis=0).astype(BF16)
        return arriving, gbias

    _, gbias = lax.fori_loop(
        0, span // 2, two_steps, (carry_in, jnp.zeros((batch, hidden), F32)), unroll=4
    )
    gbias_ref[...] = jnp.sum(gbias, axis=0, keepdims=True)
    odd = bit_of("seq", 0) == 1
    wide_gradient(conv_ref, gproj_ref, stay_ref, send_ref, odd)


def deal(tile, shards, first, stay_ref, send_ref, row, odd):
    size = tile.shape[0] // shards
    for even in range(0, shards, 2):
        pair = [tile[(even + k) * size : (even + k + 1) * size].astype(BF16) for k in range(2)]
        index = (first + even) // 2
        stay_ref[index, row : row + size, :] = jnp.where(odd, pair[1], pair[0])
        send_ref[index, row : row + size, :] = jnp.where(odd, pair[0], pair[1])


def wide_gradient(left_ref, right_ref, stay_ref, send_ref, odd):
    shards = 2 * stay_ref.shape[0]
    width = stay_ref.shape[2]
    size = left_ref.shape[1] // shards
    for part in range(right_ref.shape[1] // width):
        tile = dot_tn(left_ref[...], right_ref[:, part * width : (part + 1) * width])
        deal(tile, shards, 0, stay_ref, send_ref, part * size, odd)


def tall_gradient(left_ref, right_ref, stay_ref, send_ref, odd, block=512):
    shards = 2 * stay_ref.shape[0]
    count = left_ref.shape[1] // block
    for part in range(count):
        tile = dot_tn(left_ref[:, part * block : (part + 1) * block], right_ref[...])
        deal(tile, shards // count, part * (shards // count), stay_ref, send_ref, 0, odd)


def weights_kernel(nmid_ref, gup_ref, act_ref, gt_ref, stay_up, send_up, stay_down, send_down):
    odd = bit_of("seq", 0) == 1
    wide_gradient(nmid_ref, gup_ref, stay_up, send_up, odd)
    tall_gradient(act_ref, gt_ref, stay_down, send_down, odd)


def weights_out_kernel(held_ref, gbranch_ref, stay_ref, send_ref):
    tall_gradient(held_ref, gbranch_ref, stay_ref, send_ref, bit_of("seq", 0) == 1)


def bit_of(axis, bit):
    return lax.shift_right_logical(lax.axis_index(axis), bit) & 1


def chunks(count, size, body):
    def step(index, carry):
        body(pl.ds(pl.multiple_of(index * size, size), size))
        return carry

    lax.fori_loop(0, count // size, step, 0)


def core_sum_kernel(*refs, plan):
    sources, (stay_a, send_a, stay_b, send_b) = refs[:-4], refs[-4:]
    base = 0
    for stay_ref, come_ref in zip(sources[::2], sources[1::2]):
        half = stay_ref.shape[1] // 2
        for out_stay, out_send, first, axis in ((stay_a, send_a, 0, plan[0]), (stay_b, send_b, half, plan[1])):
            low = 1 << axis
            for group in range(out_stay.shape[0]):
                fixed = (group >> axis) * 2 * low + (group & (low - 1))
                mine = fixed + low * bit_of("seq", axis + 1)
                other = fixed + low * (1 - bit_of("seq", axis + 1))

                def body(rows):
                    source = pl.ds(pl.multiple_of(rows.start + first, 16), rows.size)
                    goal = pl.ds(pl.multiple_of(rows.start + base, 16), rows.size)
                    out_stay[group, goal, :] = stay_ref[mine, source, :].astype(F32) + come_ref[
                        mine, source, :
                    ].astype(F32)
                    out_send[group, goal, :] = (
                        stay_ref[other, source, :].astype(F32) + come_ref[other, source, :].astype(F32)
                    ).astype(BF16)

                chunks(half, 16, body)
        base += half


def split_sum_kernel(*refs, plan):
    for part, (which, axis) in enumerate(plan):
        stay_ref, come_ref = refs[2 * part], refs[2 * part + 1]
        out_stay, out_send = refs[2 * len(plan) + 2 * part], refs[2 * len(plan) + 2 * part + 1]
        low = 1 << axis
        for group in range(out_stay.shape[0]):
            fixed = (group >> axis) * 2 * low + (group & (low - 1))
            mine = fixed + low * bit_of("seq", which + 1)
            other = fixed + low * (1 - bit_of("seq", which + 1))

            def body(rows):
                out_stay[group, rows, :] = stay_ref[mine, rows, :] + come_ref[mine, rows, :].astype(F32)
                out_send[group, rows, :] = (
                    stay_ref[other, rows, :] + come_ref[other, rows, :].astype(F32)
                ).astype(BF16)

            chunks(out_stay.shape[1], 16, body)


def join_sum_kernel(stay_a, come_a, stay_b, come_b, out_stay, out_send):
    half = stay_a.shape[1]
    width = out_stay.shape[1]
    here = pl.ds(pl.multiple_of(bit_of("dp", 0) * width, width), width)
    there = pl.ds(pl.multiple_of((1 - bit_of("dp", 0)) * width, width), width)
    for stay_ref, come_ref, base in ((stay_a, come_a, 0), (stay_b, come_b, half)):

        def body(rows):
            goal = pl.ds(pl.multiple_of(rows.start + base, 16), rows.size)
            out_stay[goal, :] = stay_ref[0, rows, here] + come_ref[0, rows, here].astype(F32)
            out_send[goal, :] = (
                stay_ref[0, rows, there] + come_ref[0, rows, there].astype(F32)
            ).astype(BF16)

        chunks(half, 16, body)


def column_sum_kernel(stay_ref, come_ref, out_stay, out_send, *, bit):
    width = out_stay.shape[1]
    here = pl.ds(pl.multiple_of(bit_of("dp", bit) * width, width), width)
    there = pl.ds(pl.multiple_of((1 - bit_of("dp", bit)) * width, width), width)

    def body(rows):
        out_stay[rows, :] = stay_ref[rows, here] + come_ref[rows, here].astype(F32)
        out_send[rows, :] = (stay_ref[rows, there] + come_ref[rows, there].astype(F32)).astype(BF16)

    chunks(out_stay.shape[0], 16, body)


def round_sum_kernel(stay_ref, come_ref, out_ref):
    def body(rows):
        out_ref[rows, :] = (stay_ref[rows, :].astype(F32) + come_ref[rows, :].astype(F32)).astype(BF16)

    chunks(out_ref.shape[0], 16, body)


def tail_kernel(
    gconv_ref, after_ref, xt_ref, normed_ref, halo_ref, gmid_ref, gain_ref, taps_ref, gnorm2_ref, gbias_ref,
    ginput_ref, small_ref, norm_buf, gconv_buf, wide_buf,
    *, steps,
):
    batch, span, width = ginput_ref.shape
    size = steps * batch
    lead = EDGE * batch
    gain = gain_ref[...]
    norm_buf[:lead, :] = halo_ref[...].astype(F32)
    gconv_buf[pl.ds(span * batch, after_ref.shape[0]), :] = after_ref[...].astype(F32)

    def spread(index, carry):
        rows = rows_of(index, size)
        norm_buf[pl.ds(pl.multiple_of(index * size + lead, 8), size), :] = normed_ref[rows, :].astype(F32)
        gconv_buf[rows, :] = gconv_ref[rows, :].astype(F32)
        return carry

    lax.fori_loop(0, span // steps, spread, 0)

    def chunk(index, carry):
        gnorm1, gtaps = carry
        rows = rows_of(index, size)
        here = gconv_buf[rows, :]
        gnormed = here * taps_ref[0:1, :]
        sums = []
        for tap in range(KW):
            if tap:
                later = pl.ds(pl.multiple_of(index * size + tap * batch, 8), size)
                gnormed = gnormed + gconv_buf[later, :] * taps_ref[tap : tap + 1, :]
            earlier = pl.ds(pl.multiple_of(index * size + lead - tap * batch, 8), size)
            sums.append(gtaps[tap] + jnp.sum(norm_buf[earlier, :] * here, axis=0, keepdims=True))
        values = read(xt_ref, rows)
        scale = rms(values)
        unit = values * scale
        gnorm1 = gnorm1 + jnp.sum(gnormed * unit, axis=0, keepdims=True)
        pulled = gnormed * gain
        ginput = gmid_ref[rows, :] + scale * (
            pulled - unit * jnp.mean(pulled * unit, axis=-1, keepdims=True)
        )
        write(wide_buf, rows, ginput)
        return gnorm1, tuple(sums)

    zero = jnp.zeros((1, width), F32)
    gnorm1, gtaps = lax.fori_loop(0, span // steps, chunk, (zero, (zero,) * KW))
    small_ref[0:1, :] = gnorm1
    small_ref[1:2, :] = gnorm2_ref[...]
    for tap in range(KW):
        small_ref[2 + tap : 3 + tap, :] = gtaps[tap]
    for part in range(gbias_ref.shape[1] // width):
        row = 2 + KW + part
        small_ref[row : row + 1, :] = gbias_ref[:, part * width : (part + 1) * width]
    for row in range(batch):
        ginput_ref[row] = deinterleave(wide_buf, row, batch, span)


def finish_kernel(total_ref, come_ref, *outs, sizes):
    wide = total_ref.shape[1]
    width = 2 * wide
    for source, bit in ((total_ref, bit_of("dp", 0)), (come_ref, 1 - bit_of("dp", 0))):
        row = 0
        for half in range(2):
            for out, rows in zip(outs, sizes):
                size = out.shape[0]
                for start in range(half * rows // 2, (half + 1) * rows // 2, min(size, rows // 2)):
                    count = min(size, rows // 2)
                    part, low = start // size, start % size
                    cols = pl.ds(pl.multiple_of(part * width + bit * wide, wide), wide)
                    out[low : low + count, cols] = source[row : row + count, :].astype(F32)
                    row += count


def call(
    kernel, name, out_shapes, in_specs, args, scratch=(), limit=2, after=None, rider=None, work=1
):
    ins, outs = len(args), len(out_shapes)

    def body(*refs):
        inner = list(refs[:ins])
        rest = refs[ins:]
        if rider is not None:
            mine, other, rest = rest[0], rest[1], rest[2:]
        if after is not None:
            rest = rest[1:]
        inner += rest[:outs]
        rest = rest[outs:]
        if rider is not None:
            rest[0][...] = mine[...] + other[...]
            rest = rest[1:]
        kernel(*inner, *rest)

    args, in_specs, out_shapes = list(args), list(in_specs), list(out_shapes)
    if rider is not None:
        args += rider
        in_specs += [VMEM_SPEC] * 2
        out_shapes.append((rider[0].shape, rider[0].dtype))
    if after is not None:
        args.append(after)
        in_specs.append(pl.BlockSpec(memory_space=pl.ANY))
    return pl.pallas_call(
        body,
        name=name,
        out_shape=[jax.ShapeDtypeStruct(shape, kind) for shape, kind in out_shapes],
        in_specs=in_specs,
        out_specs=[VMEM_SPEC] * len(out_shapes),
        scratch_shapes=list(scratch),
        compiler_params=pltpu.CompilerParams(vmem_limit_bytes=limit * 2**20),
        cost_estimate=pl.CostEstimate(flops=work, bytes_accessed=1, transcendentals=0),
    )(*args)


def shifted(block, axis, distance):
    devices = range(lax.axis_size(axis))
    route = [(i - distance, i) for i in devices if i - distance in devices]
    return lax.ppermute(block, axis, route)


def swap_by(block, axis, mask):
    return lax.ppermute(block, axis, [(i, i ^ mask) for i in range(lax.axis_size(axis))])


def swap(block, axis, bit):
    return swap_by(block, axis, 1 << bit)


class Order:
    def __init__(self):
        self.last = None
        self.small = None
        self.come = None
        self.hops = []
        self.turn = 0

    def ride(self, small, hops):
        self.small, self.hops, self.turn = small, list(hops), 0
        self.send()

    def send(self):
        self.come = swap(self.small, *self.hops.pop(0)) if self.hops else None

    def call(self, *args, **kwargs):
        self.turn += 1
        rider = None if self.come is None or self.turn < 2 else [self.small, self.come]
        kwargs.setdefault("work", WORK.get(args[1], 1))
        outs = list(call(*args, **kwargs, after=self.last, rider=rider))
        if rider is not None:
            self.small = outs.pop()
            self.turn = 0
            self.send()
        self.last = min(outs, key=lambda out: out.size * out.dtype.itemsize)
        return outs


def spread_sum(order, name, sources, out_shapes):
    places, _, width = sources[0][0].shape
    sizes = tuple(stay.shape[1] for stay, _ in sources)
    rows = sum(sizes)
    levels = places.bit_length() - 1
    order_a = list(range(levels))
    order_b = order_a[::-1]
    half = rows // 2

    def shapes(count):
        return [((count, half, width), F32), ((count, half, width), BF16)] * 2

    stay_a, send_a, stay_b, send_b = order.call(
        functools.partial(core_sum_kernel, plan=(order_a[0], order_b[0])), name + "_core",
        shapes(places // 2), [VMEM_SPEC] * (2 * len(sources)), [part for pair in sources for part in pair],
        limit=1,
    )
    for level in range(levels):
        come_a = swap(send_a, "seq", order_a[level] + 1)
        come_b = swap(send_b, "seq", order_b[level] + 1)
        yield None
        if level + 1 == levels:
            break
        plan = []
        for bits in (order_a, order_b):
            bit = bits[level + 1]
            plan.append((bit, bit - sum(done < bit for done in bits[: level + 1])))
        stay_a, send_a, stay_b, send_b = order.call(
            functools.partial(split_sum_kernel, plan=tuple(plan)), name + "_seq",
            shapes(places // 4 >> level), [VMEM_SPEC] * 4,
            (stay_a, come_a, stay_b, come_b),
        )
    depth = lax.axis_size("dp").bit_length() - 1
    wide = width // 2
    stay, send = order.call(
        join_sum_kernel, name + "_join", [((rows, wide), F32), ((rows, wide), BF16)],
        [VMEM_SPEC] * 4, (stay_a, come_a, stay_b, come_b),
    )
    for bit in range(1, depth - 1):
        wide = wide // 2
        come = swap(send, "dp", bit - 1)
        yield None
        stay, send = order.call(
            functools.partial(column_sum_kernel, bit=bit), name + "_dp",
            [((rows, wide), F32), ((rows, wide), BF16)], [VMEM_SPEC] * 2,
            (stay, come),
        )
    come = swap(send, "dp", depth - 2)
    yield None
    (low,) = order.call(
        round_sum_kernel, name + "_last", [((rows, wide), BF16)], [VMEM_SPEC] * 2, (stay, come)
    )
    come = swap(low, "dp", depth - 1)
    yield None
    (total,) = order.call(
        round_sum_kernel, name + "_total", [((rows, wide), BF16)], [VMEM_SPEC] * 2, (low, come)
    )
    for bit in range(depth - 2, 0, -1):
        come = swap(total, "dp", bit)
        upper = bit_of("dp", bit) == 1
        total = jnp.concatenate(
            [jnp.where(upper, come, total), jnp.where(upper, total, come)], axis=1
        )
    come = swap(total, "dp", 0)
    yield None
    yield order.call(
        functools.partial(finish_kernel, sizes=sizes), name + "_finish", [(shape, F32) for shape in out_shapes],
        [VMEM_SPEC] * 2, (total, come),
    )


def on_device(
    inputs, doc_start, norm1_gain, conv_weight, gate_bias, w_in, w_out, norm2_gain, w_up, w_down, out_grad
):
    batch, span, width = inputs.shape
    hidden = w_out.shape[0]
    inner = w_up.shape[1]
    tokens = batch * span
    lanes = width // LANES
    seq_count, dp_count = lax.axis_size("seq"), lax.axis_size("dp")
    seq_depth, dp_depth = seq_count.bit_length() - 1, dp_count.bit_length() - 1
    pairs = seq_count // 2
    seq_at = lax.axis_index("seq").astype(jnp.int32)
    taps = jnp.transpose(conv_weight)
    gain1, gain2, bias = norm1_gain[None], norm2_gain[None], gate_bias[None]
    order = Order()

    xt, normed, edge, keep = order.call(
        functools.partial(ingest_kernel, steps=16), "ingest",
        [
            ((lanes, tokens, LANES), F32), ((tokens, width), BF16), ((EDGE * batch, width), BF16),
            ((tokens, LANES), F32),
        ],
        [pl.BlockSpec(memory_space=pltpu.HBM)] + [VMEM_SPEC] * 2, (inputs, doc_start, gain1),
        [pltpu.VMEM((batch, span, width), BF16), pltpu.SemaphoreType.DMA((batch,))],
        limit=LIMITS["ingest"],
    )
    halo = shifted(edge, "seq", 1)
    gt, gact = order.call(
        functools.partial(prepare_kernel, steps=64, block=512), "prepare",
        [((tokens, width), BF16), ((tokens, inner // 2), BF16)],
        [VMEM_SPEC] * 2, (out_grad, w_down), [pltpu.VMEM((lanes, tokens, LANES), F32)],
        limit=LIMITS["prepare"],
    )
    conv_out, gate, cand, totals = order.call(
        functools.partial(front_kernel, steps=64, block=512), "front",
        [
            ((tokens, width), BF16), ((tokens, hidden), F32), ((tokens, hidden), F32),
            ((2, batch, hidden), F32),
        ],
        [VMEM_SPEC] * 6, (normed, halo, keep, taps, bias, w_in),
        [pltpu.VMEM((tokens + EDGE * batch, width), F32)],
        limit=LIMITS["front"],
    )
    chips = seq_count // 2
    mate_totals = swap(totals, "seq", 0)
    (chip_totals,) = order.call(
        chip_totals_kernel, "chip_totals", [(totals.shape, F32)], [VMEM_SPEC] * 2, (totals, mate_totals)
    )
    all_totals = [swap_by(chip_totals, "seq", 2 * mask) for mask in range(1, chips)]
    (more,) = order.call(
        functools.partial(prepare_rest_kernel, size=512, block=512), "prepare_rest",
        [((tokens, inner // 2), BF16)], [VMEM_SPEC] * 2, (gt, w_down), limit=LIMITS["prepare_rest"],
    )
    prev, held, mid, nmid, act, gup = order.call(
        functools.partial(forward_kernel, chips=chips, steps=64, block=512), "forward",
        [
            ((tokens, hidden), F32), ((tokens, hidden), BF16), ((tokens, width), F32),
            ((tokens, width), BF16), ((tokens, inner), BF16), ((tokens, inner), BF16),
        ],
        [VMEM_SPEC] * (9 + chips),
        (mate_totals, *all_totals, xt, keep, gate, cand, gact, more, gain2, w_out, w_up),
        limit=LIMITS["forward"],
    )
    up_rows = inner // seq_count
    stay_up, send_up, stay_down, send_down = order.call(
        weights_kernel, "weights", [((pairs, up_rows, width), BF16)] * 4,
        [VMEM_SPEC] * 4, (nmid, gup, act, gt), limit=LIMITS["weights"],
    )
    come_up, come_down = swap(send_up, "seq", 0), swap(send_down, "seq", 0)
    gmid, gbranch, gheld, outgoing, gnorm2 = order.call(
        functools.partial(reverse_kernel, steps=64), "reverse",
        [
            ((tokens, width), F32), ((tokens, width), BF16), ((tokens, hidden), F32),
            ((batch, hidden), F32), ((1, width), F32),
        ],
        [VMEM_SPEC] * 8, (gup, mid, gt, gain2, keep, gate, w_out, w_up),
        limit=LIMITS["reverse"],
    )
    mate_outgoing = swap(outgoing, "seq", 0)
    out_rows = hidden // seq_count
    in_rows = 2 * hidden // seq_count
    stay_out, send_out = order.call(
        weights_out_kernel, "weights_out", [((pairs, out_rows, width), BF16)] * 2,
        [VMEM_SPEC] * 2, (held, gbranch), limit=LIMITS["weights"],
    )
    come_out = swap(send_out, "seq", 0)
    (chip_outgoing,) = order.call(
        chip_outgoing_kernel, "chip_outgoing", [(outgoing.shape, F32)], [VMEM_SPEC] * 4,
        (outgoing, mate_outgoing, totals, mate_totals),
    )
    all_outgoing = [swap_by(chip_outgoing, "seq", 2 * mask) for mask in range(1, chips)]
    first = spread_sum(
        order, "first", [(stay_up, come_up), (stay_down, come_down)],
        [(width // seq_count, inner), (up_rows, width)],
    )
    next(first)
    gproj, gbias, stay_in, send_in = order.call(
        functools.partial(back_kernel, chips=chips), "back",
        [((tokens, 2 * hidden), BF16), ((1, hidden), F32)] + [((pairs, in_rows, width), BF16)] * 2,
        [VMEM_SPEC] * (6 + 2 * chips),
        (
            *all_totals, *all_outgoing, mate_totals, mate_outgoing, keep, gate, cand, prev, gheld, conv_out,
        ),
        limit=LIMITS["back"],
    )
    come_in = swap(send_in, "seq", 0)
    (gconv,) = order.call(
        functools.partial(gconv_kernel, steps=64), "gconv", [((tokens, width), BF16)],
        [VMEM_SPEC] * 2, (gproj, w_in), limit=LIMITS["gconv"],
    )
    after = shifted(gconv[: EDGE * batch], "seq", -1)
    order.last = after
    second = spread_sum(
        order, "second", [(stay_in, come_in), (stay_out, come_out)],
        [(width // seq_count, 2 * hidden), (out_rows, width)],
    )
    next(first)
    next(second)
    bias_rows = hidden // width
    ginput, small = order.call(
        functools.partial(tail_kernel, steps=16), "tail",
        [((batch, span, width), F32), ((2 + KW + bias_rows, width), F32)],
        [VMEM_SPEC] * 10,
        (gconv, after, xt, normed, halo, gmid, gain1, taps, gnorm2, gbias),
        [
            pltpu.VMEM((tokens + EDGE * batch, width), F32),
            pltpu.VMEM((tokens + EDGE * batch, width), F32),
            pltpu.VMEM((lanes, tokens, LANES), F32),
        ],
        limit=LIMITS["tail"],
    )
    order.ride(
        small, [("seq", bit) for bit in range(seq_depth)] + [("dp", bit) for bit in range(dp_depth)]
    )
    next(first)
    next(second)
    (result,) = order.call(
        functools.partial(result_kernel, steps=64), "result", [((batch, span, width), BF16)],
        [VMEM_SPEC] * 3, (act, mid, w_down), [pltpu.VMEM((lanes, tokens, LANES), F32)],
        limit=LIMITS["result"],
    )
    next(first)
    next(second)
    next(first)
    next(second)
    done = {}
    while len(done) < 2:
        for part in (first, second):
            if part not in done:
                outs = next(part)
                if outs is not None:
                    done[part] = outs
    while order.come is not None:
        order.small = order.small + order.come
        order.send()
    small = order.small
    gw_up, gw_down = done[first]
    gw_in, gw_out = done[second]

    def own(values):
        size = values.shape[0] // seq_count
        return lax.dynamic_slice_in_dim(values, seq_at * size, size, 0)

    return (
        result, ginput, own(small[0]), own(jnp.transpose(small[2 : 2 + KW])),
        own(small[2 + KW :].reshape(-1)), gw_in, gw_out, own(small[1]), gw_up, gw_down,
    )


def solution(mesh):
    rows, flat = P("dp", "seq", None), P()
    in_specs = (rows, P("dp", "seq")) + (flat,) * 8 + (rows,)
    vec, mat = P("seq"), P("seq", None)
    out_specs = (rows, rows, vec, mat, vec, mat, mat, vec, mat, mat)
    return jax.shard_map(
        on_device, mesh=mesh, in_specs=in_specs, out_specs=out_specs, check_vma=False
    )
```

```python
import functools

import jax
import jax.numpy as jnp
from jax import lax
from jax.experimental import pallas as pl
from jax.experimental.pallas import tpu as pltpu
from jax.sharding import PartitionSpec as P

KW = 4
EPS = 1e-05
EDGE = 8
SMALL = 16
LANES = 128
FINAL = ("result", "inputs", "first_finish", "second_finish")
WORK = dict.fromkeys(("ingest", "prepare", "front", "forward", "first_seq", "back", "chip_outgoing"), 10**10)
LIMITS = {"ingest": 2, "prepare": 3, "prepare_rest": 1, "front": 4, "forward": 3, "weights": 3, "reverse": 2, "back": 3, "gconv": 1, "taps": 5, "inputs": 5, "result": 4}
F32 = jnp.float32
BF16 = jnp.bfloat16
GELU_C = 0.7978845608028654
GELU_A = 0.044715

VMEM_SPEC = pl.BlockSpec(memory_space=pltpu.VMEM)


def dot(left, right):
    return jnp.dot(left, right, preferred_element_type=F32)


def dot_nt(left, right):
    return lax.dot_general(left, right, (((1,), (1,)), ((), ())), preferred_element_type=F32)


def dot_tn(left, right):
    return lax.dot_general(left, right, (((0,), (0,)), ((), ())), preferred_element_type=F32)


def widen(column, lanes):
    return jnp.concatenate([column] * (lanes // column.shape[1]), axis=1)


def rms(values):
    return lax.rsqrt(jnp.mean(values * values, axis=-1, keepdims=True) + EPS)


def rows_of(index, count):
    return pl.ds(pl.multiple_of(index * count, count), count)


def interleave(buf, row, batch, values):
    for lane in range(buf.shape[0]):
        cols = slice(lane * LANES, (lane + 1) * LANES)
        buf[lane, pl.ds(row, values.shape[0], stride=batch), :] = values[:, cols].astype(F32)


def deinterleave(buf, row, batch, span):
    parts = [buf[lane, pl.ds(row, span, stride=batch), :] for lane in range(buf.shape[0])]
    return jnp.concatenate(parts, axis=1)


def read(buf, rows):
    return jnp.concatenate([buf[lane, rows, :] for lane in range(buf.shape[0])], axis=1)


def write(buf, rows, values):
    for lane in range(buf.shape[0]):
        buf[lane, rows, :] = values[:, lane * LANES : (lane + 1) * LANES]


def ingest_kernel(x_ref, start_ref, gain_ref, xt_ref, normed_ref, edge_ref, keep_ref, x_buf, start_buf, gain_buf, sems, *, steps):
    batch, span, width = x_ref.shape
    size = steps * batch
    copies = [pltpu.make_async_copy(x_ref.at[row], x_buf.at[row], sems.at[row]) for row in range(batch)]
    start_copy = pltpu.make_async_copy(start_ref, start_buf, sems.at[batch])
    gain_copy = pltpu.make_async_copy(gain_ref, gain_buf, sems.at[batch + 1])
    for copy in (start_copy, *copies, gain_copy):
        copy.start()
    start_copy.wait()
    keep = 1.0 - start_buf[...].astype(F32)
    for token in range(span):
        keep_ref[token * batch : (token + 1) * batch, :] = jnp.broadcast_to(
            keep[:, token : token + 1], (batch, LANES)
        )
    for row, copy in enumerate(copies):
        copy.wait()
        interleave(xt_ref, row, batch, x_buf[row])
    gain_copy.wait()

    def chunk(index, carry):
        rows = rows_of(index, size)
        values = read(xt_ref, rows)
        normed_ref[rows, :] = (values * rms(values) * gain_buf[...]).astype(BF16)
        return carry

    lax.fori_loop(0, span // steps, chunk, 0)
    edge_ref[...] = normed_ref[(span - EDGE) * batch :, :]


def prepare_kernel(g_ref, w_down_ref, gt_ref, gact_ref, wide_buf, *, steps, block):
    batch, span, width = g_ref.shape
    size = steps * batch
    for row in range(batch):
        interleave(wide_buf, row, batch, g_ref[row])

    def chunk(index, carry):
        rows = rows_of(index, size)
        g_low = read(wide_buf, rows).astype(BF16)
        gt_ref[rows, :] = g_low
        for part in range(gact_ref.shape[1] // block):
            cols = slice(part * block, (part + 1) * block)
            gact_ref[rows, cols] = dot_nt(g_low, w_down_ref[cols, :]).astype(BF16)
        return carry

    lax.fori_loop(0, span // steps, chunk, 0)


def prepare_rest_kernel(gt_ref, w_down_ref, gact_ref, *, size, block):
    first = w_down_ref.shape[0] - gact_ref.shape[1]

    def chunk(index, carry):
        rows = rows_of(index, size)
        for part in range(gact_ref.shape[1] // block):
            cols = slice(part * block, (part + 1) * block)
            weights = w_down_ref[first + part * block : first + (part + 1) * block, :]
            gact_ref[rows, cols] = dot_nt(gt_ref[rows, :], weights).astype(BF16)
        return carry

    lax.fori_loop(0, gt_ref.shape[0] // size, chunk, 0)


def chip_totals_kernel(mine_ref, mate_ref, chip_ref):
    odd = bit_of("seq", 0) == 1
    prod, state = mine_ref[0], mine_ref[1]
    mate_prod, mate_state = mate_ref[0], mate_ref[1]
    chip_ref[0] = prod * mate_prod
    chip_ref[1] = jnp.where(odd, prod * mate_state + state, mate_prod * state + mate_state)


def chip_outgoing_kernel(mine_ref, mate_ref, totals_ref, mate_totals_ref, chip_ref):
    odd = bit_of("seq", 0) == 1
    mine, mate = mine_ref[...], mate_ref[...]
    chip_ref[...] = jnp.where(odd, mate_totals_ref[0] * mine + mate, totals_ref[0] * mate + mine)


def from_chip(refs, source, chip, part):
    value = refs[0][part]
    for mask in range(2, len(refs) + 1):
        value = jnp.where((source ^ chip) == mask, refs[mask - 1][part], value)
    return value


def front_kernel(
    normed_ref, halo_ref, keep_ref, taps_ref, bias_ref, w_ref,
    conv_ref, gate_ref, cand_ref, total_ref, norm_buf,
    *, steps, block,
):
    batch, hidden = total_ref.shape[1:]
    tokens, width = normed_ref.shape
    span = tokens // batch
    size = steps * batch
    lead = EDGE * batch
    norm_buf[:lead, :] = halo_ref[...].astype(F32)

    def chunk(index, carry):
        rows = rows_of(index, size)
        here = normed_ref[rows, :].astype(F32)
        norm_buf[pl.ds(pl.multiple_of(index * size + lead, 8), size), :] = here
        mixing = here * taps_ref[0:1, :]
        for tap in range(1, KW):
            start = pl.multiple_of(index * size + lead - tap * batch, 8)
            mixing = mixing + norm_buf[pl.ds(start, size), :] * taps_ref[tap : tap + 1, :]
        conv_low = mixing.astype(BF16)
        conv_ref[rows, :] = conv_low
        for part in range(hidden // block):
            cols = slice(part * block, (part + 1) * block)
            more = slice(hidden + part * block, hidden + (part + 1) * block)
            gate_ref[rows, cols] = jax.nn.sigmoid(dot(conv_low, w_ref[:, cols]) + bias_ref[:, cols])
            cand_ref[rows, cols] = dot(conv_low, w_ref[:, more])

        def step(offset, carry):
            prod, state = carry
            here = rows_of(index * steps + offset, batch)
            gate = gate_ref[here, :]
            decay = (1.0 - gate) * widen(keep_ref[here, :], hidden)
            return decay * prod, decay * state + gate * cand_ref[here, :]

        return lax.fori_loop(0, steps, step, carry, unroll=8)

    first = (jnp.ones((batch, hidden), F32), jnp.zeros((batch, hidden), F32))
    prod, state = lax.fori_loop(0, span // steps, chunk, first)
    total_ref[0] = prod
    total_ref[1] = state


def forward_kernel(
    mate_ref, *refs, chips, steps, block,
):
    chip_refs = refs[: chips - 1]
    (
        xt_ref, keep_ref, gate_ref, cand_ref, gact_ref, more_ref, gain_ref, w_out_ref, w_up_ref,
        carry_ref, held_ref, mid_ref, nmid_ref, act_ref, gup_ref,
    ) = refs[chips - 1 :]
    batch, hidden = mate_ref.shape[1:]
    inner = w_up_ref.shape[1]
    span = gate_ref.shape[0] // batch
    size = steps * batch
    chip = lax.shift_right_logical(lax.axis_index("seq"), 1)
    carry_in = jnp.zeros((batch, hidden), F32)
    for source in range(chips - 1):
        prod = from_chip(chip_refs, source, chip, 0)
        state = from_chip(chip_refs, source, chip, 1)
        carry_in = jnp.where(source < chip, prod * carry_in + state, carry_in)
    carry_in = jnp.where(bit_of("seq", 0) == 1, mate_ref[0] * carry_in + mate_ref[1], carry_in)
    carry_ref[...] = carry_in
    gain = gain_ref[...]

    def chunk(index, state):
        rows = rows_of(index, size)

        def two_steps(pair, state):
            out = []
            for side in range(2):
                here = pl.ds(pl.multiple_of((index * steps + 2 * pair + side) * batch, batch), batch)
                gate = gate_ref[here, :]
                decay = (1.0 - gate) * widen(keep_ref[here, :], hidden)
                state = decay * state + gate * cand_ref[here, :]
                out.append(state)
            both = rows_of(index * (steps // 2) + pair, 2 * batch)
            held_ref[both, :] = jnp.concatenate(out, axis=0).astype(BF16)
            return state

        state = lax.fori_loop(0, steps // 2, two_steps, state, unroll=4)
        middle = read(xt_ref, rows) + dot(held_ref[rows, :], w_out_ref[...])
        mid_ref[rows, :] = middle
        nmid = (middle * rms(middle) * gain).astype(BF16)
        nmid_ref[rows, :] = nmid
        for part in range(inner // block):
            cols = slice(part * block, (part + 1) * block)
            up = dot(nmid, w_up_ref[:, cols])
            square = up * up
            half = 0.5 + 0.5 * jnp.tanh(up * (GELU_C + (GELU_C * GELU_A) * square))
            act = up * half
            slope = half + act * (1.0 - half) * (2.0 * GELU_C + (6.0 * GELU_C * GELU_A) * square)
            act_ref[rows, cols] = act.astype(BF16)
            start = part * block
            source, start = (gact_ref, start) if start < gact_ref.shape[1] else (more_ref, start - gact_ref.shape[1])
            gact = source[rows, start : start + block].astype(F32)
            gup_ref[rows, cols] = (slope * gact).astype(BF16)
        return state

    lax.fori_loop(0, span // steps, chunk, carry_in)


def result_kernel(act_ref, mid_ref, w_down_ref, result_ref, wide_buf, *, steps):
    batch, span, width = result_ref.shape

    def chunk(index, carry):
        rows = rows_of(index, steps * batch)
        write(wide_buf, rows, mid_ref[rows, :] + dot(act_ref[rows, :], w_down_ref[...]))
        return carry

    lax.fori_loop(0, span // steps, chunk, 0)
    for row in range(batch):
        result_ref[row] = deinterleave(wide_buf, row, batch, span).astype(BF16)


def gconv_kernel(gproj_ref, w_in_ref, gconv_ref, *, steps):
    size = steps * 8

    def chunk(index, carry):
        rows = rows_of(index, size)
        gconv_ref[rows, :] = dot_nt(gproj_ref[rows, :], w_in_ref[...]).astype(BF16)
        return carry

    lax.fori_loop(0, gproj_ref.shape[0] // size, chunk, 0)


def reverse_kernel(
    gup_ref, mid_ref, gt_ref, gain_ref, keep_ref, gate_ref, w_out_ref, w_up_ref,
    gmid_ref, gbranch_ref, gheld_ref, outgoing_ref, gnorm2_ref,
    *, steps,
):
    tokens, width = mid_ref.shape
    batch, hidden = outgoing_ref.shape
    span = tokens // batch
    size = steps * batch
    gain = gain_ref[...]

    def chunk(offset, carry):
        arriving, gnorm2 = carry
        index = span // steps - 1 - offset
        rows = rows_of(index, size)
        gnmid = dot_nt(gup_ref[rows, :], w_up_ref[...])
        middle = mid_ref[rows, :]
        scale = rms(middle)
        unit = middle * scale
        gnorm2 = gnorm2 + jnp.sum(gnmid * unit, axis=0, keepdims=True)
        pulled = gnmid * gain
        gmid = gt_ref[rows, :].astype(F32) + scale * (
            pulled - unit * jnp.mean(pulled * unit, axis=-1, keepdims=True)
        )
        gmid_ref[rows, :] = gmid
        gbranch = gmid.astype(BF16)
        gbranch_ref[rows, :] = gbranch
        gheld_ref[rows, :] = dot_nt(gbranch, w_out_ref[...])

        def back(offset, arriving):
            here = rows_of(index * steps + steps - 1 - offset, batch)
            decay = (1.0 - gate_ref[here, :]) * widen(keep_ref[here, :], hidden)
            return decay * (gheld_ref[here, :] + arriving)

        return lax.fori_loop(0, steps, back, arriving, unroll=8), gnorm2

    first = (jnp.zeros((batch, hidden), F32), jnp.zeros((1, width), F32))
    outgoing, gnorm2 = lax.fori_loop(0, span // steps, chunk, first)
    outgoing_ref[...] = outgoing
    gnorm2_ref[...] = gnorm2


def back_kernel(*refs, chips):
    chip_refs, out_refs = refs[: chips - 1], refs[chips - 1 : 2 * chips - 2]
    (
        mate_ref, mate_out_ref, keep_ref, gate_ref, cand_ref, state_ref, held_ref, gheld_ref, conv_ref, w_in_ref,
        gproj_ref, gbias_ref, edge_ref, stay_ref, send_ref,
    ) = refs[2 * chips - 2 :]
    batch, hidden = mate_out_ref.shape
    span = gate_ref.shape[0] // batch
    chip = lax.shift_right_logical(lax.axis_index("seq"), 1)
    carry_in = jnp.zeros((batch, hidden), F32)
    for source in range(chips - 1, 0, -1):
        prod = from_chip(chip_refs, source, chip, 0)
        state = from_chip(out_refs, source, chip, slice(None))
        carry_in = jnp.where(source > chip, prod * carry_in + state, carry_in)
    carry_in = jnp.where(bit_of("seq", 0) == 0, mate_ref[0] * carry_in + mate_out_ref[...], carry_in)

    def two_steps(offset, carry):
        arriving, gbias = carry
        pair = span // 2 - 1 - offset
        logits = [None, None]
        cands = [None, None]
        before = held_ref[rows_of(jnp.maximum(pair - 1, 0), 2 * batch), :].astype(F32)[batch:]
        prevs = [
            jnp.where(pair == 0, state_ref[...], before),
            held_ref[rows_of(pair, 2 * batch), :].astype(F32)[:batch],
        ]
        for side in (1, 0):
            here = pl.ds(pl.multiple_of((2 * pair + side) * batch, batch), batch)
            gate = gate_ref[here, :]
            keep = widen(keep_ref[here, :], hidden)
            gstate = gheld_ref[here, :] + arriving
            rest = 1.0 - gate
            cands[side] = gstate * gate
            logits[side] = cands[side] * (cand_ref[here, :] - prevs[side] * keep) * rest
            arriving = rest * keep * gstate
            gbias = gbias + logits[side]
        both = rows_of(pair, 2 * batch)
        gproj_ref[both, :hidden] = jnp.concatenate(logits, axis=0).astype(BF16)
        gproj_ref[both, hidden:] = jnp.concatenate(cands, axis=0).astype(BF16)
        return arriving, gbias

    _, gbias = lax.fori_loop(
        0, span // 2, two_steps, (carry_in, jnp.zeros((batch, hidden), F32)), unroll=4
    )
    gbias_ref[...] = jnp.sum(gbias, axis=0, keepdims=True)
    edge_ref[...] = dot_nt(gproj_ref[: edge_ref.shape[0], :], w_in_ref[...]).astype(BF16)
    odd = bit_of("seq", 0) == 1
    wide_gradient(conv_ref, gproj_ref, stay_ref, send_ref, odd)


def deal(tile, shards, first, stay_ref, send_ref, row, odd):
    size = tile.shape[0] // shards
    for even in range(0, shards, 2):
        pair = [tile[(even + k) * size : (even + k + 1) * size].astype(BF16) for k in range(2)]
        index = (first + even) // 2
        stay_ref[index, row : row + size, :] = jnp.where(odd, pair[1], pair[0])
        send_ref[index, row : row + size, :] = jnp.where(odd, pair[0], pair[1])


def wide_gradient(left_ref, right_ref, stay_ref, send_ref, odd):
    shards = 2 * stay_ref.shape[0]
    width = stay_ref.shape[2]
    size = left_ref.shape[1] // shards
    for part in range(right_ref.shape[1] // width):
        tile = dot_tn(left_ref[...], right_ref[:, part * width : (part + 1) * width])
        deal(tile, shards, 0, stay_ref, send_ref, part * size, odd)


def tall_gradient(left_ref, right_ref, stay_ref, send_ref, odd, block=512):
    shards = 2 * stay_ref.shape[0]
    count = left_ref.shape[1] // block
    for part in range(count):
        tile = dot_tn(left_ref[:, part * block : (part + 1) * block], right_ref[...])
        deal(tile, shards // count, part * (shards // count), stay_ref, send_ref, 0, odd)


def weights_kernel(nmid_ref, gup_ref, act_ref, gt_ref, stay_up, send_up, stay_down, send_down):
    odd = bit_of("seq", 0) == 1
    wide_gradient(nmid_ref, gup_ref, stay_up, send_up, odd)
    tall_gradient(act_ref, gt_ref, stay_down, send_down, odd)


def weights_out_kernel(held_ref, gbranch_ref, stay_ref, send_ref):
    tall_gradient(held_ref, gbranch_ref, stay_ref, send_ref, bit_of("seq", 0) == 1)


def bit_of(axis, bit):
    return lax.shift_right_logical(lax.axis_index(axis), bit) & 1


def chunks(count, size, body):
    def step(index, carry):
        body(pl.ds(pl.multiple_of(index * size, size), size))
        return carry

    lax.fori_loop(0, count // size, step, 0)


def core_sum_kernel(*refs, plan):
    sources, (stay_a, send_a, stay_b, send_b) = refs[:-4], refs[-4:]
    base = 0
    for stay_ref, come_ref in zip(sources[::2], sources[1::2]):
        half = stay_ref.shape[1] // 2
        for out_stay, out_send, first, axis in ((stay_a, send_a, 0, plan[0]), (stay_b, send_b, half, plan[1])):
            low = 1 << axis
            for group in range(out_stay.shape[0]):
                fixed = (group >> axis) * 2 * low + (group & (low - 1))
                mine = fixed + low * bit_of("seq", axis + 1)
                other = fixed + low * (1 - bit_of("seq", axis + 1))

                def body(rows):
                    source = pl.ds(pl.multiple_of(rows.start + first, 16), rows.size)
                    goal = pl.ds(pl.multiple_of(rows.start + base, 16), rows.size)
                    out_stay[group, goal, :] = stay_ref[mine, source, :].astype(F32) + come_ref[
                        mine, source, :
                    ].astype(F32)
                    out_send[group, goal, :] = (
                        stay_ref[other, source, :].astype(F32) + come_ref[other, source, :].astype(F32)
                    ).astype(BF16)

                chunks(half, 16, body)
        base += half


def split_sum_kernel(*refs, plan, counts):
    ins = 2 * sum(counts)
    outs = refs[ins:]
    source = 0
    for part, (which, axis) in enumerate(plan):
        out_stay, out_send = outs[2 * part], outs[2 * part + 1]
        low = 1 << axis
        base = 0
        for pair in range(counts[part]):
            stay_ref, come_ref = refs[source], refs[source + 1]
            source += 2
            for group in range(out_stay.shape[0]):
                fixed = (group >> axis) * 2 * low + (group & (low - 1))
                mine = fixed + low * bit_of("seq", which + 1)
                other = fixed + low * (1 - bit_of("seq", which + 1))

                def body(rows):
                    goal = pl.ds(pl.multiple_of(rows.start + base, 16), rows.size)
                    out_stay[group, goal, :] = stay_ref[mine, rows, :].astype(F32) + come_ref[
                        mine, rows, :
                    ].astype(F32)
                    out_send[group, goal, :] = (
                        stay_ref[other, rows, :].astype(F32) + come_ref[other, rows, :].astype(F32)
                    ).astype(BF16)

                chunks(stay_ref.shape[1], 16, body)
            base += stay_ref.shape[1]


def join_sum_kernel(stay_a, come_a, stay_b, come_b, out_stay, out_send):
    width = out_stay.shape[1]
    here = pl.ds(pl.multiple_of(bit_of("dp", 0) * width, width), width)
    there = pl.ds(pl.multiple_of((1 - bit_of("dp", 0)) * width, width), width)
    for stay_ref, come_ref, base in ((stay_a, come_a, 0), (stay_b, come_b, stay_a.shape[1])):

        def body(rows):
            goal = pl.ds(pl.multiple_of(rows.start + base, 16), rows.size)
            out_stay[goal, :] = stay_ref[0, rows, here] + come_ref[0, rows, here].astype(F32)
            out_send[goal, :] = (
                stay_ref[0, rows, there] + come_ref[0, rows, there].astype(F32)
            ).astype(BF16)

        chunks(stay_ref.shape[1], 16, body)


def column_sum_kernel(stay_ref, come_ref, out_stay, out_send, *, bit):
    width = out_stay.shape[1]
    here = pl.ds(pl.multiple_of(bit_of("dp", bit) * width, width), width)
    there = pl.ds(pl.multiple_of((1 - bit_of("dp", bit)) * width, width), width)

    def body(rows):
        out_stay[rows, :] = stay_ref[rows, here] + come_ref[rows, here].astype(F32)
        out_send[rows, :] = (stay_ref[rows, there] + come_ref[rows, there].astype(F32)).astype(BF16)

    chunks(out_stay.shape[0], 16, body)


def round_sum_kernel(stay_ref, come_ref, out_ref):
    def body(rows):
        out_ref[rows, :] = (stay_ref[rows, :].astype(F32) + come_ref[rows, :].astype(F32)).astype(BF16)

    chunks(out_ref.shape[0], 16, body)


def taps_kernel(
    gconv_ref, after_ref, xt_ref, normed_ref, halo_ref, taps_ref, gnorm2_ref, gbias_ref,
    gnormed_ref, stay_ref, send_ref, norm_buf, gconv_buf,
    *, steps,
):
    tokens, width = gconv_ref.shape
    batch = halo_ref.shape[0] // EDGE
    size = steps * batch
    lead = EDGE * batch
    norm_buf[:lead, :] = halo_ref[...].astype(F32)
    gconv_buf[tokens : tokens + after_ref.shape[0], :] = after_ref[...].astype(F32)

    def spread(index, carry):
        rows = rows_of(index, size)
        norm_buf[pl.ds(pl.multiple_of(index * size + lead, 8), size), :] = normed_ref[rows, :].astype(F32)
        gconv_buf[rows, :] = gconv_ref[rows, :].astype(F32)
        return carry

    lax.fori_loop(0, tokens // size, spread, 0)

    def chunk(index, carry):
        gnorm1, gtaps = carry
        rows = rows_of(index, size)
        here = gconv_buf[rows, :]
        gnormed = here * taps_ref[0:1, :]
        sums = []
        for tap in range(KW):
            if tap:
                later = pl.ds(pl.multiple_of(index * size + tap * batch, 8), size)
                gnormed = gnormed + gconv_buf[later, :] * taps_ref[tap : tap + 1, :]
            earlier = pl.ds(pl.multiple_of(index * size + lead - tap * batch, 8), size)
            sums.append(gtaps[tap] + jnp.sum(norm_buf[earlier, :] * here, axis=0, keepdims=True))
        gnormed_ref[rows, :] = gnormed
        values = read(xt_ref, rows)
        gnorm1 = gnorm1 + jnp.sum(gnormed * (values * rms(values)), axis=0, keepdims=True)
        return gnorm1, tuple(sums)

    zero = jnp.zeros((1, width), F32)
    gnorm1, gtaps = lax.fori_loop(0, tokens // size, chunk, (zero, (zero,) * KW))
    places = 2 * stay_ref.shape[0]
    odd = bit_of("seq", 0) == 1
    rows = []
    for place in range(places):
        parts = [
            vector[:, place * (vector.shape[1] // places) : (place + 1) * (vector.shape[1] // places)]
            for vector in (gnorm1, gnorm2_ref[...], *gtaps, gbias_ref[...])
        ]
        row = jnp.concatenate(parts, axis=1)
        if row.shape[1] < width:
            row = jnp.concatenate([row, jnp.zeros((1, width - row.shape[1]), F32)], axis=1)
        rows.append(jnp.broadcast_to(row, (stay_ref.shape[1], width)))
    for index in range(places // 2):
        pair = rows[2 * index : 2 * index + 2]
        stay_ref[index] = jnp.where(odd, pair[1], pair[0]).astype(BF16)
        send_ref[index] = jnp.where(odd, pair[0], pair[1]).astype(BF16)


def inputs_kernel(gnormed_ref, xt_ref, gmid_ref, gain_ref, ginput_ref, wide_buf, *, steps):
    batch, span, width = ginput_ref.shape
    gain = gain_ref[...]

    def chunk(index, carry):
        rows = rows_of(index, steps * batch)
        values = read(xt_ref, rows)
        scale = rms(values)
        unit = values * scale
        pulled = gnormed_ref[rows, :] * gain
        ginput = gmid_ref[rows, :] + scale * (
            pulled - unit * jnp.mean(pulled * unit, axis=-1, keepdims=True)
        )
        write(wide_buf, rows, ginput)
        return carry

    lax.fori_loop(0, span // steps, chunk, 0)
    for row in range(batch):
        ginput_ref[row] = deinterleave(wide_buf, row, batch, span)


def finish_kernel(total_ref, come_ref, *outs, sizes):
    wide = total_ref.shape[1]
    width = 2 * wide
    half = sum(sizes) // 2
    if len(outs) > len(sizes):
        low = bit_of("dp", 0) == 0
        mine, other = [ref[half : half + SMALL, :].astype(F32) for ref in (total_ref, come_ref)]
        row = jnp.concatenate([jnp.where(low, mine, other), jnp.where(low, other, mine)], axis=1)
        column = 0
        for out in outs[len(sizes) :]:
            for line in range(out.shape[0]):
                out[line : line + 1, :] = row[0:1, column : column + out.shape[1]]
                column += out.shape[1]
    for source, bit in ((total_ref, bit_of("dp", 0)), (come_ref, 1 - bit_of("dp", 0))):
        for part_b in range(2):
            row = part_b * (total_ref.shape[0] - half)
            for out, rows in zip(outs, sizes):
                size = out.shape[0]
                count = min(size, rows // 2)
                for start in range(part_b * rows // 2, (part_b + 1) * rows // 2, count):
                    part, low_row = start // size, start % size
                    cols = pl.ds(pl.multiple_of(part * width + bit * wide, wide), wide)
                    out[low_row : low_row + count, cols] = source[row : row + count, :].astype(F32)
                    row += count


def call(
    kernel, name, out_shapes, in_specs, args, scratch=(), limit=2, after=(), work=1
):
    ins, outs = len(args), len(out_shapes)

    def body(*refs):
        inner = list(refs[:ins])
        rest = refs[ins:]
        rest = rest[len(after) :]
        inner += rest[:outs]
        rest = rest[outs:]
        if name in FINAL:
            rest[0][...] = jnp.zeros((8, LANES), F32)
            rest = rest[1:]
        kernel(*inner, *rest)

    args, in_specs, out_shapes = list(args), list(in_specs), list(out_shapes)
    if name in FINAL:
        out_shapes.append(((8, LANES), F32))
    args += after
    in_specs += [pl.BlockSpec(memory_space=pl.ANY)] * len(after)
    return pl.pallas_call(
        body,
        name=name,
        out_shape=[
            (pltpu.HBM if name in FINAL and index < outs else jax.ShapeDtypeStruct)(shape, kind)
            for index, (shape, kind) in enumerate(out_shapes)
        ],
        in_specs=in_specs,
        out_specs=[VMEM_SPEC] * len(out_shapes),
        scratch_shapes=list(scratch),
        compiler_params=pltpu.CompilerParams(vmem_limit_bytes=limit * 2**20),
        cost_estimate=pl.CostEstimate(flops=work, bytes_accessed=1, transcendentals=0),
    )(*args)


def shifted(block, axis, distance):
    devices = range(lax.axis_size(axis))
    route = [(i - distance, i) for i in devices if i - distance in devices]
    return lax.ppermute(block, axis, route)


def swap_by(block, axis, mask):
    return lax.ppermute(block, axis, [(i, i ^ mask) for i in range(lax.axis_size(axis))])


def swap(block, axis, bit):
    return swap_by(block, axis, 1 << bit)


class Order:
    def __init__(self):
        self.last = ()

    def call(self, *args, **kwargs):
        kwargs.setdefault("work", WORK.get(args[1], 1))
        outs = list(call(*args, **kwargs, after=self.last))
        self.last = (min(outs, key=lambda out: out.size * out.dtype.itemsize),)
        if args[1] in FINAL:
            outs.pop()
        return outs


def spread_sum(order, name, sources, out_shapes, late=()):
    places, _, width = sources[0][0].shape
    sizes = tuple(stay.shape[1] for stay, _ in sources)
    rows = sum(sizes)
    levels = places.bit_length() - 1
    order_a = list(range(levels))
    order_b = order_a[::-1]
    half = rows // 2

    def shapes(count, more=0):
        out = []
        for part in (half + more, half):
            out += [((count, part, width), F32), ((count, part, width), BF16)]
        return out

    stay_a, send_a, stay_b, send_b = order.call(
        functools.partial(core_sum_kernel, plan=(order_a[0], order_b[0])), name + "_core",
        shapes(places // 2), [VMEM_SPEC] * (2 * len(sources)), [part for pair in sources for part in pair],
        limit=1,
    )
    for level in range(levels):
        come_a = swap(send_a, "seq", order_a[level] + 1)
        come_b = swap(send_b, "seq", order_b[level] + 1)
        yield None
        if level + 1 == levels:
            break
        plan = []
        for bits in (order_a, order_b):
            bit = bits[level + 1]
            plan.append((bit, bit - sum(done < bit for done in bits[: level + 1])))
        sources = [stay_a, come_a, *(late if level == 0 else ()), stay_b, come_b]
        more = SMALL if late else 0
        stay_a, send_a, stay_b, send_b = order.call(
            functools.partial(
                split_sum_kernel, plan=tuple(plan), counts=(2 if late and level == 0 else 1, 1)
            ),
            name + "_seq", shapes(places // 4 >> level, more), [VMEM_SPEC] * len(sources), sources,
        )
    rows += SMALL if late else 0
    depth = lax.axis_size("dp").bit_length() - 1
    wide = width // 2
    stay, send = order.call(
        join_sum_kernel, name + "_join", [((rows, wide), F32), ((rows, wide), BF16)],
        [VMEM_SPEC] * 4, (stay_a, come_a, stay_b, come_b),
    )
    for bit in range(1, depth - 1):
        wide = wide // 2
        come = swap(send, "dp", bit - 1)
        yield None
        stay, send = order.call(
            functools.partial(column_sum_kernel, bit=bit), name + "_dp",
            [((rows, wide), F32), ((rows, wide), BF16)], [VMEM_SPEC] * 2,
            (stay, come),
        )
    come = swap(send, "dp", depth - 2)
    yield None
    (low,) = order.call(
        round_sum_kernel, name + "_last", [((rows, wide), BF16)], [VMEM_SPEC] * 2, (stay, come)
    )
    come = swap(low, "dp", depth - 1)
    yield None
    (total,) = order.call(
        round_sum_kernel, name + "_total", [((rows, wide), BF16)], [VMEM_SPEC] * 2, (low, come)
    )
    for bit in range(depth - 2, 0, -1):
        come = swap(total, "dp", bit)
        upper = bit_of("dp", bit) == 1
        total = jnp.concatenate(
            [jnp.where(upper, come, total), jnp.where(upper, total, come)], axis=1
        )
    come = swap(total, "dp", 0)
    yield None
    yield order.call(
        functools.partial(finish_kernel, sizes=sizes), name + "_finish", [(shape, F32) for shape in out_shapes],
        [VMEM_SPEC] * 2, (total, come),
    )


def on_device(
    inputs, doc_start, norm1_gain, conv_weight, gate_bias, w_in, w_out, norm2_gain, w_up, w_down, out_grad
):
    batch, span, width = inputs.shape
    hidden = w_out.shape[0]
    inner = w_up.shape[1]
    tokens = batch * span
    lanes = width // LANES
    seq_count, dp_count = lax.axis_size("seq"), lax.axis_size("dp")
    seq_depth, dp_depth = seq_count.bit_length() - 1, dp_count.bit_length() - 1
    pairs = seq_count // 2
    seq_at = lax.axis_index("seq").astype(jnp.int32)
    taps = jnp.transpose(conv_weight)
    gain1, gain2, bias = norm1_gain[None], norm2_gain[None], gate_bias[None]
    order = Order()

    xt, normed, edge, keep = order.call(
        functools.partial(ingest_kernel, steps=16), "ingest",
        [
            ((lanes, tokens, LANES), F32), ((tokens, width), BF16), ((EDGE * batch, width), BF16),
            ((tokens, LANES), F32),
        ],
        [pl.BlockSpec(memory_space=pltpu.HBM)] * 3,
        [pltpu.with_memory_space_constraint(part, pltpu.HBM) for part in (inputs, doc_start, gain1)],
        [
            pltpu.VMEM((batch, span, width), BF16), pltpu.VMEM((batch, span), jnp.int32),
            pltpu.VMEM((1, width), F32), pltpu.SemaphoreType.DMA((batch + 2,)),
        ],
        limit=LIMITS["ingest"],
    )
    halo = shifted(edge, "seq", 1)
    gt, gact = order.call(
        functools.partial(prepare_kernel, steps=64, block=512), "prepare",
        [((tokens, width), BF16), ((tokens, inner // 2), BF16)],
        [VMEM_SPEC] * 2, (out_grad, w_down), [pltpu.VMEM((lanes, tokens, LANES), F32)],
        limit=LIMITS["prepare"],
    )
    conv_out, gate, cand, totals = order.call(
        functools.partial(front_kernel, steps=64, block=512), "front",
        [
            ((tokens, width), BF16), ((tokens, hidden), F32), ((tokens, hidden), F32),
            ((2, batch, hidden), F32),
        ],
        [VMEM_SPEC] * 6, (normed, halo, keep, taps, bias, w_in),
        [pltpu.VMEM((tokens + EDGE * batch, width), F32)],
        limit=LIMITS["front"],
    )
    chips = seq_count // 2
    mate_totals = swap(totals, "seq", 0)
    (chip_totals,) = order.call(
        chip_totals_kernel, "chip_totals", [(totals.shape, F32)], [VMEM_SPEC] * 2, (totals, mate_totals)
    )
    all_totals = [swap_by(chip_totals, "seq", 2 * mask) for mask in range(1, chips)]
    (more,) = order.call(
        functools.partial(prepare_rest_kernel, size=512, block=512), "prepare_rest",
        [((tokens, inner // 2), BF16)], [VMEM_SPEC] * 2, (gt, w_down), limit=LIMITS["prepare_rest"],
    )
    state_in, held, mid, nmid, act, gup = order.call(
        functools.partial(forward_kernel, chips=chips, steps=64, block=512), "forward",
        [
            ((batch, hidden), F32), ((tokens, hidden), BF16), ((tokens, width), F32),
            ((tokens, width), BF16), ((tokens, inner), BF16), ((tokens, inner), BF16),
        ],
        [VMEM_SPEC] * (9 + chips),
        (mate_totals, *all_totals, xt, keep, gate, cand, gact, more, gain2, w_out, w_up),
        limit=LIMITS["forward"],
    )
    up_rows = inner // seq_count
    stay_up, send_up, stay_down, send_down = order.call(
        weights_kernel, "weights", [((pairs, up_rows, width), BF16)] * 4,
        [VMEM_SPEC] * 4, (nmid, gup, act, gt), limit=LIMITS["weights"],
    )
    come_up, come_down = swap(send_up, "seq", 0), swap(send_down, "seq", 0)
    gmid, gbranch, gheld, outgoing, gnorm2 = order.call(
        functools.partial(reverse_kernel, steps=64), "reverse",
        [
            ((tokens, width), F32), ((tokens, width), BF16), ((tokens, hidden), F32),
            ((batch, hidden), F32), ((1, width), F32),
        ],
        [VMEM_SPEC] * 8, (gup, mid, gt, gain2, keep, gate, w_out, w_up),
        limit=LIMITS["reverse"],
    )
    mate_outgoing = swap(outgoing, "seq", 0)
    out_rows = hidden // seq_count
    in_rows = 2 * hidden // seq_count
    stay_out, send_out = order.call(
        weights_out_kernel, "weights_out", [((pairs, out_rows, width), BF16)] * 2,
        [VMEM_SPEC] * 2, (held, gbranch), limit=LIMITS["weights"],
    )
    come_out = swap(send_out, "seq", 0)
    (chip_outgoing,) = order.call(
        chip_outgoing_kernel, "chip_outgoing", [(outgoing.shape, F32)], [VMEM_SPEC] * 4,
        (outgoing, mate_outgoing, totals, mate_totals),
    )
    all_outgoing = [swap_by(chip_outgoing, "seq", 2 * mask) for mask in range(1, chips)]
    first = spread_sum(
        order, "first", [(stay_up, come_up), (stay_down, come_down)],
        [(width // seq_count, inner), (up_rows, width)],
    )
    next(first)
    gproj, gbias, gconv_edge, stay_in, send_in = order.call(
        functools.partial(back_kernel, chips=chips), "back",
        [((tokens, 2 * hidden), BF16), ((1, hidden), F32), ((EDGE * batch, width), BF16)]
        + [((pairs, in_rows, width), BF16)] * 2,
        [VMEM_SPEC] * (8 + 2 * chips),
        (
            *all_totals, *all_outgoing, mate_totals, mate_outgoing, keep, gate, cand, state_in, held, gheld, conv_out, w_in,
        ),
        limit=LIMITS["back"],
    )
    after = shifted(gconv_edge, "seq", -1)
    come_in = swap(send_in, "seq", 0)
    (gconv,) = order.call(
        functools.partial(gconv_kernel, steps=64), "gconv", [((tokens, width), BF16)],
        [VMEM_SPEC] * 2, (gproj, w_in), limit=LIMITS["gconv"],
    )
    order.last = (*order.last, after)
    late = []
    share = width // seq_count
    second = spread_sum(
        order, "second", [(stay_in, come_in), (stay_out, come_out)],
        [
            (share, 2 * hidden), (out_rows, width), (1, share), (1, share), (KW, share),
            (1, hidden // seq_count),
        ],
        late,
    )
    next(first)
    next(second)
    gnormed, stay_small, send_small = order.call(
        functools.partial(taps_kernel, steps=16), "taps",
        [((tokens, width), F32)] + [((pairs, SMALL, width), BF16)] * 2, [VMEM_SPEC] * 8,
        (gconv, after, xt, normed, halo, taps, gnorm2, gbias),
        [
            pltpu.VMEM((tokens + EDGE * batch, width), F32),
            pltpu.VMEM((tokens + EDGE * batch, width), F32),
        ],
        limit=LIMITS["taps"],
    )
    come_small = swap(send_small, "seq", 0)
    next(first)
    stay_small, send_small = order.call(
        functools.partial(split_sum_kernel, plan=((0, 0),), counts=(1,)), "small",
        [((pairs // 2, SMALL, width), F32), ((pairs // 2, SMALL, width), BF16)], [VMEM_SPEC] * 2,
        (stay_small, come_small),
    )
    late += [stay_small, swap(send_small, "seq", 1)]
    (result,) = order.call(
        functools.partial(result_kernel, steps=64), "result", [((batch, span, width), BF16)],
        [VMEM_SPEC] * 3, (act, mid, w_down), [pltpu.VMEM((lanes, tokens, LANES), F32)],
        limit=LIMITS["result"],
    )
    next(first)
    next(second)
    next(second)
    (ginput,) = order.call(
        functools.partial(inputs_kernel, steps=16), "inputs", [((batch, span, width), F32)],
        [VMEM_SPEC] * 4, (gnormed, xt, gmid, gain1), [pltpu.VMEM((lanes, tokens, LANES), F32)],
        limit=LIMITS["inputs"],
    )
    next(first)
    next(second)
    done = {}
    while len(done) < 2:
        for part in (second, first):
            if part not in done:
                outs = next(part)
                if outs is not None:
                    done[part] = outs
    gw_up, gw_down = done[first]
    gw_in, gw_out, gnorm1, gnorm2, gtaps, gbias = done[second]
    return (
        result, ginput, gnorm1[0], jnp.transpose(gtaps), gbias[0], gw_in, gw_out, gnorm2[0], gw_up, gw_down,
    )


def solution(mesh):
    rows, flat = P("dp", "seq", None), P()
    in_specs = (rows, P("dp", "seq")) + (flat,) * 8 + (rows,)
    vec, mat = P("seq"), P("seq", None)
    out_specs = (rows, rows, vec, mat, vec, mat, mat, vec, mat, mat)
    return jax.shard_map(
        on_device, mesh=mesh, in_specs=in_specs, out_specs=out_specs, check_vma=False
    )
```

```python
import functools

import jax
import jax.numpy as jnp
from jax import lax
from jax.experimental import pallas as pl
from jax.experimental.pallas import tpu as pltpu
from jax.sharding import PartitionSpec as P

KW = 4
EPS = 1e-05
EDGE = 8
SMALL = 16
LANES = 128
FINAL = ("result", "inputs", "first_finish", "second_finish")
WORK = {"second_join": 5 * 10**9, "result": 2000000000} | dict.fromkeys(("ingest", "prepare", "front", "forward", "first_seq", "back", "chip_outgoing"), 10**10)
LIMITS = {"ingest": 2, "prepare": 3, "prepare_rest": 1, "front": 7, "forward": 6, "weights": 3, "reverse": 5, "back": 3, "gconv": 1, "taps": 5, "inputs": 5, "result": 4}
F32 = jnp.float32
BF16 = jnp.bfloat16
GELU_C = 0.7978845608028654
GELU_A = 0.044715

VMEM_SPEC = pl.BlockSpec(memory_space=pltpu.VMEM)


def dot(left, right):
    return jnp.dot(left, right, preferred_element_type=F32)


def dot_nt(left, right):
    return lax.dot_general(left, right, (((1,), (1,)), ((), ())), preferred_element_type=F32)


def dot_tn(left, right):
    return lax.dot_general(left, right, (((0,), (0,)), ((), ())), preferred_element_type=F32)


def widen(column, lanes):
    return jnp.concatenate([column] * (lanes // column.shape[1]), axis=1)


def rms(values):
    return lax.rsqrt(jnp.mean(values * values, axis=-1, keepdims=True) + EPS)


def rows_of(index, count):
    return pl.ds(pl.multiple_of(index * count, count), count)


def interleave(buf, row, batch, values):
    for lane in range(buf.shape[0]):
        cols = slice(lane * LANES, (lane + 1) * LANES)
        buf[lane, pl.ds(row, values.shape[0], stride=batch), :] = values[:, cols].astype(F32)


def deinterleave(buf, row, batch, span):
    parts = [buf[lane, pl.ds(row, span, stride=batch), :] for lane in range(buf.shape[0])]
    return jnp.concatenate(parts, axis=1)


def read(buf, rows):
    return jnp.concatenate([buf[lane, rows, :] for lane in range(buf.shape[0])], axis=1)


def write(buf, rows, values):
    for lane in range(buf.shape[0]):
        buf[lane, rows, :] = values[:, lane * LANES : (lane + 1) * LANES]


def ingest_kernel(x_ref, start_ref, gain_ref, xt_ref, normed_ref, edge_ref, keep_ref, x_buf, start_buf, gain_buf, sems, *, steps):
    batch, span, width = x_ref.shape
    size = steps * batch
    copies = [pltpu.make_async_copy(x_ref.at[row], x_buf.at[row], sems.at[row]) for row in range(batch)]
    start_copy = pltpu.make_async_copy(start_ref, start_buf, sems.at[batch])
    gain_copy = pltpu.make_async_copy(gain_ref, gain_buf, sems.at[batch + 1])
    for copy in (start_copy, *copies, gain_copy):
        copy.start()
    start_copy.wait()
    keep = 1.0 - start_buf[...].astype(F32)
    for token in range(span):
        keep_ref[token * batch : (token + 1) * batch, :] = jnp.broadcast_to(
            keep[:, token : token + 1], (batch, LANES)
        )
    for row, copy in enumerate(copies):
        copy.wait()
        interleave(xt_ref, row, batch, x_buf[row])
    gain_copy.wait()

    def chunk(index, carry):
        rows = rows_of(index, size)
        values = read(xt_ref, rows)
        normed_ref[rows, :] = (values * rms(values) * gain_buf[...]).astype(BF16)
        return carry

    lax.fori_loop(0, span // steps, chunk, 0)
    edge_ref[...] = normed_ref[(span - EDGE) * batch :, :]


def prepare_kernel(g_ref, w_down_ref, gt_ref, gact_ref, wide_buf, *, steps, block):
    batch, span, width = g_ref.shape
    size = steps * batch
    for row in range(batch):
        interleave(wide_buf, row, batch, g_ref[row])

    def chunk(index, carry):
        rows = rows_of(index, size)
        g_low = read(wide_buf, rows).astype(BF16)
        gt_ref[rows, :] = g_low
        for part in range(gact_ref.shape[1] // block):
            cols = slice(part * block, (part + 1) * block)
            gact_ref[rows, cols] = dot_nt(g_low, w_down_ref[cols, :]).astype(BF16)
        return carry

    lax.fori_loop(0, span // steps, chunk, 0)


def prepare_rest_kernel(gt_ref, w_down_ref, gact_ref, *, size, block):
    first = w_down_ref.shape[0] - gact_ref.shape[1]

    def chunk(index, carry):
        rows = rows_of(index, size)
        for part in range(gact_ref.shape[1] // block):
            cols = slice(part * block, (part + 1) * block)
            weights = w_down_ref[first + part * block : first + (part + 1) * block, :]
            gact_ref[rows, cols] = dot_nt(gt_ref[rows, :], weights).astype(BF16)
        return carry

    lax.fori_loop(0, gt_ref.shape[0] // size, chunk, 0)


def chip_totals_kernel(mine_ref, mate_ref, chip_ref):
    odd = bit_of("seq", 0) == 1
    prod, state = mine_ref[0], mine_ref[1]
    mate_prod, mate_state = mate_ref[0], mate_ref[1]
    chip_ref[0] = prod * mate_prod
    chip_ref[1] = jnp.where(odd, prod * mate_state + state, mate_prod * state + mate_state)


def chip_outgoing_kernel(mine_ref, mate_ref, totals_ref, mate_totals_ref, chip_ref):
    odd = bit_of("seq", 0) == 1
    mine, mate = mine_ref[...], mate_ref[...]
    chip_ref[...] = jnp.where(odd, mate_totals_ref[0] * mine + mate, totals_ref[0] * mate + mine)


def from_chip(refs, source, chip, part):
    value = refs[0][part]
    for mask in range(2, len(refs) + 1):
        value = jnp.where((source ^ chip) == mask, refs[mask - 1][part], value)
    return value


def front_kernel(
    normed_ref, halo_ref, keep_ref, taps_ref, bias_ref, w_ref,
    conv_ref, gate_ref, cand_ref, total_ref, norm_buf,
    *, steps, block,
):
    batch, hidden = total_ref.shape[1:]
    tokens, width = normed_ref.shape
    span = tokens // batch
    size = steps * batch
    lead = EDGE * batch
    norm_buf[:lead, :] = halo_ref[...].astype(F32)

    def chunk(index, carry):
        rows = rows_of(index, size)
        here = normed_ref[rows, :].astype(F32)
        norm_buf[pl.ds(pl.multiple_of(index * size + lead, 8), size), :] = here
        mixing = here * taps_ref[0:1, :]
        for tap in range(1, KW):
            start = pl.multiple_of(index * size + lead - tap * batch, 8)
            mixing = mixing + norm_buf[pl.ds(start, size), :] * taps_ref[tap : tap + 1, :]
        conv_low = mixing.astype(BF16)
        conv_ref[rows, :] = conv_low
        for part in range(hidden // block):
            cols = slice(part * block, (part + 1) * block)
            more = slice(hidden + part * block, hidden + (part + 1) * block)
            gate_ref[rows, cols] = jax.nn.sigmoid(dot(conv_low, w_ref[:, cols]) + bias_ref[:, cols])
            cand_ref[rows, cols] = dot(conv_low, w_ref[:, more])

        def step(offset, carry):
            prod, state = carry
            here = rows_of(index * steps + offset, batch)
            gate = gate_ref[here, :]
            decay = (1.0 - gate) * widen(keep_ref[here, :], hidden)
            return decay * prod, decay * state + gate * cand_ref[here, :]

        return lax.fori_loop(0, steps, step, carry, unroll=8)

    first = (jnp.ones((batch, hidden), F32), jnp.zeros((batch, hidden), F32))
    prod, state = lax.fori_loop(0, span // steps, chunk, first)
    total_ref[0] = prod
    total_ref[1] = state


def forward_kernel(
    mate_ref, *refs, chips, steps, block,
):
    chip_refs = refs[: chips - 1]
    (
        xt_ref, keep_ref, gate_ref, cand_ref, gact_ref, more_ref, gain_ref, w_out_ref, w_up_ref,
        carry_ref, held_ref, mid_ref, nmid_ref, act_ref, gup_ref,
    ) = refs[chips - 1 :]
    batch, hidden = mate_ref.shape[1:]
    inner = w_up_ref.shape[1]
    span = gate_ref.shape[0] // batch
    size = steps * batch
    chip = lax.shift_right_logical(lax.axis_index("seq"), 1)
    carry_in = jnp.zeros((batch, hidden), F32)
    for source in range(chips - 1):
        prod = from_chip(chip_refs, source, chip, 0)
        state = from_chip(chip_refs, source, chip, 1)
        carry_in = jnp.where(source < chip, prod * carry_in + state, carry_in)
    carry_in = jnp.where(bit_of("seq", 0) == 1, mate_ref[0] * carry_in + mate_ref[1], carry_in)
    carry_ref[...] = carry_in
    gain = gain_ref[...]

    def chunk(index, state):
        rows = rows_of(index, size)

        def two_steps(pair, state):
            out = []
            for side in range(2):
                here = pl.ds(pl.multiple_of((index * steps + 2 * pair + side) * batch, batch), batch)
                gate = gate_ref[here, :]
                decay = (1.0 - gate) * widen(keep_ref[here, :], hidden)
                state = decay * state + gate * cand_ref[here, :]
                out.append(state)
            both = rows_of(index * (steps // 2) + pair, 2 * batch)
            held_ref[both, :] = jnp.concatenate(out, axis=0).astype(BF16)
            return state

        state = lax.fori_loop(0, steps // 2, two_steps, state, unroll=4)
        middle = read(xt_ref, rows) + dot(held_ref[rows, :], w_out_ref[...])
        mid_ref[rows, :] = middle
        nmid = (middle * rms(middle) * gain).astype(BF16)
        nmid_ref[rows, :] = nmid
        for part in range(inner // block):
            cols = slice(part * block, (part + 1) * block)
            up = dot(nmid, w_up_ref[:, cols])
            square = up * up
            half = 0.5 + 0.5 * jnp.tanh(up * (GELU_C + (GELU_C * GELU_A) * square))
            act = up * half
            slope = half + act * (1.0 - half) * (2.0 * GELU_C + (6.0 * GELU_C * GELU_A) * square)
            act_ref[rows, cols] = act.astype(BF16)
            start = part * block
            source, start = (gact_ref, start) if start < gact_ref.shape[1] else (more_ref, start - gact_ref.shape[1])
            gact = source[rows, start : start + block].astype(F32)
            gup_ref[rows, cols] = (slope * gact).astype(BF16)
        return state

    lax.fori_loop(0, span // steps, chunk, carry_in)


def result_kernel(act_ref, mid_ref, w_down_ref, result_ref, wide_buf, *, steps):
    batch, span, width = result_ref.shape

    def chunk(index, carry):
        rows = rows_of(index, steps * batch)
        write(wide_buf, rows, mid_ref[rows, :] + dot(act_ref[rows, :], w_down_ref[...]))
        return carry

    lax.fori_loop(0, span // steps, chunk, 0)
    for row in range(batch):
        result_ref[row] = deinterleave(wide_buf, row, batch, span).astype(BF16)


def gconv_kernel(gproj_ref, w_in_ref, gconv_ref, *, steps):
    size = steps * 8

    def chunk(index, carry):
        rows = rows_of(index, size)
        gconv_ref[rows, :] = dot_nt(gproj_ref[rows, :], w_in_ref[...]).astype(BF16)
        return carry

    lax.fori_loop(0, gproj_ref.shape[0] // size, chunk, 0)


def reverse_kernel(
    gup_ref, mid_ref, gt_ref, gain_ref, keep_ref, gate_ref, w_out_ref, w_up_ref,
    gmid_ref, gbranch_ref, gheld_ref, outgoing_ref, gnorm2_ref,
    *, steps,
):
    tokens, width = mid_ref.shape
    batch, hidden = outgoing_ref.shape
    span = tokens // batch
    size = steps * batch
    gain = gain_ref[...]

    def chunk(offset, carry):
        arriving, gnorm2 = carry
        index = span // steps - 1 - offset
        rows = rows_of(index, size)
        gnmid = dot_nt(gup_ref[rows, :], w_up_ref[...])
        middle = mid_ref[rows, :]
        scale = rms(middle)
        unit = middle * scale
        gnorm2 = gnorm2 + jnp.sum(gnmid * unit, axis=0, keepdims=True)
        pulled = gnmid * gain
        gmid = gt_ref[rows, :].astype(F32) + scale * (
            pulled - unit * jnp.mean(pulled * unit, axis=-1, keepdims=True)
        )
        gmid_ref[rows, :] = gmid
        gbranch = gmid.astype(BF16)
        gbranch_ref[rows, :] = gbranch
        gheld_ref[rows, :] = dot_nt(gbranch, w_out_ref[...])

        def back(offset, arriving):
            here = rows_of(index * steps + steps - 1 - offset, batch)
            decay = (1.0 - gate_ref[here, :]) * widen(keep_ref[here, :], hidden)
            return decay * (gheld_ref[here, :] + arriving)

        return lax.fori_loop(0, steps, back, arriving, unroll=8), gnorm2

    first = (jnp.zeros((batch, hidden), F32), jnp.zeros((1, width), F32))
    outgoing, gnorm2 = lax.fori_loop(0, span // steps, chunk, first)
    outgoing_ref[...] = outgoing
    gnorm2_ref[...] = gnorm2


def back_kernel(*refs, chips):
    chip_refs, out_refs = refs[: chips - 1], refs[chips - 1 : 2 * chips - 2]
    (
        mate_ref, mate_out_ref, keep_ref, gate_ref, cand_ref, state_ref, held_ref, gheld_ref, conv_ref, w_in_ref,
        gproj_ref, gbias_ref, edge_ref, stay_ref, send_ref,
    ) = refs[2 * chips - 2 :]
    batch, hidden = mate_out_ref.shape
    span = gate_ref.shape[0] // batch
    chip = lax.shift_right_logical(lax.axis_index("seq"), 1)
    carry_in = jnp.zeros((batch, hidden), F32)
    for source in range(chips - 1, 0, -1):
        prod = from_chip(chip_refs, source, chip, 0)
        state = from_chip(out_refs, source, chip, slice(None))
        carry_in = jnp.where(source > chip, prod * carry_in + state, carry_in)
    carry_in = jnp.where(bit_of("seq", 0) == 0, mate_ref[0] * carry_in + mate_out_ref[...], carry_in)

    def two_steps(offset, carry):
        arriving, gbias = carry
        pair = span // 2 - 1 - offset
        logits = [None, None]
        cands = [None, None]
        before = held_ref[rows_of(jnp.maximum(pair - 1, 0), 2 * batch), :].astype(F32)[batch:]
        prevs = [
            jnp.where(pair == 0, state_ref[...], before),
            held_ref[rows_of(pair, 2 * batch), :].astype(F32)[:batch],
        ]
        for side in (1, 0):
            here = pl.ds(pl.multiple_of((2 * pair + side) * batch, batch), batch)
            gate = gate_ref[here, :]
            keep = widen(keep_ref[here, :], hidden)
            gstate = gheld_ref[here, :] + arriving
            rest = 1.0 - gate
            cands[side] = gstate * gate
            logits[side] = cands[side] * (cand_ref[here, :] - prevs[side] * keep) * rest
            arriving = rest * keep * gstate
            gbias = gbias + logits[side]
        both = rows_of(pair, 2 * batch)
        gproj_ref[both, :hidden] = jnp.concatenate(logits, axis=0).astype(BF16)
        gproj_ref[both, hidden:] = jnp.concatenate(cands, axis=0).astype(BF16)
        return arriving, gbias

    _, gbias = lax.fori_loop(
        0, span // 2, two_steps, (carry_in, jnp.zeros((batch, hidden), F32)), unroll=4
    )
    gbias_ref[...] = jnp.sum(gbias, axis=0, keepdims=True)
    edge_ref[...] = dot_nt(gproj_ref[: edge_ref.shape[0], :], w_in_ref[...]).astype(BF16)
    odd = bit_of("seq", 0) == 1
    wide_gradient(conv_ref, gproj_ref, stay_ref, send_ref, odd)


def deal(tile, shards, first, stay_ref, send_ref, row, odd):
    size = tile.shape[0] // shards
    for even in range(0, shards, 2):
        pair = [tile[(even + k) * size : (even + k + 1) * size].astype(BF16) for k in range(2)]
        index = (first + even) // 2
        stay_ref[index, row : row + size, :] = jnp.where(odd, pair[1], pair[0])
        send_ref[index, row : row + size, :] = jnp.where(odd, pair[0], pair[1])


def wide_gradient(left_ref, right_ref, stay_ref, send_ref, odd):
    shards = 2 * stay_ref.shape[0]
    width = stay_ref.shape[2]
    size = left_ref.shape[1] // shards
    for part in range(right_ref.shape[1] // width):
        tile = dot_tn(left_ref[...], right_ref[:, part * width : (part + 1) * width])
        deal(tile, shards, 0, stay_ref, send_ref, part * size, odd)


def tall_gradient(left_ref, right_ref, stay_ref, send_ref, odd, block=512):
    shards = 2 * stay_ref.shape[0]
    count = left_ref.shape[1] // block
    for part in range(count):
        tile = dot_tn(left_ref[:, part * block : (part + 1) * block], right_ref[...])
        deal(tile, shards // count, part * (shards // count), stay_ref, send_ref, 0, odd)


def weights_kernel(nmid_ref, gup_ref, act_ref, gt_ref, stay_up, send_up, stay_down, send_down):
    odd = bit_of("seq", 0) == 1
    wide_gradient(nmid_ref, gup_ref, stay_up, send_up, odd)
    tall_gradient(act_ref, gt_ref, stay_down, send_down, odd)


def weights_out_kernel(held_ref, gbranch_ref, stay_ref, send_ref):
    tall_gradient(held_ref, gbranch_ref, stay_ref, send_ref, bit_of("seq", 0) == 1)


def bit_of(axis, bit):
    return lax.shift_right_logical(lax.axis_index(axis), bit) & 1


def chunks(count, size, body):
    def step(index, carry):
        body(pl.ds(pl.multiple_of(index * size, size), size))
        return carry

    lax.fori_loop(0, count // size, step, 0)


def core_sum_kernel(*refs, plan):
    sources, (stay_a, send_a, stay_b, send_b) = refs[:-4], refs[-4:]
    base = 0
    for stay_ref, come_ref in zip(sources[::2], sources[1::2]):
        half = stay_ref.shape[1] // 2
        for out_stay, out_send, first, axis in ((stay_a, send_a, 0, plan[0]), (stay_b, send_b, half, plan[1])):
            low = 1 << axis
            for group in range(out_stay.shape[0]):
                fixed = (group >> axis) * 2 * low + (group & (low - 1))
                mine = fixed + low * bit_of("seq", axis + 1)
                other = fixed + low * (1 - bit_of("seq", axis + 1))

                def body(rows):
                    source = pl.ds(pl.multiple_of(rows.start + first, 16), rows.size)
                    goal = pl.ds(pl.multiple_of(rows.start + base, 16), rows.size)
                    out_stay[group, goal, :] = stay_ref[mine, source, :].astype(F32) + come_ref[
                        mine, source, :
                    ].astype(F32)
                    out_send[group, goal, :] = (
                        stay_ref[other, source, :].astype(F32) + come_ref[other, source, :].astype(F32)
                    ).astype(BF16)

                chunks(half, 16, body)
        base += half


def split_sum_kernel(*refs, plan, counts):
    ins = 2 * sum(counts)
    outs = refs[ins:]
    source = 0
    for part, (which, axis) in enumerate(plan):
        out_stay, out_send = outs[2 * part], outs[2 * part + 1]
        low = 1 << axis
        base = 0
        for pair in range(counts[part]):
            stay_ref, come_ref = refs[source], refs[source + 1]
            source += 2
            for group in range(out_stay.shape[0]):
                fixed = (group >> axis) * 2 * low + (group & (low - 1))
                mine = fixed + low * bit_of("seq", which + 1)
                other = fixed + low * (1 - bit_of("seq", which + 1))

                def body(rows):
                    goal = pl.ds(pl.multiple_of(rows.start + base, 16), rows.size)
                    out_stay[group, goal, :] = stay_ref[mine, rows, :].astype(F32) + come_ref[
                        mine, rows, :
                    ].astype(F32)
                    out_send[group, goal, :] = (
                        stay_ref[other, rows, :].astype(F32) + come_ref[other, rows, :].astype(F32)
                    ).astype(BF16)

                chunks(stay_ref.shape[1], 16, body)
            base += stay_ref.shape[1]


def join_sum_kernel(stay_a, come_a, stay_b, come_b, out_stay, out_send):
    width = out_stay.shape[1]
    here = pl.ds(pl.multiple_of(bit_of("dp", 0) * width, width), width)
    there = pl.ds(pl.multiple_of((1 - bit_of("dp", 0)) * width, width), width)
    for stay_ref, come_ref, base in ((stay_a, come_a, 0), (stay_b, come_b, stay_a.shape[1])):

        def body(rows):
            goal = pl.ds(pl.multiple_of(rows.start + base, 16), rows.size)
            out_stay[goal, :] = stay_ref[0, rows, here] + come_ref[0, rows, here].astype(F32)
            out_send[goal, :] = (
                stay_ref[0, rows, there] + come_ref[0, rows, there].astype(F32)
            ).astype(BF16)

        chunks(stay_ref.shape[1], 16, body)


def column_sum_kernel(stay_ref, come_ref, out_stay, out_send, *, bit):
    width = out_stay.shape[1]
    here = pl.ds(pl.multiple_of(bit_of("dp", bit) * width, width), width)
    there = pl.ds(pl.multiple_of((1 - bit_of("dp", bit)) * width, width), width)

    def body(rows):
        out_stay[rows, :] = stay_ref[rows, here] + come_ref[rows, here].astype(F32)
        out_send[rows, :] = (stay_ref[rows, there] + come_ref[rows, there].astype(F32)).astype(BF16)

    chunks(out_stay.shape[0], 16, body)


def round_sum_kernel(stay_ref, come_ref, out_ref):
    def body(rows):
        out_ref[rows, :] = (stay_ref[rows, :].astype(F32) + come_ref[rows, :].astype(F32)).astype(BF16)

    chunks(out_ref.shape[0], 16, body)


def taps_kernel(
    gconv_ref, after_ref, xt_ref, normed_ref, halo_ref, taps_ref, gnorm2_ref, gbias_ref,
    gnormed_ref, stay_ref, send_ref, norm_buf, gconv_buf,
    *, steps,
):
    tokens, width = gconv_ref.shape
    batch = halo_ref.shape[0] // EDGE
    size = steps * batch
    lead = EDGE * batch
    norm_buf[:lead, :] = halo_ref[...].astype(F32)
    gconv_buf[tokens : tokens + after_ref.shape[0], :] = after_ref[...].astype(F32)

    def spread(index, carry):
        rows = rows_of(index, size)
        norm_buf[pl.ds(pl.multiple_of(index * size + lead, 8), size), :] = normed_ref[rows, :].astype(F32)
        gconv_buf[rows, :] = gconv_ref[rows, :].astype(F32)
        return carry

    lax.fori_loop(0, tokens // size, spread, 0)

    def chunk(index, carry):
        gnorm1, gtaps = carry
        rows = rows_of(index, size)
        here = gconv_buf[rows, :]
        gnormed = here * taps_ref[0:1, :]
        sums = []
        for tap in range(KW):
            if tap:
                later = pl.ds(pl.multiple_of(index * size + tap * batch, 8), size)
                gnormed = gnormed + gconv_buf[later, :] * taps_ref[tap : tap + 1, :]
            earlier = pl.ds(pl.multiple_of(index * size + lead - tap * batch, 8), size)
            sums.append(gtaps[tap] + jnp.sum(norm_buf[earlier, :] * here, axis=0, keepdims=True))
        gnormed_ref[rows, :] = gnormed
        values = read(xt_ref, rows)
        gnorm1 = gnorm1 + jnp.sum(gnormed * (values * rms(values)), axis=0, keepdims=True)
        return gnorm1, tuple(sums)

    zero = jnp.zeros((1, width), F32)
    gnorm1, gtaps = lax.fori_loop(0, tokens // size, chunk, (zero, (zero,) * KW))
    places = 2 * stay_ref.shape[0]
    odd = bit_of("seq", 0) == 1
    rows = []
    for place in range(places):
        parts = [
            vector[:, place * (vector.shape[1] // places) : (place + 1) * (vector.shape[1] // places)]
            for vector in (gnorm1, gnorm2_ref[...], *gtaps, gbias_ref[...])
        ]
        row = jnp.concatenate(parts, axis=1)
        if row.shape[1] < width:
            row = jnp.concatenate([row, jnp.zeros((1, width - row.shape[1]), F32)], axis=1)
        rows.append(jnp.broadcast_to(row, (stay_ref.shape[1], width)))
    for index in range(places // 2):
        pair = rows[2 * index : 2 * index + 2]
        stay_ref[index] = jnp.where(odd, pair[1], pair[0]).astype(BF16)
        send_ref[index] = jnp.where(odd, pair[0], pair[1]).astype(BF16)


def inputs_kernel(gnormed_ref, xt_ref, gmid_ref, gain_ref, ginput_ref, wide_buf, *, steps):
    batch, span, width = ginput_ref.shape
    gain = gain_ref[...]

    def chunk(index, carry):
        rows = rows_of(index, steps * batch)
        values = read(xt_ref, rows)
        scale = rms(values)
        unit = values * scale
        pulled = gnormed_ref[rows, :] * gain
        ginput = gmid_ref[rows, :] + scale * (
            pulled - unit * jnp.mean(pulled * unit, axis=-1, keepdims=True)
        )
        write(wide_buf, rows, ginput)
        return carry

    lax.fori_loop(0, span // steps, chunk, 0)
    for row in range(batch):
        ginput_ref[row] = deinterleave(wide_buf, row, batch, span)


def finish_kernel(total_ref, come_ref, *outs, sizes):
    wide = total_ref.shape[1]
    width = 2 * wide
    half = sum(sizes) // 2
    if len(outs) > len(sizes):
        low = bit_of("dp", 0) == 0
        mine, other = [ref[half : half + SMALL, :].astype(F32) for ref in (total_ref, come_ref)]
        row = jnp.concatenate([jnp.where(low, mine, other), jnp.where(low, other, mine)], axis=1)
        column = 0
        for out in outs[len(sizes) :]:
            for line in range(out.shape[0]):
                out[line : line + 1, :] = row[0:1, column : column + out.shape[1]]
                column += out.shape[1]
    for source, bit in ((total_ref, bit_of("dp", 0)), (come_ref, 1 - bit_of("dp", 0))):
        for part_b in range(2):
            row = part_b * (total_ref.shape[0] - half)
            for out, rows in zip(outs, sizes):
                size = out.shape[0]
                count = min(size, rows // 2)
                for start in range(part_b * rows // 2, (part_b + 1) * rows // 2, count):
                    part, low_row = start // size, start % size
                    cols = pl.ds(pl.multiple_of(part * width + bit * wide, wide), wide)
                    out[low_row : low_row + count, cols] = source[row : row + count, :].astype(F32)
                    row += count


def call(
    kernel, name, out_shapes, in_specs, args, scratch=(), limit=2, after=(), work=1
):
    ins, outs = len(args), len(out_shapes)

    def body(*refs):
        inner = list(refs[:ins])
        rest = refs[ins:]
        rest = rest[len(after) :]
        inner += rest[:outs]
        rest = rest[outs:]
        if name in FINAL:
            rest[0][...] = jnp.zeros((8, LANES), F32)
            rest = rest[1:]
        kernel(*inner, *rest)

    args, in_specs, out_shapes = list(args), list(in_specs), list(out_shapes)
    if name in FINAL:
        out_shapes.append(((8, LANES), F32))
    args += after
    in_specs += [pl.BlockSpec(memory_space=pl.ANY)] * len(after)
    return pl.pallas_call(
        body,
        name=name,
        out_shape=[
            (pltpu.HBM if name in FINAL and index < outs else jax.ShapeDtypeStruct)(shape, kind)
            for index, (shape, kind) in enumerate(out_shapes)
        ],
        in_specs=in_specs,
        out_specs=[VMEM_SPEC] * len(out_shapes),
        scratch_shapes=list(scratch),
        compiler_params=pltpu.CompilerParams(vmem_limit_bytes=limit * 2**20),
        cost_estimate=pl.CostEstimate(flops=work, bytes_accessed=1, transcendentals=0),
    )(*args)


def shifted(block, axis, distance):
    devices = range(lax.axis_size(axis))
    route = [(i - distance, i) for i in devices if i - distance in devices]
    return lax.ppermute(block, axis, route)


def swap_by(block, axis, mask):
    return lax.ppermute(block, axis, [(i, i ^ mask) for i in range(lax.axis_size(axis))])


def swap(block, axis, bit):
    return swap_by(block, axis, 1 << bit)


class Order:
    def __init__(self):
        self.last = ()

    def call(self, *args, **kwargs):
        kwargs.setdefault("work", WORK.get(args[1], 1))
        outs = list(call(*args, **kwargs, after=self.last))
        self.last = (min(outs, key=lambda out: out.size * out.dtype.itemsize),)
        if args[1] in FINAL:
            outs.pop()
        return outs


def spread_sum(order, name, sources, out_shapes, late=()):
    places, _, width = sources[0][0].shape
    sizes = tuple(stay.shape[1] for stay, _ in sources)
    rows = sum(sizes)
    levels = places.bit_length() - 1
    order_a = list(range(levels))
    order_b = order_a[::-1]
    half = rows // 2

    def shapes(count, more=0):
        out = []
        for part in (half + more, half):
            out += [((count, part, width), F32), ((count, part, width), BF16)]
        return out

    stay_a, send_a, stay_b, send_b = order.call(
        functools.partial(core_sum_kernel, plan=(order_a[0], order_b[0])), name + "_core",
        shapes(places // 2), [VMEM_SPEC] * (2 * len(sources)), [part for pair in sources for part in pair],
        limit=1,
    )
    for level in range(levels):
        come_a = swap(send_a, "seq", order_a[level] + 1)
        come_b = swap(send_b, "seq", order_b[level] + 1)
        yield None
        if level + 1 == levels:
            break
        plan = []
        for bits in (order_a, order_b):
            bit = bits[level + 1]
            plan.append((bit, bit - sum(done < bit for done in bits[: level + 1])))
        sources = [stay_a, come_a, *(late if level == 0 else ()), stay_b, come_b]
        more = SMALL if late else 0
        stay_a, send_a, stay_b, send_b = order.call(
            functools.partial(
                split_sum_kernel, plan=tuple(plan), counts=(2 if late and level == 0 else 1, 1)
            ),
            name + "_seq", shapes(places // 4 >> level, more), [VMEM_SPEC] * len(sources), sources,
        )
    rows += SMALL if late else 0
    depth = lax.axis_size("dp").bit_length() - 1
    wide = width // 2
    stay, send = order.call(
        join_sum_kernel, name + "_join", [((rows, wide), F32), ((rows, wide), BF16)],
        [VMEM_SPEC] * 4, (stay_a, come_a, stay_b, come_b),
    )
    for bit in range(1, depth - 1):
        wide = wide // 2
        come = swap(send, "dp", bit - 1)
        yield None
        stay, send = order.call(
            functools.partial(column_sum_kernel, bit=bit), name + "_dp",
            [((rows, wide), F32), ((rows, wide), BF16)], [VMEM_SPEC] * 2,
            (stay, come),
        )
    come = swap(send, "dp", depth - 2)
    yield None
    (low,) = order.call(
        round_sum_kernel, name + "_last", [((rows, wide), BF16)], [VMEM_SPEC] * 2, (stay, come)
    )
    come = swap(low, "dp", depth - 1)
    yield None
    (total,) = order.call(
        round_sum_kernel, name + "_total", [((rows, wide), BF16)], [VMEM_SPEC] * 2, (low, come)
    )
    for bit in range(depth - 2, 0, -1):
        come = swap(total, "dp", bit)
        upper = bit_of("dp", bit) == 1
        total = jnp.concatenate(
            [jnp.where(upper, come, total), jnp.where(upper, total, come)], axis=1
        )
    come = swap(total, "dp", 0)
    yield None
    yield order.call(
        functools.partial(finish_kernel, sizes=sizes), name + "_finish", [(shape, F32) for shape in out_shapes],
        [VMEM_SPEC] * 2, (total, come),
    )


def on_device(
    inputs, doc_start, norm1_gain, conv_weight, gate_bias, w_in, w_out, norm2_gain, w_up, w_down, out_grad
):
    batch, span, width = inputs.shape
    hidden = w_out.shape[0]
    inner = w_up.shape[1]
    tokens = batch * span
    lanes = width // LANES
    seq_count, dp_count = lax.axis_size("seq"), lax.axis_size("dp")
    seq_depth, dp_depth = seq_count.bit_length() - 1, dp_count.bit_length() - 1
    pairs = seq_count // 2
    seq_at = lax.axis_index("seq").astype(jnp.int32)
    taps = jnp.transpose(conv_weight)
    gain1, gain2, bias = norm1_gain[None], norm2_gain[None], gate_bias[None]
    order = Order()

    xt, normed, edge, keep = order.call(
        functools.partial(ingest_kernel, steps=16), "ingest",
        [
            ((lanes, tokens, LANES), F32), ((tokens, width), BF16), ((EDGE * batch, width), BF16),
            ((tokens, LANES), F32),
        ],
        [pl.BlockSpec(memory_space=pltpu.HBM)] * 3,
        [pltpu.with_memory_space_constraint(part, pltpu.HBM) for part in (inputs, doc_start, gain1)],
        [
            pltpu.VMEM((batch, span, width), BF16), pltpu.VMEM((batch, span), jnp.int32),
            pltpu.VMEM((1, width), F32), pltpu.SemaphoreType.DMA((batch + 2,)),
        ],
        limit=LIMITS["ingest"],
    )
    halo = shifted(edge, "seq", 1)
    gt, gact = order.call(
        functools.partial(prepare_kernel, steps=64, block=512), "prepare",
        [((tokens, width), BF16), ((tokens, inner // 2), BF16)],
        [VMEM_SPEC] * 2, (out_grad, w_down), [pltpu.VMEM((lanes, tokens, LANES), F32)],
        limit=LIMITS["prepare"],
    )
    conv_out, gate, cand, totals = order.call(
        functools.partial(front_kernel, steps=span, block=256), "front",
        [
            ((tokens, width), BF16), ((tokens, hidden), F32), ((tokens, hidden), F32),
            ((2, batch, hidden), F32),
        ],
        [VMEM_SPEC] * 6, (normed, halo, keep, taps, bias, w_in),
        [pltpu.VMEM((tokens + EDGE * batch, width), F32)],
        limit=LIMITS["front"],
    )
    chips = seq_count // 2
    mate_totals = swap(totals, "seq", 0)
    (chip_totals,) = order.call(
        chip_totals_kernel, "chip_totals", [(totals.shape, F32)], [VMEM_SPEC] * 2, (totals, mate_totals)
    )
    all_totals = [swap_by(chip_totals, "seq", 2 * mask) for mask in range(1, chips)]
    (more,) = order.call(
        functools.partial(prepare_rest_kernel, size=512, block=512), "prepare_rest",
        [((tokens, inner // 2), BF16)], [VMEM_SPEC] * 2, (gt, w_down), limit=LIMITS["prepare_rest"],
    )
    state_in, held, mid, nmid, act, gup = order.call(
        functools.partial(forward_kernel, chips=chips, steps=span, block=256), "forward",
        [
            ((batch, hidden), F32), ((tokens, hidden), BF16), ((tokens, width), F32),
            ((tokens, width), BF16), ((tokens, inner), BF16), ((tokens, inner), BF16),
        ],
        [VMEM_SPEC] * (9 + chips),
        (mate_totals, *all_totals, xt, keep, gate, cand, gact, more, gain2, w_out, w_up),
        limit=LIMITS["forward"],
    )
    up_rows = inner // seq_count
    stay_up, send_up, stay_down, send_down = order.call(
        weights_kernel, "weights", [((pairs, up_rows, width), BF16)] * 4,
        [VMEM_SPEC] * 4, (nmid, gup, act, gt), limit=LIMITS["weights"],
    )
    come_up, come_down = swap(send_up, "seq", 0), swap(send_down, "seq", 0)
    gmid, gbranch, gheld, outgoing, gnorm2 = order.call(
        functools.partial(reverse_kernel, steps=span), "reverse",
        [
            ((tokens, width), F32), ((tokens, width), BF16), ((tokens, hidden), F32),
            ((batch, hidden), F32), ((1, width), F32),
        ],
        [VMEM_SPEC] * 8, (gup, mid, gt, gain2, keep, gate, w_out, w_up),
        limit=LIMITS["reverse"],
    )
    mate_outgoing = swap(outgoing, "seq", 0)
    out_rows = hidden // seq_count
    in_rows = 2 * hidden // seq_count
    stay_out, send_out = order.call(
        weights_out_kernel, "weights_out", [((pairs, out_rows, width), BF16)] * 2,
        [VMEM_SPEC] * 2, (held, gbranch), limit=LIMITS["weights"],
    )
    come_out = swap(send_out, "seq", 0)
    (chip_outgoing,) = order.call(
        chip_outgoing_kernel, "chip_outgoing", [(outgoing.shape, F32)], [VMEM_SPEC] * 4,
        (outgoing, mate_outgoing, totals, mate_totals),
    )
    all_outgoing = [swap_by(chip_outgoing, "seq", 2 * mask) for mask in range(1, chips)]
    first = spread_sum(
        order, "first", [(stay_up, come_up), (stay_down, come_down)],
        [(width // seq_count, inner), (up_rows, width)],
    )
    next(first)
    gproj, gbias, gconv_edge, stay_in, send_in = order.call(
        functools.partial(back_kernel, chips=chips), "back",
        [((tokens, 2 * hidden), BF16), ((1, hidden), F32), ((EDGE * batch, width), BF16)]
        + [((pairs, in_rows, width), BF16)] * 2,
        [VMEM_SPEC] * (8 + 2 * chips),
        (
            *all_totals, *all_outgoing, mate_totals, mate_outgoing, keep, gate, cand, state_in, held, gheld, conv_out, w_in,
        ),
        limit=LIMITS["back"],
    )
    after = shifted(gconv_edge, "seq", -1)
    come_in = swap(send_in, "seq", 0)
    (gconv,) = order.call(
        functools.partial(gconv_kernel, steps=64), "gconv", [((tokens, width), BF16)],
        [VMEM_SPEC] * 2, (gproj, w_in), limit=LIMITS["gconv"],
    )
    order.last = (*order.last, after)
    late = []
    share = width // seq_count
    second = spread_sum(
        order, "second", [(stay_in, come_in), (stay_out, come_out)],
        [
            (share, 2 * hidden), (out_rows, width), (1, share), (1, share), (KW, share),
            (1, hidden // seq_count),
        ],
        late,
    )
    next(first)
    next(second)
    gnormed, stay_small, send_small = order.call(
        functools.partial(taps_kernel, steps=16), "taps",
        [((tokens, width), F32)] + [((pairs, SMALL, width), BF16)] * 2, [VMEM_SPEC] * 8,
        (gconv, after, xt, normed, halo, taps, gnorm2, gbias),
        [
            pltpu.VMEM((tokens + EDGE * batch, width), F32),
            pltpu.VMEM((tokens + EDGE * batch, width), F32),
        ],
        limit=LIMITS["taps"],
    )
    come_small = swap(send_small, "seq", 0)
    next(first)
    stay_small, send_small = order.call(
        functools.partial(split_sum_kernel, plan=((0, 0),), counts=(1,)), "small",
        [((pairs // 2, SMALL, width), F32), ((pairs // 2, SMALL, width), BF16)], [VMEM_SPEC] * 2,
        (stay_small, come_small),
    )
    late += [stay_small, swap(send_small, "seq", 1)]
    (result,) = order.call(
        functools.partial(result_kernel, steps=64), "result", [((batch, span, width), BF16)],
        [VMEM_SPEC] * 3, (act, mid, w_down), [pltpu.VMEM((lanes, tokens, LANES), F32)],
        limit=LIMITS["result"],
    )
    next(second)
    next(first)
    next(second)
    (ginput,) = order.call(
        functools.partial(inputs_kernel, steps=16), "inputs", [((batch, span, width), F32)],
        [VMEM_SPEC] * 4, (gnormed, xt, gmid, gain1), [pltpu.VMEM((lanes, tokens, LANES), F32)],
        limit=LIMITS["inputs"],
    )
    next(first)
    next(second)
    done = {}
    while len(done) < 2:
        for part in (second, first):
            if part not in done:
                outs = next(part)
                if outs is not None:
                    done[part] = outs
    gw_up, gw_down = done[first]
    gw_in, gw_out, gnorm1, gnorm2, gtaps, gbias = done[second]
    return (
        result, ginput, gnorm1[0], jnp.transpose(gtaps), gbias[0], gw_in, gw_out, gnorm2[0], gw_up, gw_down,
    )


def solution(mesh):
    rows, flat = P("dp", "seq", None), P()
    in_specs = (rows, P("dp", "seq")) + (flat,) * 8 + (rows,)
    vec, mat = P("seq"), P("seq", None)
    out_specs = (rows, rows, vec, mat, vec, mat, mat, vec, mat, mat)
    return jax.shard_map(
        on_device, mesh=mesh, in_specs=in_specs, out_specs=out_specs, check_vma=False
    )
```

```python
import functools

import jax
import jax.numpy as jnp
from jax import lax
from jax.experimental import pallas as pl
from jax.experimental.pallas import tpu as pltpu
from jax.sharding import PartitionSpec as P

KW = 4
EPS = 1e-05
EDGE = 8
SMALL = 16
LANES = 128
FINAL = ("result", "inputs", "first_finish", "second_finish")
WORK = {"second_join": 5 * 10**9, "result": 2000000000} | dict.fromkeys(("ingest", "prepare", "front", "forward", "first_seq", "back", "chip_outgoing"), 10**10)
LIMITS = {"ingest": 4, "prepare": 6, "prepare_rest": 3, "front": 7, "forward": 6, "weights": 3, "reverse": 5, "back": 3, "gconv": 3, "taps": 5, "inputs": 7, "result": 7}
F32 = jnp.float32
BF16 = jnp.bfloat16
GELU_C = 0.7978845608028654
GELU_A = 0.044715

VMEM_SPEC = pl.BlockSpec(memory_space=pltpu.VMEM)


def dot(left, right):
    return jnp.dot(left, right, preferred_element_type=F32)


def dot_nt(left, right):
    return lax.dot_general(left, right, (((1,), (1,)), ((), ())), preferred_element_type=F32)


def dot_tn(left, right):
    return lax.dot_general(left, right, (((0,), (0,)), ((), ())), preferred_element_type=F32)


def widen(column, lanes):
    return jnp.concatenate([column] * (lanes // column.shape[1]), axis=1)


def rms(values):
    return lax.rsqrt(jnp.mean(values * values, axis=-1, keepdims=True) + EPS)


def rows_of(index, count):
    return pl.ds(pl.multiple_of(index * count, count), count)


def interleave(buf, row, batch, values):
    for lane in range(buf.shape[0]):
        cols = slice(lane * LANES, (lane + 1) * LANES)
        buf[lane, pl.ds(row, values.shape[0], stride=batch), :] = values[:, cols].astype(F32)


def deinterleave(buf, row, batch, span):
    parts = [buf[lane, pl.ds(row, span, stride=batch), :] for lane in range(buf.shape[0])]
    return jnp.concatenate(parts, axis=1)


def read(buf, rows):
    return jnp.concatenate([buf[lane, rows, :] for lane in range(buf.shape[0])], axis=1)


def write(buf, rows, values):
    for lane in range(buf.shape[0]):
        buf[lane, rows, :] = values[:, lane * LANES : (lane + 1) * LANES]


def ingest_kernel(x_ref, start_ref, gain_ref, xt_ref, normed_ref, edge_ref, keep_ref, x_buf, start_buf, gain_buf, sems, *, steps):
    batch, span, width = x_ref.shape
    size = steps * batch
    copies = [pltpu.make_async_copy(x_ref.at[row], x_buf.at[row], sems.at[row]) for row in range(batch)]
    start_copy = pltpu.make_async_copy(start_ref, start_buf, sems.at[batch])
    gain_copy = pltpu.make_async_copy(gain_ref, gain_buf, sems.at[batch + 1])
    for copy in (start_copy, *copies, gain_copy):
        copy.start()
    start_copy.wait()
    keep = 1.0 - start_buf[...].astype(F32)
    for token in range(span):
        keep_ref[token * batch : (token + 1) * batch, :] = jnp.broadcast_to(
            keep[:, token : token + 1], (batch, LANES)
        )
    for row, copy in enumerate(copies):
        copy.wait()
        interleave(xt_ref, row, batch, x_buf[row])
    gain_copy.wait()

    def chunk(index, carry):
        rows = rows_of(index, size)
        values = read(xt_ref, rows)
        normed_ref[rows, :] = (values * rms(values) * gain_buf[...]).astype(BF16)
        return carry

    lax.fori_loop(0, span // steps, chunk, 0)
    edge_ref[...] = normed_ref[(span - EDGE) * batch :, :]


def prepare_kernel(g_ref, w_down_ref, gt_ref, gact_ref, wide_buf, *, steps, block):
    batch, span, width = g_ref.shape
    size = steps * batch
    for row in range(batch):
        interleave(wide_buf, row, batch, g_ref[row])

    def chunk(index, carry):
        rows = rows_of(index, size)
        g_low = read(wide_buf, rows).astype(BF16)
        gt_ref[rows, :] = g_low
        for part in range(gact_ref.shape[1] // block):
            cols = slice(part * block, (part + 1) * block)
            gact_ref[rows, cols] = dot_nt(g_low, w_down_ref[cols, :]).astype(BF16)
        return carry

    lax.fori_loop(0, span // steps, chunk, 0)


def prepare_rest_kernel(gt_ref, w_down_ref, gact_ref, *, size, block):
    first = w_down_ref.shape[0] - gact_ref.shape[1]

    def chunk(index, carry):
        rows = rows_of(index, size)
        for part in range(gact_ref.shape[1] // block):
            cols = slice(part * block, (part + 1) * block)
            weights = w_down_ref[first + part * block : first + (part + 1) * block, :]
            gact_ref[rows, cols] = dot_nt(gt_ref[rows, :], weights).astype(BF16)
        return carry

    lax.fori_loop(0, gt_ref.shape[0] // size, chunk, 0)


def chip_totals_kernel(mine_ref, mate_ref, chip_ref):
    odd = bit_of("seq", 0) == 1
    prod, state = mine_ref[0], mine_ref[1]
    mate_prod, mate_state = mate_ref[0], mate_ref[1]
    chip_ref[0] = prod * mate_prod
    chip_ref[1] = jnp.where(odd, prod * mate_state + state, mate_prod * state + mate_state)


def chip_outgoing_kernel(mine_ref, mate_ref, totals_ref, mate_totals_ref, chip_ref):
    odd = bit_of("seq", 0) == 1
    mine, mate = mine_ref[...], mate_ref[...]
    chip_ref[...] = jnp.where(odd, mate_totals_ref[0] * mine + mate, totals_ref[0] * mate + mine)


def from_chip(refs, source, chip, part):
    value = refs[0][part]
    for mask in range(2, len(refs) + 1):
        value = jnp.where((source ^ chip) == mask, refs[mask - 1][part], value)
    return value


def front_kernel(
    normed_ref, inside_ref, across_ref, keep_ref, taps_ref, bias_ref, w_ref,
    conv_ref, gate_ref, cand_ref, total_ref, norm_buf,
    *, steps, block,
):
    batch, hidden = total_ref.shape[1:]
    tokens, width = normed_ref.shape
    span = tokens // batch
    size = steps * batch
    lead = EDGE * batch
    norm_buf[:lead, :] = pick_edge(inside_ref[...], across_ref[...], False)

    def chunk(index, carry):
        rows = rows_of(index, size)
        here = normed_ref[rows, :].astype(F32)
        norm_buf[pl.ds(pl.multiple_of(index * size + lead, 8), size), :] = here
        mixing = here * taps_ref[0:1, :]
        for tap in range(1, KW):
            start = pl.multiple_of(index * size + lead - tap * batch, 8)
            mixing = mixing + norm_buf[pl.ds(start, size), :] * taps_ref[tap : tap + 1, :]
        conv_low = mixing.astype(BF16)
        conv_ref[rows, :] = conv_low
        for part in range(hidden // block):
            cols = slice(part * block, (part + 1) * block)
            more = slice(hidden + part * block, hidden + (part + 1) * block)
            gate_ref[rows, cols] = jax.nn.sigmoid(dot(conv_low, w_ref[:, cols]) + bias_ref[:, cols])
            cand_ref[rows, cols] = dot(conv_low, w_ref[:, more])

        def step(offset, carry):
            prod, state = carry
            here = rows_of(index * steps + offset, batch)
            gate = gate_ref[here, :]
            decay = (1.0 - gate) * widen(keep_ref[here, :], hidden)
            return decay * prod, decay * state + gate * cand_ref[here, :]

        return lax.fori_loop(0, steps, step, carry, unroll=8)

    first = (jnp.ones((batch, hidden), F32), jnp.zeros((batch, hidden), F32))
    prod, state = lax.fori_loop(0, span // steps, chunk, first)
    total_ref[0] = prod
    total_ref[1] = state


def forward_kernel(
    mate_ref, *refs, chips, steps, block,
):
    chip_refs = refs[: chips - 1]
    (
        xt_ref, keep_ref, gate_ref, cand_ref, gact_ref, more_ref, gain_ref, w_out_ref, w_up_ref,
        carry_ref, held_ref, mid_ref, nmid_ref, act_ref, gup_ref,
    ) = refs[chips - 1 :]
    batch, hidden = mate_ref.shape[1:]
    inner = w_up_ref.shape[1]
    span = gate_ref.shape[0] // batch
    size = steps * batch
    chip = lax.shift_right_logical(lax.axis_index("seq"), 1)
    carry_in = jnp.zeros((batch, hidden), F32)
    for source in range(chips - 1):
        prod = from_chip(chip_refs, source, chip, 0)
        state = from_chip(chip_refs, source, chip, 1)
        carry_in = jnp.where(source < chip, prod * carry_in + state, carry_in)
    carry_in = jnp.where(bit_of("seq", 0) == 1, mate_ref[0] * carry_in + mate_ref[1], carry_in)
    carry_ref[...] = carry_in
    gain = gain_ref[...]

    def chunk(index, state):
        rows = rows_of(index, size)

        def two_steps(pair, state):
            out = []
            for side in range(2):
                here = pl.ds(pl.multiple_of((index * steps + 2 * pair + side) * batch, batch), batch)
                gate = gate_ref[here, :]
                decay = (1.0 - gate) * widen(keep_ref[here, :], hidden)
                state = decay * state + gate * cand_ref[here, :]
                out.append(state)
            both = rows_of(index * (steps // 2) + pair, 2 * batch)
            held_ref[both, :] = jnp.concatenate(out, axis=0).astype(BF16)
            return state

        state = lax.fori_loop(0, steps // 2, two_steps, state, unroll=4)
        middle = read(xt_ref, rows) + dot(held_ref[rows, :], w_out_ref[...])
        mid_ref[rows, :] = middle
        nmid = (middle * rms(middle) * gain).astype(BF16)
        nmid_ref[rows, :] = nmid
        for part in range(inner // block):
            cols = slice(part * block, (part + 1) * block)
            up = dot(nmid, w_up_ref[:, cols])
            square = up * up
            half = 0.5 + 0.5 * jnp.tanh(up * (GELU_C + (GELU_C * GELU_A) * square))
            act = up * half
            slope = half + act * (1.0 - half) * (2.0 * GELU_C + (6.0 * GELU_C * GELU_A) * square)
            act_ref[rows, cols] = act.astype(BF16)
            start = part * block
            source, start = (gact_ref, start) if start < gact_ref.shape[1] else (more_ref, start - gact_ref.shape[1])
            gact = source[rows, start : start + block].astype(F32)
            gup_ref[rows, cols] = (slope * gact).astype(BF16)
        return state

    lax.fori_loop(0, span // steps, chunk, carry_in)


def result_kernel(act_ref, mid_ref, w_down_ref, result_ref, wide_buf, *, steps):
    batch, span, width = result_ref.shape

    def chunk(index, carry):
        rows = rows_of(index, steps * batch)
        write(wide_buf, rows, mid_ref[rows, :] + dot(act_ref[rows, :], w_down_ref[...]))
        return carry

    lax.fori_loop(0, span // steps, chunk, 0)
    for row in range(batch):
        result_ref[row] = deinterleave(wide_buf, row, batch, span).astype(BF16)


def gconv_kernel(gproj_ref, w_in_ref, gconv_ref, *, steps):
    size = steps * 8

    def chunk(index, carry):
        rows = rows_of(index, size)
        gconv_ref[rows, :] = dot_nt(gproj_ref[rows, :], w_in_ref[...]).astype(BF16)
        return carry

    lax.fori_loop(0, gproj_ref.shape[0] // size, chunk, 0)


def reverse_kernel(
    gup_ref, mid_ref, gt_ref, gain_ref, keep_ref, gate_ref, w_out_ref, w_up_ref,
    gmid_ref, gbranch_ref, gheld_ref, outgoing_ref, gnorm2_ref,
    *, steps,
):
    tokens, width = mid_ref.shape
    batch, hidden = outgoing_ref.shape
    span = tokens // batch
    size = steps * batch
    gain = gain_ref[...]

    def chunk(offset, carry):
        arriving, gnorm2 = carry
        index = span // steps - 1 - offset
        rows = rows_of(index, size)
        gnmid = dot_nt(gup_ref[rows, :], w_up_ref[...])
        middle = mid_ref[rows, :]
        scale = rms(middle)
        unit = middle * scale
        gnorm2 = gnorm2 + jnp.sum(gnmid * unit, axis=0, keepdims=True)
        pulled = gnmid * gain
        gmid = gt_ref[rows, :].astype(F32) + scale * (
            pulled - unit * jnp.mean(pulled * unit, axis=-1, keepdims=True)
        )
        gmid_ref[rows, :] = gmid
        gbranch = gmid.astype(BF16)
        gbranch_ref[rows, :] = gbranch
        gheld_ref[rows, :] = dot_nt(gbranch, w_out_ref[...])

        def back(offset, arriving):
            here = rows_of(index * steps + steps - 1 - offset, batch)
            decay = (1.0 - gate_ref[here, :]) * widen(keep_ref[here, :], hidden)
            return decay * (gheld_ref[here, :] + arriving)

        return lax.fori_loop(0, steps, back, arriving, unroll=8), gnorm2

    first = (jnp.zeros((batch, hidden), F32), jnp.zeros((1, width), F32))
    outgoing, gnorm2 = lax.fori_loop(0, span // steps, chunk, first)
    outgoing_ref[...] = outgoing
    gnorm2_ref[...] = gnorm2


def back_kernel(*refs, chips):
    chip_refs, out_refs = refs[: chips - 1], refs[chips - 1 : 2 * chips - 2]
    (
        mate_ref, mate_out_ref, keep_ref, gate_ref, cand_ref, state_ref, held_ref, gheld_ref, conv_ref, w_in_ref,
        gproj_ref, gbias_ref, edge_ref, stay_ref, send_ref,
    ) = refs[2 * chips - 2 :]
    batch, hidden = mate_out_ref.shape
    span = gate_ref.shape[0] // batch
    chip = lax.shift_right_logical(lax.axis_index("seq"), 1)
    carry_in = jnp.zeros((batch, hidden), F32)
    for source in range(chips - 1, 0, -1):
        prod = from_chip(chip_refs, source, chip, 0)
        state = from_chip(out_refs, source, chip, slice(None))
        carry_in = jnp.where(source > chip, prod * carry_in + state, carry_in)
    carry_in = jnp.where(bit_of("seq", 0) == 0, mate_ref[0] * carry_in + mate_out_ref[...], carry_in)

    def two_steps(offset, carry):
        arriving, gbias = carry
        pair = span // 2 - 1 - offset
        logits = [None, None]
        cands = [None, None]
        before = held_ref[rows_of(jnp.maximum(pair - 1, 0), 2 * batch), :].astype(F32)[batch:]
        prevs = [
            jnp.where(pair == 0, state_ref[...], before),
            held_ref[rows_of(pair, 2 * batch), :].astype(F32)[:batch],
        ]
        for side in (1, 0):
            here = pl.ds(pl.multiple_of((2 * pair + side) * batch, batch), batch)
            gate = gate_ref[here, :]
            keep = widen(keep_ref[here, :], hidden)
            gstate = gheld_ref[here, :] + arriving
            rest = 1.0 - gate
            cands[side] = gstate * gate
            logits[side] = cands[side] * (cand_ref[here, :] - prevs[side] * keep) * rest
            arriving = rest * keep * gstate
            gbias = gbias + logits[side]
        both = rows_of(pair, 2 * batch)
        gproj_ref[both, :hidden] = jnp.concatenate(logits, axis=0).astype(BF16)
        gproj_ref[both, hidden:] = jnp.concatenate(cands, axis=0).astype(BF16)
        return arriving, gbias

    _, gbias = lax.fori_loop(
        0, span // 2, two_steps, (carry_in, jnp.zeros((batch, hidden), F32)), unroll=4
    )
    gbias_ref[...] = jnp.sum(gbias, axis=0, keepdims=True)
    edge_ref[...] = dot_nt(gproj_ref[: edge_ref.shape[0], :], w_in_ref[...]).astype(BF16)
    odd = bit_of("seq", 0) == 1
    wide_gradient(conv_ref, gproj_ref, stay_ref, send_ref, odd)


def deal(tile, shards, first, stay_ref, send_ref, row, odd):
    size = tile.shape[0] // shards
    for even in range(0, shards, 2):
        pair = [tile[(even + k) * size : (even + k + 1) * size].astype(BF16) for k in range(2)]
        index = (first + even) // 2
        stay_ref[index, row : row + size, :] = jnp.where(odd, pair[1], pair[0])
        send_ref[index, row : row + size, :] = jnp.where(odd, pair[0], pair[1])


def wide_gradient(left_ref, right_ref, stay_ref, send_ref, odd):
    shards = 2 * stay_ref.shape[0]
    width = stay_ref.shape[2]
    size = left_ref.shape[1] // shards
    for part in range(right_ref.shape[1] // width):
        tile = dot_tn(left_ref[...], right_ref[:, part * width : (part + 1) * width])
        deal(tile, shards, 0, stay_ref, send_ref, part * size, odd)


def tall_gradient(left_ref, right_ref, stay_ref, send_ref, odd, block=512):
    shards = 2 * stay_ref.shape[0]
    count = left_ref.shape[1] // block
    for part in range(count):
        tile = dot_tn(left_ref[:, part * block : (part + 1) * block], right_ref[...])
        deal(tile, shards // count, part * (shards // count), stay_ref, send_ref, 0, odd)


def weights_kernel(nmid_ref, gup_ref, act_ref, gt_ref, stay_up, send_up, stay_down, send_down):
    odd = bit_of("seq", 0) == 1
    wide_gradient(nmid_ref, gup_ref, stay_up, send_up, odd)
    tall_gradient(act_ref, gt_ref, stay_down, send_down, odd)


def weights_out_kernel(held_ref, gbranch_ref, stay_ref, send_ref):
    tall_gradient(held_ref, gbranch_ref, stay_ref, send_ref, bit_of("seq", 0) == 1)


def bit_of(axis, bit):
    return lax.shift_right_logical(lax.axis_index(axis), bit) & 1


def chunks(count, size, body):
    def step(index, carry):
        body(pl.ds(pl.multiple_of(index * size, size), size))
        return carry

    lax.fori_loop(0, count // size, step, 0)


def core_sum_kernel(*refs, plan):
    sources, (stay_a, send_a, stay_b, send_b) = refs[:-4], refs[-4:]
    base = 0
    for stay_ref, come_ref in zip(sources[::2], sources[1::2]):
        half = stay_ref.shape[1] // 2
        for out_stay, out_send, first, axis in ((stay_a, send_a, 0, plan[0]), (stay_b, send_b, half, plan[1])):
            low = 1 << axis
            for group in range(out_stay.shape[0]):
                fixed = (group >> axis) * 2 * low + (group & (low - 1))
                mine = fixed + low * bit_of("seq", axis + 1)
                other = fixed + low * (1 - bit_of("seq", axis + 1))

                def body(rows):
                    source = pl.ds(pl.multiple_of(rows.start + first, 16), rows.size)
                    goal = pl.ds(pl.multiple_of(rows.start + base, 16), rows.size)
                    out_stay[group, goal, :] = stay_ref[mine, source, :].astype(F32) + come_ref[
                        mine, source, :
                    ].astype(F32)
                    out_send[group, goal, :] = (
                        stay_ref[other, source, :].astype(F32) + come_ref[other, source, :].astype(F32)
                    ).astype(BF16)

                chunks(half, 16, body)
        base += half


def split_sum_kernel(*refs, plan, counts):
    ins = 2 * sum(counts)
    outs = refs[ins:]
    source = 0
    for part, (which, axis) in enumerate(plan):
        out_stay, out_send = outs[2 * part], outs[2 * part + 1]
        low = 1 << axis
        base = 0
        for pair in range(counts[part]):
            stay_ref, come_ref = refs[source], refs[source + 1]
            source += 2
            for group in range(out_stay.shape[0]):
                fixed = (group >> axis) * 2 * low + (group & (low - 1))
                mine = fixed + low * bit_of("seq", which + 1)
                other = fixed + low * (1 - bit_of("seq", which + 1))

                def body(rows):
                    goal = pl.ds(pl.multiple_of(rows.start + base, 16), rows.size)
                    out_stay[group, goal, :] = stay_ref[mine, rows, :].astype(F32) + come_ref[
                        mine, rows, :
                    ].astype(F32)
                    out_send[group, goal, :] = (
                        stay_ref[other, rows, :].astype(F32) + come_ref[other, rows, :].astype(F32)
                    ).astype(BF16)

                chunks(stay_ref.shape[1], 16, body)
            base += stay_ref.shape[1]


def join_sum_kernel(stay_a, come_a, stay_b, come_b, out_stay, out_send):
    width = out_stay.shape[1]
    here = pl.ds(pl.multiple_of(bit_of("dp", 0) * width, width), width)
    there = pl.ds(pl.multiple_of((1 - bit_of("dp", 0)) * width, width), width)
    for stay_ref, come_ref, base in ((stay_a, come_a, 0), (stay_b, come_b, stay_a.shape[1])):

        def body(rows):
            goal = pl.ds(pl.multiple_of(rows.start + base, 16), rows.size)
            out_stay[goal, :] = stay_ref[0, rows, here] + come_ref[0, rows, here].astype(F32)
            out_send[goal, :] = (
                stay_ref[0, rows, there] + come_ref[0, rows, there].astype(F32)
            ).astype(BF16)

        chunks(stay_ref.shape[1], 16, body)


def column_sum_kernel(stay_ref, come_ref, out_stay, out_send, *, bit):
    width = out_stay.shape[1]
    here = pl.ds(pl.multiple_of(bit_of("dp", bit) * width, width), width)
    there = pl.ds(pl.multiple_of((1 - bit_of("dp", bit)) * width, width), width)

    def body(rows):
        out_stay[rows, :] = stay_ref[rows, here] + come_ref[rows, here].astype(F32)
        out_send[rows, :] = (stay_ref[rows, there] + come_ref[rows, there].astype(F32)).astype(BF16)

    chunks(out_stay.shape[0], 16, body)


def round_sum_kernel(stay_ref, come_ref, out_ref):
    def body(rows):
        out_ref[rows, :] = (stay_ref[rows, :].astype(F32) + come_ref[rows, :].astype(F32)).astype(BF16)

    chunks(out_ref.shape[0], 16, body)


def taps_kernel(
    gconv_ref, after_ref, ahead_ref, xt_ref, normed_ref, halo_ref, across_ref, taps_ref, gnorm2_ref, gbias_ref,
    gnormed_ref, stay_ref, send_ref, norm_buf, gconv_buf,
    *, steps,
):
    tokens, width = gconv_ref.shape
    batch = halo_ref.shape[0] // EDGE
    size = steps * batch
    lead = EDGE * batch
    norm_buf[:lead, :] = pick_edge(halo_ref[...], across_ref[...], False)
    gconv_buf[tokens : tokens + after_ref.shape[0], :] = pick_edge(after_ref[...], ahead_ref[...], True)

    def spread(index, carry):
        rows = rows_of(index, size)
        norm_buf[pl.ds(pl.multiple_of(index * size + lead, 8), size), :] = normed_ref[rows, :].astype(F32)
        gconv_buf[rows, :] = gconv_ref[rows, :].astype(F32)
        return carry

    lax.fori_loop(0, tokens // size, spread, 0)

    def chunk(index, carry):
        gnorm1, gtaps = carry
        rows = rows_of(index, size)
        here = gconv_buf[rows, :]
        gnormed = here * taps_ref[0:1, :]
        sums = []
        for tap in range(KW):
            if tap:
                later = pl.ds(pl.multiple_of(index * size + tap * batch, 8), size)
                gnormed = gnormed + gconv_buf[later, :] * taps_ref[tap : tap + 1, :]
            earlier = pl.ds(pl.multiple_of(index * size + lead - tap * batch, 8), size)
            sums.append(gtaps[tap] + jnp.sum(norm_buf[earlier, :] * here, axis=0, keepdims=True))
        gnormed_ref[rows, :] = gnormed
        values = read(xt_ref, rows)
        gnorm1 = gnorm1 + jnp.sum(gnormed * (values * rms(values)), axis=0, keepdims=True)
        return gnorm1, tuple(sums)

    zero = jnp.zeros((1, width), F32)
    gnorm1, gtaps = lax.fori_loop(0, tokens // size, chunk, (zero, (zero,) * KW))
    places = 2 * stay_ref.shape[0]
    odd = bit_of("seq", 0) == 1
    rows = []
    for place in range(places):
        parts = [
            vector[:, place * (vector.shape[1] // places) : (place + 1) * (vector.shape[1] // places)]
            for vector in (gnorm1, gnorm2_ref[...], *gtaps, gbias_ref[...])
        ]
        row = jnp.concatenate(parts, axis=1)
        if row.shape[1] < width:
            row = jnp.concatenate([row, jnp.zeros((1, width - row.shape[1]), F32)], axis=1)
        rows.append(jnp.broadcast_to(row, (stay_ref.shape[1], width)))
    for index in range(places // 2):
        pair = rows[2 * index : 2 * index + 2]
        stay_ref[index] = jnp.where(odd, pair[1], pair[0]).astype(BF16)
        send_ref[index] = jnp.where(odd, pair[0], pair[1]).astype(BF16)


def inputs_kernel(gnormed_ref, xt_ref, gmid_ref, gain_ref, ginput_ref, wide_buf, *, steps):
    batch, span, width = ginput_ref.shape
    gain = gain_ref[...]

    def chunk(index, carry):
        rows = rows_of(index, steps * batch)
        values = read(xt_ref, rows)
        scale = rms(values)
        unit = values * scale
        pulled = gnormed_ref[rows, :] * gain
        ginput = gmid_ref[rows, :] + scale * (
            pulled - unit * jnp.mean(pulled * unit, axis=-1, keepdims=True)
        )
        write(wide_buf, rows, ginput)
        return carry

    lax.fori_loop(0, span // steps, chunk, 0)
    for row in range(batch):
        ginput_ref[row] = deinterleave(wide_buf, row, batch, span)


def finish_kernel(total_ref, come_ref, *outs, sizes):
    wide = total_ref.shape[1]
    width = 2 * wide
    half = sum(sizes) // 2
    if len(outs) > len(sizes):
        low = bit_of("dp", 0) == 0
        mine, other = [ref[half : half + SMALL, :].astype(F32) for ref in (total_ref, come_ref)]
        row = jnp.concatenate([jnp.where(low, mine, other), jnp.where(low, other, mine)], axis=1)
        column = 0
        for out in outs[len(sizes) :]:
            for line in range(out.shape[0]):
                out[line : line + 1, :] = row[0:1, column : column + out.shape[1]]
                column += out.shape[1]
    for source, bit in ((total_ref, bit_of("dp", 0)), (come_ref, 1 - bit_of("dp", 0))):
        for part_b in range(2):
            row = part_b * (total_ref.shape[0] - half)
            for out, rows in zip(outs, sizes):
                size = out.shape[0]
                count = min(size, rows // 2)
                for start in range(part_b * rows // 2, (part_b + 1) * rows // 2, count):
                    part, low_row = start // size, start % size
                    cols = pl.ds(pl.multiple_of(part * width + bit * wide, wide), wide)
                    out[low_row : low_row + count, cols] = source[row : row + count, :].astype(F32)
                    row += count


def call(
    kernel, name, out_shapes, in_specs, args, scratch=(), limit=2, after=(), work=1
):
    ins, outs = len(args), len(out_shapes)

    def body(*refs):
        inner = list(refs[:ins])
        rest = refs[ins:]
        rest = rest[len(after) :]
        inner += rest[:outs]
        rest = rest[outs:]
        if name in FINAL:
            rest[0][...] = jnp.zeros((8, LANES), F32)
            rest = rest[1:]
        kernel(*inner, *rest)

    args, in_specs, out_shapes = list(args), list(in_specs), list(out_shapes)
    if name in FINAL:
        out_shapes.append(((8, LANES), F32))
    args += after
    in_specs += [pl.BlockSpec(memory_space=pl.ANY)] * len(after)
    return pl.pallas_call(
        body,
        name=name,
        out_shape=[
            (pltpu.HBM if name in FINAL and index < outs else jax.ShapeDtypeStruct)(shape, kind)
            for index, (shape, kind) in enumerate(out_shapes)
        ],
        in_specs=in_specs,
        out_specs=[VMEM_SPEC] * len(out_shapes),
        scratch_shapes=list(scratch),
        compiler_params=pltpu.CompilerParams(vmem_limit_bytes=limit * 2**20),
        cost_estimate=pl.CostEstimate(flops=work, bytes_accessed=1, transcendentals=0),
    )(*args)


def neighbour(block, axis):
    count = lax.axis_size(axis)
    inside = swap_by(block, axis, 1)
    across = lax.ppermute(block, axis, [(i, (i + 1 if i % 2 else i - 1) % count) for i in range(count)])
    return inside, across


def pick_edge(inside, across, ahead):
    place = lax.axis_index("seq")
    end = lax.axis_size("seq") - 1 if ahead else 0
    odd = bit_of("seq", 0) == 1
    value = jnp.where(odd != ahead, inside.astype(F32), across.astype(F32))
    return jnp.where(place == end, jnp.zeros_like(value), value)


def swap_by(block, axis, mask):
    return lax.ppermute(block, axis, [(i, i ^ mask) for i in range(lax.axis_size(axis))])


def swap(block, axis, bit):
    return swap_by(block, axis, 1 << bit)


class Order:
    def __init__(self):
        self.last = ()

    def call(self, *args, **kwargs):
        kwargs.setdefault("work", WORK.get(args[1], 1))
        outs = list(call(*args, **kwargs, after=self.last))
        self.last = (min(outs, key=lambda out: out.size * out.dtype.itemsize),)
        if args[1] in FINAL:
            outs.pop()
        return outs


def spread_sum(order, name, sources, out_shapes, late=()):
    places, _, width = sources[0][0].shape
    sizes = tuple(stay.shape[1] for stay, _ in sources)
    rows = sum(sizes)
    levels = places.bit_length() - 1
    order_a = list(range(levels))
    order_b = order_a[::-1]
    half = rows // 2

    def shapes(count, more=0):
        out = []
        for part in (half + more, half):
            out += [((count, part, width), F32), ((count, part, width), BF16)]
        return out

    stay_a, send_a, stay_b, send_b = order.call(
        functools.partial(core_sum_kernel, plan=(order_a[0], order_b[0])), name + "_core",
        shapes(places // 2), [VMEM_SPEC] * (2 * len(sources)), [part for pair in sources for part in pair],
        limit=1,
    )
    for level in range(levels):
        come_a = swap(send_a, "seq", order_a[level] + 1)
        come_b = swap(send_b, "seq", order_b[level] + 1)
        yield None
        if level + 1 == levels:
            break
        plan = []
        for bits in (order_a, order_b):
            bit = bits[level + 1]
            plan.append((bit, bit - sum(done < bit for done in bits[: level + 1])))
        sources = [stay_a, come_a, *(late if level == 0 else ()), stay_b, come_b]
        more = SMALL if late else 0
        stay_a, send_a, stay_b, send_b = order.call(
            functools.partial(
                split_sum_kernel, plan=tuple(plan), counts=(2 if late and level == 0 else 1, 1)
            ),
            name + "_seq", shapes(places // 4 >> level, more), [VMEM_SPEC] * len(sources), sources,
        )
    rows += SMALL if late else 0
    depth = lax.axis_size("dp").bit_length() - 1
    wide = width // 2
    stay, send = order.call(
        join_sum_kernel, name + "_join", [((rows, wide), F32), ((rows, wide), BF16)],
        [VMEM_SPEC] * 4, (stay_a, come_a, stay_b, come_b),
    )
    for bit in range(1, depth - 1):
        wide = wide // 2
        come = swap(send, "dp", bit - 1)
        yield None
        stay, send = order.call(
            functools.partial(column_sum_kernel, bit=bit), name + "_dp",
            [((rows, wide), F32), ((rows, wide), BF16)], [VMEM_SPEC] * 2,
            (stay, come),
        )
    come = swap(send, "dp", depth - 2)
    yield None
    (low,) = order.call(
        round_sum_kernel, name + "_last", [((rows, wide), BF16)], [VMEM_SPEC] * 2, (stay, come)
    )
    come = swap(low, "dp", depth - 1)
    yield None
    (total,) = order.call(
        round_sum_kernel, name + "_total", [((rows, wide), BF16)], [VMEM_SPEC] * 2, (low, come)
    )
    for bit in range(depth - 2, 0, -1):
        come = swap(total, "dp", bit)
        upper = bit_of("dp", bit) == 1
        total = jnp.concatenate(
            [jnp.where(upper, come, total), jnp.where(upper, total, come)], axis=1
        )
    come = swap(total, "dp", 0)
    yield None
    yield order.call(
        functools.partial(finish_kernel, sizes=sizes), name + "_finish", [(shape, F32) for shape in out_shapes],
        [VMEM_SPEC] * 2, (total, come),
    )


def on_device(
    inputs, doc_start, norm1_gain, conv_weight, gate_bias, w_in, w_out, norm2_gain, w_up, w_down, out_grad
):
    batch, span, width = inputs.shape
    hidden = w_out.shape[0]
    inner = w_up.shape[1]
    tokens = batch * span
    lanes = width // LANES
    seq_count, dp_count = lax.axis_size("seq"), lax.axis_size("dp")
    seq_depth, dp_depth = seq_count.bit_length() - 1, dp_count.bit_length() - 1
    pairs = seq_count // 2
    seq_at = lax.axis_index("seq").astype(jnp.int32)
    taps = jnp.transpose(conv_weight)
    gain1, gain2, bias = norm1_gain[None], norm2_gain[None], gate_bias[None]
    order = Order()

    xt, normed, edge, keep = order.call(
        functools.partial(ingest_kernel, steps=span), "ingest",
        [
            ((lanes, tokens, LANES), F32), ((tokens, width), BF16), ((EDGE * batch, width), BF16),
            ((tokens, LANES), F32),
        ],
        [pl.BlockSpec(memory_space=pltpu.HBM)] * 3,
        [pltpu.with_memory_space_constraint(part, pltpu.HBM) for part in (inputs, doc_start, gain1)],
        [
            pltpu.VMEM((batch, span, width), BF16), pltpu.VMEM((batch, span), jnp.int32),
            pltpu.VMEM((1, width), F32), pltpu.SemaphoreType.DMA((batch + 2,)),
        ],
        limit=LIMITS["ingest"],
    )
    halo = neighbour(edge, "seq")
    gt, gact = order.call(
        functools.partial(prepare_kernel, steps=span, block=256), "prepare",
        [((tokens, width), BF16), ((tokens, inner // 2), BF16)],
        [VMEM_SPEC] * 2, (out_grad, w_down), [pltpu.VMEM((lanes, tokens, LANES), F32)],
        limit=LIMITS["prepare"],
    )
    conv_out, gate, cand, totals = order.call(
        functools.partial(front_kernel, steps=span, block=256), "front",
        [
            ((tokens, width), BF16), ((tokens, hidden), F32), ((tokens, hidden), F32),
            ((2, batch, hidden), F32),
        ],
        [VMEM_SPEC] * 7, (normed, *halo, keep, taps, bias, w_in),
        [pltpu.VMEM((tokens + EDGE * batch, width), F32)],
        limit=LIMITS["front"],
    )
    chips = seq_count // 2
    mate_totals = swap(totals, "seq", 0)
    (chip_totals,) = order.call(
        chip_totals_kernel, "chip_totals", [(totals.shape, F32)], [VMEM_SPEC] * 2, (totals, mate_totals)
    )
    all_totals = [swap_by(chip_totals, "seq", 2 * mask) for mask in range(1, chips)]
    (more,) = order.call(
        functools.partial(prepare_rest_kernel, size=tokens, block=256), "prepare_rest",
        [((tokens, inner // 2), BF16)], [VMEM_SPEC] * 2, (gt, w_down), limit=LIMITS["prepare_rest"],
    )
    state_in, held, mid, nmid, act, gup = order.call(
        functools.partial(forward_kernel, chips=chips, steps=span, block=256), "forward",
        [
            ((batch, hidden), F32), ((tokens, hidden), BF16), ((tokens, width), F32),
            ((tokens, width), BF16), ((tokens, inner), BF16), ((tokens, inner), BF16),
        ],
        [VMEM_SPEC] * (9 + chips),
        (mate_totals, *all_totals, xt, keep, gate, cand, gact, more, gain2, w_out, w_up),
        limit=LIMITS["forward"],
    )
    up_rows = inner // seq_count
    stay_up, send_up, stay_down, send_down = order.call(
        weights_kernel, "weights", [((pairs, up_rows, width), BF16)] * 4,
        [VMEM_SPEC] * 4, (nmid, gup, act, gt), limit=LIMITS["weights"],
    )
    come_up, come_down = swap(send_up, "seq", 0), swap(send_down, "seq", 0)
    gmid, gbranch, gheld, outgoing, gnorm2 = order.call(
        functools.partial(reverse_kernel, steps=span), "reverse",
        [
            ((tokens, width), F32), ((tokens, width), BF16), ((tokens, hidden), F32),
            ((batch, hidden), F32), ((1, width), F32),
        ],
        [VMEM_SPEC] * 8, (gup, mid, gt, gain2, keep, gate, w_out, w_up),
        limit=LIMITS["reverse"],
    )
    mate_outgoing = swap(outgoing, "seq", 0)
    out_rows = hidden // seq_count
    in_rows = 2 * hidden // seq_count
    stay_out, send_out = order.call(
        weights_out_kernel, "weights_out", [((pairs, out_rows, width), BF16)] * 2,
        [VMEM_SPEC] * 2, (held, gbranch), limit=LIMITS["weights"],
    )
    come_out = swap(send_out, "seq", 0)
    (chip_outgoing,) = order.call(
        chip_outgoing_kernel, "chip_outgoing", [(outgoing.shape, F32)], [VMEM_SPEC] * 4,
        (outgoing, mate_outgoing, totals, mate_totals),
    )
    all_outgoing = [swap_by(chip_outgoing, "seq", 2 * mask) for mask in range(1, chips)]
    first = spread_sum(
        order, "first", [(stay_up, come_up), (stay_down, come_down)],
        [(width // seq_count, inner), (up_rows, width)],
    )
    next(first)
    gproj, gbias, gconv_edge, stay_in, send_in = order.call(
        functools.partial(back_kernel, chips=chips), "back",
        [((tokens, 2 * hidden), BF16), ((1, hidden), F32), ((EDGE * batch, width), BF16)]
        + [((pairs, in_rows, width), BF16)] * 2,
        [VMEM_SPEC] * (8 + 2 * chips),
        (
            *all_totals, *all_outgoing, mate_totals, mate_outgoing, keep, gate, cand, state_in, held, gheld, conv_out, w_in,
        ),
        limit=LIMITS["back"],
    )
    after = neighbour(gconv_edge, "seq")
    come_in = swap(send_in, "seq", 0)
    (gconv,) = order.call(
        functools.partial(gconv_kernel, steps=span), "gconv", [((tokens, width), BF16)],
        [VMEM_SPEC] * 2, (gproj, w_in), limit=LIMITS["gconv"],
    )
    order.last = (*order.last, *after)
    late = []
    share = width // seq_count
    second = spread_sum(
        order, "second", [(stay_in, come_in), (stay_out, come_out)],
        [
            (share, 2 * hidden), (out_rows, width), (1, share), (1, share), (KW, share),
            (1, hidden // seq_count),
        ],
        late,
    )
    next(first)
    gnormed, stay_small, send_small = order.call(
        functools.partial(taps_kernel, steps=16), "taps",
        [((tokens, width), F32)] + [((pairs, SMALL, width), BF16)] * 2, [VMEM_SPEC] * 10,
        (gconv, *after, xt, normed, *halo, taps, gnorm2, gbias),
        [
            pltpu.VMEM((tokens + EDGE * batch, width), F32),
            pltpu.VMEM((tokens + EDGE * batch, width), F32),
        ],
        limit=LIMITS["taps"],
    )
    come_small = swap(send_small, "seq", 0)
    next(second)
    next(first)
    stay_small, send_small = order.call(
        functools.partial(split_sum_kernel, plan=((0, 0),), counts=(1,)), "small",
        [((pairs // 2, SMALL, width), F32), ((pairs // 2, SMALL, width), BF16)], [VMEM_SPEC] * 2,
        (stay_small, come_small),
    )
    late += [stay_small, swap(send_small, "seq", 1)]
    (result,) = order.call(
        functools.partial(result_kernel, steps=span), "result", [((batch, span, width), BF16)],
        [VMEM_SPEC] * 3, (act, mid, w_down), [pltpu.VMEM((lanes, tokens, LANES), F32)],
        limit=LIMITS["result"],
    )
    next(second)
    next(first)
    next(second)
    (ginput,) = order.call(
        functools.partial(inputs_kernel, steps=64), "inputs", [((batch, span, width), F32)],
        [VMEM_SPEC] * 4, (gnormed, xt, gmid, gain1), [pltpu.VMEM((lanes, tokens, LANES), F32)],
        limit=LIMITS["inputs"],
    )
    next(first)
    next(second)
    done = {}
    while len(done) < 2:
        for part in (second, first):
            if part not in done:
                outs = next(part)
                if outs is not None:
                    done[part] = outs
    gw_up, gw_down = done[first]
    gw_in, gw_out, gnorm1, gnorm2, gtaps, gbias = done[second]
    return (
        result, ginput, gnorm1[0], jnp.transpose(gtaps), gbias[0], gw_in, gw_out, gnorm2[0], gw_up, gw_down,
    )


def solution(mesh):
    rows, flat = P("dp", "seq", None), P()
    in_specs = (rows, P("dp", "seq")) + (flat,) * 8 + (rows,)
    vec, mat = P("seq"), P("seq", None)
    out_specs = (rows, rows, vec, mat, vec, mat, mat, vec, mat, mat)
    return jax.shard_map(
        on_device, mesh=mesh, in_specs=in_specs, out_specs=out_specs, check_vma=False
    )
```

```python
import functools

import jax
import jax.numpy as jnp
from jax import lax
from jax.experimental import pallas as pl
from jax.experimental.pallas import tpu as pltpu
from jax.sharding import PartitionSpec as P

KW = 4
EPS = 1e-05
EDGE = 8
SMALL = 16
LANES = 128
FINAL = ("result", "inputs", "first_finish", "second_finish")
WORK = {"second_join": 5 * 10**9, "result": 2000000000} | dict.fromkeys(("ingest", "prepare", "front", "forward", "first_seq", "back", "chip_outgoing"), 10**10)
LIMITS = {"ingest": 4, "prepare": 6, "prepare_rest": 3, "front": 7, "forward": 6, "weights": 3, "reverse": 5, "back": 3, "gconv": 3, "taps": 5, "inputs": 7, "result": 7}
F32 = jnp.float32
BF16 = jnp.bfloat16
GELU_C = 0.7978845608028654
GELU_A = 0.044715

VMEM_SPEC = pl.BlockSpec(memory_space=pltpu.VMEM)


def dot(left, right):
    return jnp.dot(left, right, preferred_element_type=F32)


def dot_nt(left, right):
    return lax.dot_general(left, right, (((1,), (1,)), ((), ())), preferred_element_type=F32)


def dot_tn(left, right):
    return lax.dot_general(left, right, (((0,), (0,)), ((), ())), preferred_element_type=F32)


def widen(column, lanes):
    return jnp.concatenate([column] * (lanes // column.shape[1]), axis=1)


def rms(values):
    return lax.rsqrt(jnp.mean(values * values, axis=-1, keepdims=True) + EPS)


def rows_of(index, count):
    return pl.ds(pl.multiple_of(index * count, count), count)


def interleave(buf, row, batch, values):
    for lane in range(buf.shape[0]):
        cols = slice(lane * LANES, (lane + 1) * LANES)
        buf[lane, pl.ds(row, values.shape[0], stride=batch), :] = values[:, cols].astype(F32)


def deinterleave(buf, row, batch, span):
    parts = [buf[lane, pl.ds(row, span, stride=batch), :] for lane in range(buf.shape[0])]
    return jnp.concatenate(parts, axis=1)


def read(buf, rows):
    return jnp.concatenate([buf[lane, rows, :] for lane in range(buf.shape[0])], axis=1)


def write(buf, rows, values):
    for lane in range(buf.shape[0]):
        buf[lane, rows, :] = values[:, lane * LANES : (lane + 1) * LANES]


def ingest_kernel(x_ref, start_ref, gain_ref, xt_ref, normed_ref, edge_ref, keep_ref, x_buf, start_buf, gain_buf, sems, *, steps):
    batch, span, width = x_ref.shape
    size = steps * batch
    copies = [pltpu.make_async_copy(x_ref.at[row], x_buf.at[row], sems.at[row]) for row in range(batch)]
    start_copy = pltpu.make_async_copy(start_ref, start_buf, sems.at[batch])
    gain_copy = pltpu.make_async_copy(gain_ref, gain_buf, sems.at[batch + 1])
    for copy in (start_copy, *copies, gain_copy):
        copy.start()
    start_copy.wait()
    keep = 1.0 - start_buf[...].astype(F32)
    for token in range(span):
        keep_ref[token * batch : (token + 1) * batch, :] = jnp.broadcast_to(
            keep[:, token : token + 1], (batch, LANES)
        )
    for row, copy in enumerate(copies):
        copy.wait()
        interleave(xt_ref, row, batch, x_buf[row])
    gain_copy.wait()

    def chunk(index, carry):
        rows = rows_of(index, size)
        values = read(xt_ref, rows)
        normed_ref[rows, :] = (values * rms(values) * gain_buf[...]).astype(BF16)
        return carry

    lax.fori_loop(0, span // steps, chunk, 0)
    edge_ref[...] = normed_ref[(span - EDGE) * batch :, :]


def prepare_kernel(g_ref, w_down_ref, gt_ref, gact_ref, wide_buf, *, steps, block):
    batch, span, width = g_ref.shape
    size = steps * batch
    for row in range(batch):
        interleave(wide_buf, row, batch, g_ref[row])

    def chunk(index, carry):
        rows = rows_of(index, size)
        g_low = read(wide_buf, rows).astype(BF16)
        gt_ref[rows, :] = g_low
        for part in range(gact_ref.shape[1] // block):
            cols = slice(part * block, (part + 1) * block)
            gact_ref[rows, cols] = dot_nt(g_low, w_down_ref[cols, :]).astype(BF16)
        return carry

    lax.fori_loop(0, span // steps, chunk, 0)


def prepare_rest_kernel(gt_ref, w_down_ref, gact_ref, *, size, block):
    first = w_down_ref.shape[0] - gact_ref.shape[1]

    def chunk(index, carry):
        rows = rows_of(index, size)
        for part in range(gact_ref.shape[1] // block):
            cols = slice(part * block, (part + 1) * block)
            weights = w_down_ref[first + part * block : first + (part + 1) * block, :]
            gact_ref[rows, cols] = dot_nt(gt_ref[rows, :], weights).astype(BF16)
        return carry

    lax.fori_loop(0, gt_ref.shape[0] // size, chunk, 0)


def chip_totals_kernel(mine_ref, mate_ref, chip_ref):
    odd = bit_of("seq", 0) == 1
    prod, state = mine_ref[0], mine_ref[1]
    mate_prod, mate_state = mate_ref[0], mate_ref[1]
    chip_ref[0] = prod * mate_prod
    chip_ref[1] = jnp.where(odd, prod * mate_state + state, mate_prod * state + mate_state)


def chip_outgoing_kernel(mine_ref, mate_ref, totals_ref, mate_totals_ref, chip_ref):
    odd = bit_of("seq", 0) == 1
    mine, mate = mine_ref[...], mate_ref[...]
    chip_ref[...] = jnp.where(odd, mate_totals_ref[0] * mine + mate, totals_ref[0] * mate + mine)


def from_chip(refs, source, chip, part):
    value = refs[0][part]
    for mask in range(2, len(refs) + 1):
        value = jnp.where((source ^ chip) == mask, refs[mask - 1][part], value)
    return value


def front_kernel(
    normed_ref, inside_ref, across_ref, keep_ref, taps_ref, bias_ref, w_ref,
    conv_ref, gate_ref, cand_ref, total_ref, norm_buf,
    *, steps, block,
):
    batch, hidden = total_ref.shape[1:]
    tokens, width = normed_ref.shape
    span = tokens // batch
    size = steps * batch
    lead = EDGE * batch
    norm_buf[:lead, :] = pick_edge(inside_ref[...], across_ref[...], False)

    def chunk(index, carry):
        rows = rows_of(index, size)
        here = normed_ref[rows, :].astype(F32)
        norm_buf[pl.ds(pl.multiple_of(index * size + lead, 8), size), :] = here
        mixing = here * taps_ref[0:1, :]
        for tap in range(1, KW):
            start = pl.multiple_of(index * size + lead - tap * batch, 8)
            mixing = mixing + norm_buf[pl.ds(start, size), :] * taps_ref[tap : tap + 1, :]
        conv_low = mixing.astype(BF16)
        conv_ref[rows, :] = conv_low
        for part in range(hidden // block):
            cols = slice(part * block, (part + 1) * block)
            more = slice(hidden + part * block, hidden + (part + 1) * block)
            gate_ref[rows, cols] = jax.nn.sigmoid(dot(conv_low, w_ref[:, cols]) + bias_ref[:, cols])
            cand_ref[rows, cols] = dot(conv_low, w_ref[:, more])

        def step(offset, carry):
            prod, state = carry
            here = rows_of(index * steps + offset, batch)
            gate = gate_ref[here, :]
            decay = (1.0 - gate) * widen(keep_ref[here, :], hidden)
            return decay * prod, decay * state + gate * cand_ref[here, :]

        return lax.fori_loop(0, steps, step, carry, unroll=8)

    first = (jnp.ones((batch, hidden), F32), jnp.zeros((batch, hidden), F32))
    prod, state = lax.fori_loop(0, span // steps, chunk, first)
    total_ref[0] = prod
    total_ref[1] = state


def forward_kernel(
    mate_ref, *refs, chips, steps, block,
):
    chip_refs = refs[: chips - 1]
    (
        xt_ref, keep_ref, gate_ref, cand_ref, gact_ref, more_ref, gain_ref, w_out_ref, w_up_ref,
        carry_ref, held_ref, mid_ref, nmid_ref, act_ref, gup_ref,
    ) = refs[chips - 1 :]
    batch, hidden = mate_ref.shape[1:]
    inner = w_up_ref.shape[1]
    span = gate_ref.shape[0] // batch
    size = steps * batch
    chip = lax.shift_right_logical(lax.axis_index("seq"), 1)
    carry_in = jnp.zeros((batch, hidden), F32)
    for source in range(chips - 1):
        prod = from_chip(chip_refs, source, chip, 0)
        state = from_chip(chip_refs, source, chip, 1)
        carry_in = jnp.where(source < chip, prod * carry_in + state, carry_in)
    carry_in = jnp.where(bit_of("seq", 0) == 1, mate_ref[0] * carry_in + mate_ref[1], carry_in)
    carry_ref[...] = carry_in
    gain = gain_ref[...]

    def chunk(index, state):
        rows = rows_of(index, size)

        def two_steps(pair, state):
            out = []
            for side in range(2):
                here = pl.ds(pl.multiple_of((index * steps + 2 * pair + side) * batch, batch), batch)
                gate = gate_ref[here, :]
                decay = (1.0 - gate) * widen(keep_ref[here, :], hidden)
                state = decay * state + gate * cand_ref[here, :]
                out.append(state)
            both = rows_of(index * (steps // 2) + pair, 2 * batch)
            held_ref[both, :] = jnp.concatenate(out, axis=0).astype(BF16)
            return state

        state = lax.fori_loop(0, steps // 2, two_steps, state, unroll=4)
        middle = read(xt_ref, rows) + dot(held_ref[rows, :], w_out_ref[...])
        mid_ref[rows, :] = middle
        nmid = (middle * rms(middle) * gain).astype(BF16)
        nmid_ref[rows, :] = nmid
        for part in range(inner // block):
            cols = slice(part * block, (part + 1) * block)
            up = dot(nmid, w_up_ref[:, cols])
            square = up * up
            half = 0.5 + 0.5 * jnp.tanh(up * (GELU_C + (GELU_C * GELU_A) * square))
            act = up * half
            slope = half + act * (1.0 - half) * (2.0 * GELU_C + (6.0 * GELU_C * GELU_A) * square)
            act_ref[rows, cols] = act.astype(BF16)
            start = part * block
            source, start = (gact_ref, start) if start < gact_ref.shape[1] else (more_ref, start - gact_ref.shape[1])
            gact = source[rows, start : start + block].astype(F32)
            gup_ref[rows, cols] = (slope * gact).astype(BF16)
        return state

    lax.fori_loop(0, span // steps, chunk, carry_in)


def result_kernel(act_ref, mid_ref, w_down_ref, result_ref, wide_buf, *, steps):
    batch, span, width = result_ref.shape

    def chunk(index, carry):
        rows = rows_of(index, steps * batch)
        write(wide_buf, rows, mid_ref[rows, :] + dot(act_ref[rows, :], w_down_ref[...]))
        return carry

    lax.fori_loop(0, span // steps, chunk, 0)
    for row in range(batch):
        result_ref[row] = deinterleave(wide_buf, row, batch, span).astype(BF16)


def gconv_kernel(gproj_ref, w_in_ref, gconv_ref, *, steps):
    size = steps * 8

    def chunk(index, carry):
        rows = rows_of(index, size)
        gconv_ref[rows, :] = dot_nt(gproj_ref[rows, :], w_in_ref[...]).astype(BF16)
        return carry

    lax.fori_loop(0, gproj_ref.shape[0] // size, chunk, 0)


def reverse_kernel(
    gup_ref, mid_ref, gt_ref, gain_ref, keep_ref, gate_ref, w_out_ref, w_up_ref,
    gmid_ref, gbranch_ref, gheld_ref, outgoing_ref, gnorm2_ref,
    *, steps,
):
    tokens, width = mid_ref.shape
    batch, hidden = outgoing_ref.shape
    span = tokens // batch
    size = steps * batch
    gain = gain_ref[...]

    def chunk(offset, carry):
        arriving, gnorm2 = carry
        index = span // steps - 1 - offset
        rows = rows_of(index, size)
        gnmid = dot_nt(gup_ref[rows, :], w_up_ref[...])
        middle = mid_ref[rows, :]
        scale = rms(middle)
        unit = middle * scale
        gnorm2 = gnorm2 + jnp.sum(gnmid * unit, axis=0, keepdims=True)
        pulled = gnmid * gain
        gmid = gt_ref[rows, :].astype(F32) + scale * (
            pulled - unit * jnp.mean(pulled * unit, axis=-1, keepdims=True)
        )
        gmid_ref[rows, :] = gmid
        gbranch = gmid.astype(BF16)
        gbranch_ref[rows, :] = gbranch
        gheld_ref[rows, :] = dot_nt(gbranch, w_out_ref[...])

        def back(offset, arriving):
            here = rows_of(index * steps + steps - 1 - offset, batch)
            decay = (1.0 - gate_ref[here, :]) * widen(keep_ref[here, :], hidden)
            return decay * (gheld_ref[here, :] + arriving)

        return lax.fori_loop(0, steps, back, arriving, unroll=8), gnorm2

    first = (jnp.zeros((batch, hidden), F32), jnp.zeros((1, width), F32))
    outgoing, gnorm2 = lax.fori_loop(0, span // steps, chunk, first)
    outgoing_ref[...] = outgoing
    gnorm2_ref[...] = gnorm2


def back_kernel(*refs, chips):
    chip_refs, out_refs = refs[: chips - 1], refs[chips - 1 : 2 * chips - 2]
    (
        mate_ref, mate_out_ref, keep_ref, gate_ref, cand_ref, state_ref, held_ref, gheld_ref, conv_ref, w_in_ref,
        gproj_ref, gbias_ref, edge_ref, stay_ref, send_ref,
    ) = refs[2 * chips - 2 :]
    batch, hidden = mate_out_ref.shape
    span = gate_ref.shape[0] // batch
    chip = lax.shift_right_logical(lax.axis_index("seq"), 1)
    carry_in = jnp.zeros((batch, hidden), F32)
    for source in range(chips - 1, 0, -1):
        prod = from_chip(chip_refs, source, chip, 0)
        state = from_chip(out_refs, source, chip, slice(None))
        carry_in = jnp.where(source > chip, prod * carry_in + state, carry_in)
    carry_in = jnp.where(bit_of("seq", 0) == 0, mate_ref[0] * carry_in + mate_out_ref[...], carry_in)

    def two_steps(offset, carry):
        arriving, gbias = carry
        pair = span // 2 - 1 - offset
        logits = [None, None]
        cands = [None, None]
        before = held_ref[rows_of(jnp.maximum(pair - 1, 0), 2 * batch), :].astype(F32)[batch:]
        prevs = [
            jnp.where(pair == 0, state_ref[...], before),
            held_ref[rows_of(pair, 2 * batch), :].astype(F32)[:batch],
        ]
        for side in (1, 0):
            here = pl.ds(pl.multiple_of((2 * pair + side) * batch, batch), batch)
            gate = gate_ref[here, :]
            keep = widen(keep_ref[here, :], hidden)
            gstate = gheld_ref[here, :] + arriving
            rest = 1.0 - gate
            cands[side] = gstate * gate
            logits[side] = cands[side] * (cand_ref[here, :] - prevs[side] * keep) * rest
            arriving = rest * keep * gstate
            gbias = gbias + logits[side]
        both = rows_of(pair, 2 * batch)
        gproj_ref[both, :hidden] = jnp.concatenate(logits, axis=0).astype(BF16)
        gproj_ref[both, hidden:] = jnp.concatenate(cands, axis=0).astype(BF16)
        return arriving, gbias

    _, gbias = lax.fori_loop(
        0, span // 2, two_steps, (carry_in, jnp.zeros((batch, hidden), F32)), unroll=4
    )
    gbias_ref[...] = jnp.sum(gbias, axis=0, keepdims=True)
    edge_ref[...] = dot_nt(gproj_ref[: edge_ref.shape[0], :], w_in_ref[...]).astype(BF16)
    odd = bit_of("seq", 0) == 1
    wide_gradient(conv_ref, gproj_ref, stay_ref, send_ref, odd)


def deal(tile, shards, first, stay_ref, send_ref, row, odd):
    size = tile.shape[0] // shards
    for even in range(0, shards, 2):
        pair = [tile[(even + k) * size : (even + k + 1) * size].astype(BF16) for k in range(2)]
        index = (first + even) // 2
        stay_ref[index, row : row + size, :] = jnp.where(odd, pair[1], pair[0])
        send_ref[index, row : row + size, :] = jnp.where(odd, pair[0], pair[1])


def wide_gradient(left_ref, right_ref, stay_ref, send_ref, odd):
    shards = 2 * stay_ref.shape[0]
    width = stay_ref.shape[2]
    size = left_ref.shape[1] // shards
    for part in range(right_ref.shape[1] // width):
        tile = dot_tn(left_ref[...], right_ref[:, part * width : (part + 1) * width])
        deal(tile, shards, 0, stay_ref, send_ref, part * size, odd)


def tall_gradient(left_ref, right_ref, stay_ref, send_ref, odd, block=512):
    shards = 2 * stay_ref.shape[0]
    count = left_ref.shape[1] // block
    for part in range(count):
        tile = dot_tn(left_ref[:, part * block : (part + 1) * block], right_ref[...])
        deal(tile, shards // count, part * (shards // count), stay_ref, send_ref, 0, odd)


def weights_kernel(nmid_ref, gup_ref, act_ref, gt_ref, stay_up, send_up, stay_down, send_down):
    odd = bit_of("seq", 0) == 1
    wide_gradient(nmid_ref, gup_ref, stay_up, send_up, odd)
    tall_gradient(act_ref, gt_ref, stay_down, send_down, odd)


def weights_out_kernel(held_ref, gbranch_ref, stay_ref, send_ref):
    tall_gradient(held_ref, gbranch_ref, stay_ref, send_ref, bit_of("seq", 0) == 1)


def bit_of(axis, bit):
    return lax.shift_right_logical(lax.axis_index(axis), bit) & 1


def chunks(count, size, body):
    def step(index, carry):
        body(pl.ds(pl.multiple_of(index * size, size), size))
        return carry

    lax.fori_loop(0, count // size, step, 0)


def core_sum_kernel(*refs, plan):
    sources, (stay_a, send_a, stay_b, send_b) = refs[:-4], refs[-4:]
    base = 0
    for stay_ref, come_ref in zip(sources[::2], sources[1::2]):
        half = stay_ref.shape[1] // 2
        for out_stay, out_send, first, axis in ((stay_a, send_a, 0, plan[0]), (stay_b, send_b, half, plan[1])):
            low = 1 << axis
            for group in range(out_stay.shape[0]):
                fixed = (group >> axis) * 2 * low + (group & (low - 1))
                mine = fixed + low * bit_of("seq", axis + 1)
                other = fixed + low * (1 - bit_of("seq", axis + 1))

                def body(rows):
                    source = pl.ds(pl.multiple_of(rows.start + first, 16), rows.size)
                    goal = pl.ds(pl.multiple_of(rows.start + base, 16), rows.size)
                    out_stay[group, goal, :] = stay_ref[mine, source, :].astype(F32) + come_ref[
                        mine, source, :
                    ].astype(F32)
                    out_send[group, goal, :] = (
                        stay_ref[other, source, :].astype(F32) + come_ref[other, source, :].astype(F32)
                    ).astype(BF16)

                chunks(half, 16, body)
        base += half


def split_sum_kernel(*refs, plan, counts):
    ins = 2 * sum(counts)
    outs = refs[ins:]
    source = 0
    for part, (which, axis) in enumerate(plan):
        out_stay, out_send = outs[2 * part], outs[2 * part + 1]
        low = 1 << axis
        base = 0
        for pair in range(counts[part]):
            stay_ref, come_ref = refs[source], refs[source + 1]
            source += 2
            for group in range(out_stay.shape[0]):
                fixed = (group >> axis) * 2 * low + (group & (low - 1))
                mine = fixed + low * bit_of("seq", which + 1)
                other = fixed + low * (1 - bit_of("seq", which + 1))

                def body(rows):
                    goal = pl.ds(pl.multiple_of(rows.start + base, 16), rows.size)
                    out_stay[group, goal, :] = stay_ref[mine, rows, :].astype(F32) + come_ref[
                        mine, rows, :
                    ].astype(F32)
                    out_send[group, goal, :] = (
                        stay_ref[other, rows, :].astype(F32) + come_ref[other, rows, :].astype(F32)
                    ).astype(BF16)

                chunks(stay_ref.shape[1], 16, body)
            base += stay_ref.shape[1]


def join_sum_kernel(stay_a, come_a, stay_b, come_b, out_stay, out_send):
    width = out_stay.shape[1]
    here = pl.ds(pl.multiple_of(bit_of("dp", 0) * width, width), width)
    there = pl.ds(pl.multiple_of((1 - bit_of("dp", 0)) * width, width), width)
    for stay_ref, come_ref, base in ((stay_a, come_a, 0), (stay_b, come_b, stay_a.shape[1])):

        def body(rows):
            goal = pl.ds(pl.multiple_of(rows.start + base, 16), rows.size)
            out_stay[goal, :] = stay_ref[0, rows, here] + come_ref[0, rows, here].astype(F32)
            out_send[goal, :] = (
                stay_ref[0, rows, there] + come_ref[0, rows, there].astype(F32)
            ).astype(BF16)

        chunks(stay_ref.shape[1], 16, body)


def column_sum_kernel(stay_ref, come_ref, out_stay, out_send, *, bit):
    width = out_stay.shape[1]
    here = pl.ds(pl.multiple_of(bit_of("dp", bit) * width, width), width)
    there = pl.ds(pl.multiple_of((1 - bit_of("dp", bit)) * width, width), width)

    def body(rows):
        out_stay[rows, :] = stay_ref[rows, here] + come_ref[rows, here].astype(F32)
        out_send[rows, :] = (stay_ref[rows, there] + come_ref[rows, there].astype(F32)).astype(BF16)

    chunks(out_stay.shape[0], 16, body)


def round_sum_kernel(stay_ref, come_ref, out_ref):
    def body(rows):
        out_ref[rows, :] = (stay_ref[rows, :].astype(F32) + come_ref[rows, :].astype(F32)).astype(BF16)

    chunks(out_ref.shape[0], 16, body)


def taps_kernel(
    gconv_ref, after_ref, ahead_ref, xt_ref, normed_ref, halo_ref, across_ref, taps_ref, gnorm2_ref, gbias_ref,
    gnormed_ref, stay_ref, send_ref, norm_buf, gconv_buf,
    *, steps,
):
    tokens, width = gconv_ref.shape
    batch = halo_ref.shape[0] // EDGE
    size = steps * batch
    lead = EDGE * batch
    norm_buf[:lead, :] = pick_edge(halo_ref[...], across_ref[...], False)
    gconv_buf[tokens : tokens + after_ref.shape[0], :] = pick_edge(after_ref[...], ahead_ref[...], True)

    def spread(index, carry):
        rows = rows_of(index, size)
        norm_buf[pl.ds(pl.multiple_of(index * size + lead, 8), size), :] = normed_ref[rows, :].astype(F32)
        gconv_buf[rows, :] = gconv_ref[rows, :].astype(F32)
        return carry

    lax.fori_loop(0, tokens // size, spread, 0)

    def chunk(index, carry):
        gnorm1, gtaps = carry
        rows = rows_of(index, size)
        here = gconv_buf[rows, :]
        gnormed = here * taps_ref[0:1, :]
        sums = []
        for tap in range(KW):
            if tap:
                later = pl.ds(pl.multiple_of(index * size + tap * batch, 8), size)
                gnormed = gnormed + gconv_buf[later, :] * taps_ref[tap : tap + 1, :]
            earlier = pl.ds(pl.multiple_of(index * size + lead - tap * batch, 8), size)
            sums.append(gtaps[tap] + jnp.sum(norm_buf[earlier, :] * here, axis=0, keepdims=True))
        gnormed_ref[rows, :] = gnormed
        values = read(xt_ref, rows)
        gnorm1 = gnorm1 + jnp.sum(gnormed * (values * rms(values)), axis=0, keepdims=True)
        return gnorm1, tuple(sums)

    zero = jnp.zeros((1, width), F32)
    gnorm1, gtaps = lax.fori_loop(0, tokens // size, chunk, (zero, (zero,) * KW))
    places = 2 * stay_ref.shape[0]
    odd = bit_of("seq", 0) == 1
    rows = []
    for place in range(places):
        parts = [
            vector[:, place * (vector.shape[1] // places) : (place + 1) * (vector.shape[1] // places)]
            for vector in (gnorm1, gnorm2_ref[...], *gtaps, gbias_ref[...])
        ]
        row = jnp.concatenate(parts, axis=1)
        if row.shape[1] < width:
            row = jnp.concatenate([row, jnp.zeros((1, width - row.shape[1]), F32)], axis=1)
        rows.append(jnp.broadcast_to(row, (stay_ref.shape[1], width)))
    for index in range(places // 2):
        pair = rows[2 * index : 2 * index + 2]
        stay_ref[index] = jnp.where(odd, pair[1], pair[0]).astype(BF16)
        send_ref[index] = jnp.where(odd, pair[0], pair[1]).astype(BF16)


def inputs_kernel(gnormed_ref, xt_ref, gmid_ref, gain_ref, ginput_ref, wide_buf, *, steps):
    batch, span, width = ginput_ref.shape
    gain = gain_ref[...]

    def chunk(index, carry):
        rows = rows_of(index, steps * batch)
        values = read(xt_ref, rows)
        scale = rms(values)
        unit = values * scale
        pulled = gnormed_ref[rows, :] * gain
        ginput = gmid_ref[rows, :] + scale * (
            pulled - unit * jnp.mean(pulled * unit, axis=-1, keepdims=True)
        )
        write(wide_buf, rows, ginput)
        return carry

    lax.fori_loop(0, span // steps, chunk, 0)
    for row in range(batch):
        ginput_ref[row] = deinterleave(wide_buf, row, batch, span)


def finish_kernel(total_ref, come_ref, *outs, sizes):
    wide = total_ref.shape[1]
    width = 2 * wide
    half = sum(sizes) // 2
    if len(outs) > len(sizes):
        low = bit_of("dp", 0) == 0
        mine, other = [ref[half : half + SMALL, :].astype(F32) for ref in (total_ref, come_ref)]
        row = jnp.concatenate([jnp.where(low, mine, other), jnp.where(low, other, mine)], axis=1)
        column = 0
        for out in outs[len(sizes) :]:
            for line in range(out.shape[0]):
                out[line : line + 1, :] = row[0:1, column : column + out.shape[1]]
                column += out.shape[1]
    for source, bit in ((total_ref, bit_of("dp", 0)), (come_ref, 1 - bit_of("dp", 0))):
        for part_b in range(2):
            row = part_b * (total_ref.shape[0] - half)
            for out, rows in zip(outs, sizes):
                size = out.shape[0]
                count = min(size, rows // 2)
                for start in range(part_b * rows // 2, (part_b + 1) * rows // 2, count):
                    part, low_row = start // size, start % size
                    cols = pl.ds(pl.multiple_of(part * width + bit * wide, wide), wide)
                    out[low_row : low_row + count, cols] = source[row : row + count, :].astype(F32)
                    row += count


def call(
    kernel, name, out_shapes, in_specs, args, scratch=(), limit=2, after=(), work=1
):
    ins, outs = len(args), len(out_shapes)

    def body(*refs):
        inner = list(refs[:ins])
        rest = refs[ins:]
        rest = rest[len(after) :]
        inner += rest[:outs]
        rest = rest[outs:]
        if name in FINAL:
            rest[0][...] = jnp.zeros((8, LANES), F32)
            rest = rest[1:]
        kernel(*inner, *rest)

    args, in_specs, out_shapes = list(args), list(in_specs), list(out_shapes)
    if name in FINAL:
        out_shapes.append(((8, LANES), F32))
    args += after
    in_specs += [pl.BlockSpec(memory_space=pl.ANY)] * len(after)
    return pl.pallas_call(
        body,
        name=name,
        out_shape=[
            (pltpu.HBM if name in FINAL and index < outs else jax.ShapeDtypeStruct)(shape, kind)
            for index, (shape, kind) in enumerate(out_shapes)
        ],
        in_specs=in_specs,
        out_specs=[VMEM_SPEC] * len(out_shapes),
        scratch_shapes=list(scratch),
        compiler_params=pltpu.CompilerParams(vmem_limit_bytes=limit * 2**20),
        cost_estimate=pl.CostEstimate(flops=work, bytes_accessed=1, transcendentals=0),
    )(*args)


def neighbour(block, axis):
    count = lax.axis_size(axis)
    inside = swap_by(block, axis, 1)
    across = lax.ppermute(block, axis, [(i, (i + 1 if i % 2 else i - 1) % count) for i in range(count)])
    return inside, across


def pick_edge(inside, across, ahead):
    place = lax.axis_index("seq")
    end = lax.axis_size("seq") - 1 if ahead else 0
    odd = bit_of("seq", 0) == 1
    value = jnp.where(odd != ahead, inside.astype(F32), across.astype(F32))
    return jnp.where(place == end, jnp.zeros_like(value), value)


def swap_by(block, axis, mask):
    return lax.ppermute(block, axis, [(i, i ^ mask) for i in range(lax.axis_size(axis))])


def swap(block, axis, bit):
    return swap_by(block, axis, 1 << bit)


class Order:
    def __init__(self):
        self.last = ()

    def call(self, *args, **kwargs):
        kwargs.setdefault("work", WORK.get(args[1], 1))
        outs = list(call(*args, **kwargs, after=self.last))
        self.last = (min(outs, key=lambda out: out.size * out.dtype.itemsize),)
        if args[1] in FINAL:
            outs.pop()
        return outs


def spread_sum(order, name, sources, out_shapes, late=()):
    places, _, width = sources[0][0].shape
    sizes = tuple(stay.shape[1] for stay, _ in sources)
    rows = sum(sizes)
    levels = places.bit_length() - 1
    order_a = list(range(levels))
    order_b = order_a[::-1]
    half = rows // 2

    def shapes(count, more=0):
        out = []
        for part in (half + more, half):
            out += [((count, part, width), F32), ((count, part, width), BF16)]
        return out

    stay_a, send_a, stay_b, send_b = order.call(
        functools.partial(core_sum_kernel, plan=(order_a[0], order_b[0])), name + "_core",
        shapes(places // 2), [VMEM_SPEC] * (2 * len(sources)), [part for pair in sources for part in pair],
        limit=1,
    )
    for level in range(levels):
        come_a = swap(send_a, "seq", order_a[level] + 1)
        come_b = swap(send_b, "seq", order_b[level] + 1)
        yield None
        if level + 1 == levels:
            break
        plan = []
        for bits in (order_a, order_b):
            bit = bits[level + 1]
            plan.append((bit, bit - sum(done < bit for done in bits[: level + 1])))
        sources = [stay_a, come_a, *(late if level == 0 else ()), stay_b, come_b]
        more = SMALL if late else 0
        stay_a, send_a, stay_b, send_b = order.call(
            functools.partial(
                split_sum_kernel, plan=tuple(plan), counts=(2 if late and level == 0 else 1, 1)
            ),
            name + "_seq", shapes(places // 4 >> level, more), [VMEM_SPEC] * len(sources), sources,
        )
    rows += SMALL if late else 0
    depth = lax.axis_size("dp").bit_length() - 1
    wide = width // 2
    stay, send = order.call(
        join_sum_kernel, name + "_join", [((rows, wide), F32), ((rows, wide), BF16)],
        [VMEM_SPEC] * 4, (stay_a, come_a, stay_b, come_b),
    )
    for bit in range(1, depth - 1):
        wide = wide // 2
        come = swap(send, "dp", bit - 1)
        yield None
        stay, send = order.call(
            functools.partial(column_sum_kernel, bit=bit), name + "_dp",
            [((rows, wide), F32), ((rows, wide), BF16)], [VMEM_SPEC] * 2,
            (stay, come),
        )
    come = swap(send, "dp", depth - 2)
    yield None
    (low,) = order.call(
        round_sum_kernel, name + "_last", [((rows, wide), BF16)], [VMEM_SPEC] * 2, (stay, come)
    )
    come = swap(low, "dp", depth - 1)
    yield None
    (total,) = order.call(
        round_sum_kernel, name + "_total", [((rows, wide), BF16)], [VMEM_SPEC] * 2, (low, come)
    )
    for bit in range(depth - 2, 0, -1):
        come = swap(total, "dp", bit)
        upper = bit_of("dp", bit) == 1
        total = jnp.concatenate(
            [jnp.where(upper, come, total), jnp.where(upper, total, come)], axis=1
        )
    come = swap(total, "dp", 0)
    yield None
    yield order.call(
        functools.partial(finish_kernel, sizes=sizes), name + "_finish", [(shape, F32) for shape in out_shapes],
        [VMEM_SPEC] * 2, (total, come),
    )


def on_device(
    inputs, doc_start, norm1_gain, conv_weight, gate_bias, w_in, w_out, norm2_gain, w_up, w_down, out_grad
):
    batch, span, width = inputs.shape
    hidden = w_out.shape[0]
    inner = w_up.shape[1]
    tokens = batch * span
    lanes = width // LANES
    seq_count, dp_count = lax.axis_size("seq"), lax.axis_size("dp")
    seq_depth, dp_depth = seq_count.bit_length() - 1, dp_count.bit_length() - 1
    pairs = seq_count // 2
    seq_at = lax.axis_index("seq").astype(jnp.int32)
    taps = jnp.transpose(conv_weight)
    gain1, gain2, bias = norm1_gain[None], norm2_gain[None], gate_bias[None]
    order = Order()

    xt, normed, edge, keep = order.call(
        functools.partial(ingest_kernel, steps=span), "ingest",
        [
            ((lanes, tokens, LANES), F32), ((tokens, width), BF16), ((EDGE * batch, width), BF16),
            ((tokens, LANES), F32),
        ],
        [pl.BlockSpec(memory_space=pltpu.HBM)] * 3,
        [pltpu.with_memory_space_constraint(part, pltpu.HBM) for part in (inputs, doc_start, gain1)],
        [
            pltpu.VMEM((batch, span, width), BF16), pltpu.VMEM((batch, span), jnp.int32),
            pltpu.VMEM((1, width), F32), pltpu.SemaphoreType.DMA((batch + 2,)),
        ],
        limit=LIMITS["ingest"],
    )
    halo = neighbour(edge, "seq")
    gt, gact = order.call(
        functools.partial(prepare_kernel, steps=span, block=256), "prepare",
        [((tokens, width), BF16), ((tokens, inner // 2), BF16)],
        [VMEM_SPEC] * 2, (out_grad, w_down), [pltpu.VMEM((lanes, tokens, LANES), F32)],
        limit=LIMITS["prepare"],
    )
    conv_out, gate, cand, totals = order.call(
        functools.partial(front_kernel, steps=span, block=256), "front",
        [
            ((tokens, width), BF16), ((tokens, hidden), F32), ((tokens, hidden), F32),
            ((2, batch, hidden), F32),
        ],
        [VMEM_SPEC] * 7, (normed, *halo, keep, taps, bias, w_in),
        [pltpu.VMEM((tokens + EDGE * batch, width), F32)],
        limit=LIMITS["front"],
    )
    chips = seq_count // 2
    mate_totals = swap(totals, "seq", 0)
    (chip_totals,) = order.call(
        chip_totals_kernel, "chip_totals", [(totals.shape, F32)], [VMEM_SPEC] * 2, (totals, mate_totals)
    )
    all_totals = [swap_by(chip_totals, "seq", 2 * mask) for mask in range(1, chips)]
    (more,) = order.call(
        functools.partial(prepare_rest_kernel, size=tokens, block=256), "prepare_rest",
        [((tokens, inner // 2), BF16)], [VMEM_SPEC] * 2, (gt, w_down), limit=LIMITS["prepare_rest"],
    )
    state_in, held, mid, nmid, act, gup = order.call(
        functools.partial(forward_kernel, chips=chips, steps=span, block=256), "forward",
        [
            ((batch, hidden), F32), ((tokens, hidden), BF16), ((tokens, width), F32),
            ((tokens, width), BF16), ((tokens, inner), BF16), ((tokens, inner), BF16),
        ],
        [VMEM_SPEC] * (9 + chips),
        (mate_totals, *all_totals, xt, keep, gate, cand, gact, more, gain2, w_out, w_up),
        limit=LIMITS["forward"],
    )
    up_rows = inner // seq_count
    stay_up, send_up, stay_down, send_down = order.call(
        weights_kernel, "weights", [((pairs, up_rows, width), BF16)] * 4,
        [VMEM_SPEC] * 4, (nmid, gup, act, gt), limit=LIMITS["weights"],
    )
    come_up, come_down = swap(send_up, "seq", 0), swap(send_down, "seq", 0)
    gmid, gbranch, gheld, outgoing, gnorm2 = order.call(
        functools.partial(reverse_kernel, steps=span), "reverse",
        [
            ((tokens, width), F32), ((tokens, width), BF16), ((tokens, hidden), F32),
            ((batch, hidden), F32), ((1, width), F32),
        ],
        [VMEM_SPEC] * 8, (gup, mid, gt, gain2, keep, gate, w_out, w_up),
        limit=LIMITS["reverse"],
    )
    mate_outgoing = swap(outgoing, "seq", 0)
    out_rows = hidden // seq_count
    in_rows = 2 * hidden // seq_count
    stay_out, send_out = order.call(
        weights_out_kernel, "weights_out", [((pairs, out_rows, width), BF16)] * 2,
        [VMEM_SPEC] * 2, (held, gbranch), limit=LIMITS["weights"],
    )
    come_out = swap(send_out, "seq", 0)
    (chip_outgoing,) = order.call(
        chip_outgoing_kernel, "chip_outgoing", [(outgoing.shape, F32)], [VMEM_SPEC] * 4,
        (outgoing, mate_outgoing, totals, mate_totals),
    )
    all_outgoing = [swap_by(chip_outgoing, "seq", 2 * mask) for mask in range(1, chips)]
    first = spread_sum(
        order, "first", [(stay_up, come_up), (stay_down, come_down)],
        [(width // seq_count, inner), (up_rows, width)],
    )
    next(first)
    gproj, gbias, gconv_edge, stay_in, send_in = order.call(
        functools.partial(back_kernel, chips=chips), "back",
        [((tokens, 2 * hidden), BF16), ((1, hidden), F32), ((EDGE * batch, width), BF16)]
        + [((pairs, in_rows, width), BF16)] * 2,
        [VMEM_SPEC] * (8 + 2 * chips),
        (
            *all_totals, *all_outgoing, mate_totals, mate_outgoing, keep, gate, cand, state_in, held, gheld, conv_out, w_in,
        ),
        limit=LIMITS["back"],
    )
    after = neighbour(gconv_edge, "seq")
    come_in = swap(send_in, "seq", 0)
    (gconv,) = order.call(
        functools.partial(gconv_kernel, steps=span), "gconv", [((tokens, width), BF16)],
        [VMEM_SPEC] * 2, (gproj, w_in), limit=LIMITS["gconv"],
    )
    order.last = (*order.last, after[0])
    late = []
    share = width // seq_count
    second = spread_sum(
        order, "second", [(stay_in, come_in), (stay_out, come_out)],
        [
            (share, 2 * hidden), (out_rows, width), (1, share), (1, share), (KW, share),
            (1, hidden // seq_count),
        ],
        late,
    )
    next(first)
    gnormed, stay_small, send_small = order.call(
        functools.partial(taps_kernel, steps=16), "taps",
        [((tokens, width), F32)] + [((pairs, SMALL, width), BF16)] * 2, [VMEM_SPEC] * 10,
        (gconv, *after, xt, normed, *halo, taps, gnorm2, gbias),
        [
            pltpu.VMEM((tokens + EDGE * batch, width), F32),
            pltpu.VMEM((tokens + EDGE * batch, width), F32),
        ],
        limit=LIMITS["taps"],
    )
    come_small = swap(send_small, "seq", 0)
    next(second)
    next(first)
    stay_small, send_small = order.call(
        functools.partial(split_sum_kernel, plan=((0, 0),), counts=(1,)), "small",
        [((pairs // 2, SMALL, width), F32), ((pairs // 2, SMALL, width), BF16)], [VMEM_SPEC] * 2,
        (stay_small, come_small),
    )
    late += [stay_small, swap(send_small, "seq", 1)]
    (result,) = order.call(
        functools.partial(result_kernel, steps=span), "result", [((batch, span, width), BF16)],
        [VMEM_SPEC] * 3, (act, mid, w_down), [pltpu.VMEM((lanes, tokens, LANES), F32)],
        limit=LIMITS["result"],
    )
    next(second)
    next(first)
    next(second)
    (ginput,) = order.call(
        functools.partial(inputs_kernel, steps=64), "inputs", [((batch, span, width), F32)],
        [VMEM_SPEC] * 4, (gnormed, xt, gmid, gain1), [pltpu.VMEM((lanes, tokens, LANES), F32)],
        limit=LIMITS["inputs"],
    )
    next(first)
    next(second)
    done = {}
    while len(done) < 2:
        for part in (second, first):
            if part not in done:
                outs = next(part)
                if outs is not None:
                    done[part] = outs
    gw_up, gw_down = done[first]
    gw_in, gw_out, gnorm1, gnorm2, gtaps, gbias = done[second]
    return (
        result, ginput, gnorm1[0], jnp.transpose(gtaps), gbias[0], gw_in, gw_out, gnorm2[0], gw_up, gw_down,
    )


def solution(mesh):
    rows, flat = P("dp", "seq", None), P()
    in_specs = (rows, P("dp", "seq")) + (flat,) * 8 + (rows,)
    vec, mat = P("seq"), P("seq", None)
    out_specs = (rows, rows, vec, mat, vec, mat, mat, vec, mat, mat)
    return jax.shard_map(
        on_device, mesh=mesh, in_specs=in_specs, out_specs=out_specs, check_vma=False
    )
```

```python
import functools

import jax
import jax.numpy as jnp
from jax import lax
from jax.experimental import pallas as pl
from jax.experimental.pallas import tpu as pltpu
from jax.sharding import PartitionSpec as P

KW = 4
EPS = 1e-05
EDGE = 8
SMALL = 16
LANES = 128
FINAL = ("result", "inputs", "first_finish", "second_finish")
WORK = {"second_core": 10**9, "second_join": 5 * 10**9, "result": 2000000000} | dict.fromkeys(("ingest", "prepare", "front", "forward", "first_seq", "back", "chip_outgoing"), 10**10)
LIMITS = {"ingest": 4, "prepare": 6, "prepare_rest": 3, "front": 7, "forward": 6, "weights": 3, "reverse": 5, "back": 3, "gconv": 3, "taps": 5, "inputs": 7, "result": 7}
F32 = jnp.float32
BF16 = jnp.bfloat16
GELU_C = 0.7978845608028654
GELU_A = 0.044715

VMEM_SPEC = pl.BlockSpec(memory_space=pltpu.VMEM)


def dot(left, right):
    return jnp.dot(left, right, preferred_element_type=F32)


def dot_nt(left, right):
    return lax.dot_general(left, right, (((1,), (1,)), ((), ())), preferred_element_type=F32)


def dot_tn(left, right):
    return lax.dot_general(left, right, (((0,), (0,)), ((), ())), preferred_element_type=F32)


def widen(column, lanes):
    return jnp.concatenate([column] * (lanes // column.shape[1]), axis=1)


def rms(values):
    return lax.rsqrt(jnp.mean(values * values, axis=-1, keepdims=True) + EPS)


def rows_of(index, count):
    return pl.ds(pl.multiple_of(index * count, count), count)


def interleave(buf, row, batch, values):
    for lane in range(buf.shape[0]):
        cols = slice(lane * LANES, (lane + 1) * LANES)
        buf[lane, pl.ds(row, values.shape[0], stride=batch), :] = values[:, cols].astype(F32)


def deinterleave(buf, row, batch, span):
    parts = [buf[lane, pl.ds(row, span, stride=batch), :] for lane in range(buf.shape[0])]
    return jnp.concatenate(parts, axis=1)


def read(buf, rows):
    return jnp.concatenate([buf[lane, rows, :] for lane in range(buf.shape[0])], axis=1)


def write(buf, rows, values):
    for lane in range(buf.shape[0]):
        buf[lane, rows, :] = values[:, lane * LANES : (lane + 1) * LANES]


def ingest_kernel(x_ref, start_ref, gain_ref, xt_ref, normed_ref, edge_ref, keep_ref, x_buf, start_buf, gain_buf, sems, *, steps):
    batch, span, width = x_ref.shape
    size = steps * batch
    copies = [pltpu.make_async_copy(x_ref.at[row], x_buf.at[row], sems.at[row]) for row in range(batch)]
    start_copy = pltpu.make_async_copy(start_ref, start_buf, sems.at[batch])
    gain_copy = pltpu.make_async_copy(gain_ref, gain_buf, sems.at[batch + 1])
    for copy in (start_copy, *copies, gain_copy):
        copy.start()
    start_copy.wait()
    keep = 1.0 - start_buf[...].astype(F32)
    for token in range(span):
        keep_ref[token * batch : (token + 1) * batch, :] = jnp.broadcast_to(
            keep[:, token : token + 1], (batch, LANES)
        )
    for row, copy in enumerate(copies):
        copy.wait()
        interleave(xt_ref, row, batch, x_buf[row])
    gain_copy.wait()

    def chunk(index, carry):
        rows = rows_of(index, size)
        values = read(xt_ref, rows)
        normed_ref[rows, :] = (values * rms(values) * gain_buf[...]).astype(BF16)
        return carry

    lax.fori_loop(0, span // steps, chunk, 0)
    edge_ref[...] = normed_ref[(span - EDGE) * batch :, :]


def prepare_kernel(g_ref, w_down_ref, gt_ref, gact_ref, wide_buf, *, steps, block):
    batch, span, width = g_ref.shape
    size = steps * batch
    for row in range(batch):
        interleave(wide_buf, row, batch, g_ref[row])

    def chunk(index, carry):
        rows = rows_of(index, size)
        g_low = read(wide_buf, rows).astype(BF16)
        gt_ref[rows, :] = g_low
        for part in range(gact_ref.shape[1] // block):
            cols = slice(part * block, (part + 1) * block)
            gact_ref[rows, cols] = dot_nt(g_low, w_down_ref[cols, :]).astype(BF16)
        return carry

    lax.fori_loop(0, span // steps, chunk, 0)


def prepare_rest_kernel(gt_ref, w_down_ref, gact_ref, *, size, block):
    first = w_down_ref.shape[0] - gact_ref.shape[1]

    def chunk(index, carry):
        rows = rows_of(index, size)
        for part in range(gact_ref.shape[1] // block):
            cols = slice(part * block, (part + 1) * block)
            weights = w_down_ref[first + part * block : first + (part + 1) * block, :]
            gact_ref[rows, cols] = dot_nt(gt_ref[rows, :], weights).astype(BF16)
        return carry

    lax.fori_loop(0, gt_ref.shape[0] // size, chunk, 0)


def chip_totals_kernel(mine_ref, mate_ref, chip_ref):
    odd = bit_of("seq", 0) == 1
    prod, state = mine_ref[0], mine_ref[1]
    mate_prod, mate_state = mate_ref[0], mate_ref[1]
    chip_ref[0] = prod * mate_prod
    chip_ref[1] = jnp.where(odd, prod * mate_state + state, mate_prod * state + mate_state)


def chip_outgoing_kernel(mine_ref, mate_ref, totals_ref, mate_totals_ref, chip_ref):
    odd = bit_of("seq", 0) == 1
    mine, mate = mine_ref[...], mate_ref[...]
    chip_ref[...] = jnp.where(odd, mate_totals_ref[0] * mine + mate, totals_ref[0] * mate + mine)


def from_chip(refs, source, chip, part):
    value = refs[0][part]
    for mask in range(2, len(refs) + 1):
        value = jnp.where((source ^ chip) == mask, refs[mask - 1][part], value)
    return value


def front_kernel(
    normed_ref, inside_ref, across_ref, keep_ref, taps_ref, bias_ref, w_ref,
    conv_ref, gate_ref, cand_ref, total_ref, norm_buf,
    *, steps, block,
):
    batch, hidden = total_ref.shape[1:]
    tokens, width = normed_ref.shape
    span = tokens // batch
    size = steps * batch
    lead = EDGE * batch
    norm_buf[:lead, :] = pick_edge(inside_ref[...], across_ref[...], False)

    def chunk(index, carry):
        rows = rows_of(index, size)
        here = normed_ref[rows, :].astype(F32)
        norm_buf[pl.ds(pl.multiple_of(index * size + lead, 8), size), :] = here
        mixing = here * taps_ref[0:1, :]
        for tap in range(1, KW):
            start = pl.multiple_of(index * size + lead - tap * batch, 8)
            mixing = mixing + norm_buf[pl.ds(start, size), :] * taps_ref[tap : tap + 1, :]
        conv_low = mixing.astype(BF16)
        conv_ref[rows, :] = conv_low
        for part in range(hidden // block):
            cols = slice(part * block, (part + 1) * block)
            more = slice(hidden + part * block, hidden + (part + 1) * block)
            gate_ref[rows, cols] = jax.nn.sigmoid(dot(conv_low, w_ref[:, cols]) + bias_ref[:, cols])
            cand_ref[rows, cols] = dot(conv_low, w_ref[:, more])

        def step(offset, carry):
            prod, state = carry
            here = rows_of(index * steps + offset, batch)
            gate = gate_ref[here, :]
            decay = (1.0 - gate) * widen(keep_ref[here, :], hidden)
            return decay * prod, decay * state + gate * cand_ref[here, :]

        return lax.fori_loop(0, steps, step, carry, unroll=16)

    first = (jnp.ones((batch, hidden), F32), jnp.zeros((batch, hidden), F32))
    prod, state = lax.fori_loop(0, span // steps, chunk, first)
    total_ref[0] = prod
    total_ref[1] = state


def forward_kernel(
    mate_ref, *refs, chips, steps, block,
):
    chip_refs = refs[: chips - 1]
    (
        xt_ref, keep_ref, gate_ref, cand_ref, gact_ref, more_ref, gain_ref, w_out_ref, w_up_ref,
        carry_ref, held_ref, mid_ref, nmid_ref, act_ref, gup_ref,
    ) = refs[chips - 1 :]
    batch, hidden = mate_ref.shape[1:]
    inner = w_up_ref.shape[1]
    span = gate_ref.shape[0] // batch
    size = steps * batch
    chip = lax.shift_right_logical(lax.axis_index("seq"), 1)
    carry_in = jnp.zeros((batch, hidden), F32)
    for source in range(chips - 1):
        prod = from_chip(chip_refs, source, chip, 0)
        state = from_chip(chip_refs, source, chip, 1)
        carry_in = jnp.where(source < chip, prod * carry_in + state, carry_in)
    carry_in = jnp.where(bit_of("seq", 0) == 1, mate_ref[0] * carry_in + mate_ref[1], carry_in)
    carry_ref[...] = carry_in
    gain = gain_ref[...]

    def chunk(index, state):
        rows = rows_of(index, size)

        def two_steps(pair, state):
            out = []
            for side in range(2):
                here = pl.ds(pl.multiple_of((index * steps + 2 * pair + side) * batch, batch), batch)
                gate = gate_ref[here, :]
                decay = (1.0 - gate) * widen(keep_ref[here, :], hidden)
                state = decay * state + gate * cand_ref[here, :]
                out.append(state)
            both = rows_of(index * (steps // 2) + pair, 2 * batch)
            held_ref[both, :] = jnp.concatenate(out, axis=0).astype(BF16)
            return state

        state = lax.fori_loop(0, steps // 2, two_steps, state, unroll=8)
        middle = read(xt_ref, rows) + dot(held_ref[rows, :], w_out_ref[...])
        mid_ref[rows, :] = middle
        nmid = (middle * rms(middle) * gain).astype(BF16)
        nmid_ref[rows, :] = nmid
        for part in range(inner // block):
            cols = slice(part * block, (part + 1) * block)
            up = dot(nmid, w_up_ref[:, cols])
            square = up * up
            half = jax.nn.sigmoid(up * (2.0 * GELU_C + (2.0 * GELU_C * GELU_A) * square))
            act = up * half
            slope = half + act * (1.0 - half) * (2.0 * GELU_C + (6.0 * GELU_C * GELU_A) * square)
            act_ref[rows, cols] = act.astype(BF16)
            start = part * block
            source, start = (gact_ref, start) if start < gact_ref.shape[1] else (more_ref, start - gact_ref.shape[1])
            gact = source[rows, start : start + block].astype(F32)
            gup_ref[rows, cols] = (slope * gact).astype(BF16)
        return state

    lax.fori_loop(0, span // steps, chunk, carry_in)


def result_kernel(act_ref, mid_ref, w_down_ref, result_ref, wide_buf, *, steps):
    batch, span, width = result_ref.shape

    def chunk(index, carry):
        rows = rows_of(index, steps * batch)
        write(wide_buf, rows, mid_ref[rows, :] + dot(act_ref[rows, :], w_down_ref[...]))
        return carry

    lax.fori_loop(0, span // steps, chunk, 0)
    for row in range(batch):
        result_ref[row] = deinterleave(wide_buf, row, batch, span).astype(BF16)


def gconv_kernel(gproj_ref, w_in_ref, gconv_ref, *, steps):
    size = steps * 8

    def chunk(index, carry):
        rows = rows_of(index, size)
        gconv_ref[rows, :] = dot_nt(gproj_ref[rows, :], w_in_ref[...]).astype(BF16)
        return carry

    lax.fori_loop(0, gproj_ref.shape[0] // size, chunk, 0)


def reverse_kernel(
    gup_ref, mid_ref, gt_ref, gain_ref, keep_ref, gate_ref, w_out_ref, w_up_ref,
    gmid_ref, gbranch_ref, gheld_ref, outgoing_ref, gnorm2_ref,
    *, steps,
):
    tokens, width = mid_ref.shape
    batch, hidden = outgoing_ref.shape
    span = tokens // batch
    size = steps * batch
    gain = gain_ref[...]

    def chunk(offset, carry):
        arriving, gnorm2 = carry
        index = span // steps - 1 - offset
        rows = rows_of(index, size)
        gnmid = dot_nt(gup_ref[rows, :], w_up_ref[...])
        middle = mid_ref[rows, :]
        scale = rms(middle)
        unit = middle * scale
        gnorm2 = gnorm2 + jnp.sum(gnmid * unit, axis=0, keepdims=True)
        pulled = gnmid * gain
        gmid = gt_ref[rows, :].astype(F32) + scale * (
            pulled - unit * jnp.mean(pulled * unit, axis=-1, keepdims=True)
        )
        gmid_ref[rows, :] = gmid
        gbranch = gmid.astype(BF16)
        gbranch_ref[rows, :] = gbranch
        gheld_ref[rows, :] = dot_nt(gbranch, w_out_ref[...])

        def back(offset, arriving):
            here = rows_of(index * steps + steps - 1 - offset, batch)
            decay = (1.0 - gate_ref[here, :]) * widen(keep_ref[here, :], hidden)
            return decay * (gheld_ref[here, :] + arriving)

        return lax.fori_loop(0, steps, back, arriving, unroll=16), gnorm2

    first = (jnp.zeros((batch, hidden), F32), jnp.zeros((1, width), F32))
    outgoing, gnorm2 = lax.fori_loop(0, span // steps, chunk, first)
    outgoing_ref[...] = outgoing
    gnorm2_ref[...] = gnorm2


def back_kernel(*refs, chips):
    chip_refs, out_refs = refs[: chips - 1], refs[chips - 1 : 2 * chips - 2]
    (
        mate_ref, mate_out_ref, keep_ref, gate_ref, cand_ref, state_ref, held_ref, gheld_ref, conv_ref, w_in_ref,
        gproj_ref, gbias_ref, edge_ref, stay_ref, send_ref,
    ) = refs[2 * chips - 2 :]
    batch, hidden = mate_out_ref.shape
    span = gate_ref.shape[0] // batch
    chip = lax.shift_right_logical(lax.axis_index("seq"), 1)
    carry_in = jnp.zeros((batch, hidden), F32)
    for source in range(chips - 1, 0, -1):
        prod = from_chip(chip_refs, source, chip, 0)
        state = from_chip(out_refs, source, chip, slice(None))
        carry_in = jnp.where(source > chip, prod * carry_in + state, carry_in)
    carry_in = jnp.where(bit_of("seq", 0) == 0, mate_ref[0] * carry_in + mate_out_ref[...], carry_in)

    def two_steps(offset, carry):
        arriving, gbias = carry
        pair = span // 2 - 1 - offset
        logits = [None, None]
        cands = [None, None]
        before = held_ref[rows_of(jnp.maximum(pair - 1, 0), 2 * batch), :].astype(F32)[batch:]
        prevs = [
            jnp.where(pair == 0, state_ref[...], before),
            held_ref[rows_of(pair, 2 * batch), :].astype(F32)[:batch],
        ]
        for side in (1, 0):
            here = pl.ds(pl.multiple_of((2 * pair + side) * batch, batch), batch)
            gate = gate_ref[here, :]
            keep = widen(keep_ref[here, :], hidden)
            gstate = gheld_ref[here, :] + arriving
            rest = 1.0 - gate
            cands[side] = gstate * gate
            logits[side] = cands[side] * (cand_ref[here, :] - prevs[side] * keep) * rest
            arriving = rest * keep * gstate
            gbias = gbias + logits[side]
        both = rows_of(pair, 2 * batch)
        gproj_ref[both, :hidden] = jnp.concatenate(logits, axis=0).astype(BF16)
        gproj_ref[both, hidden:] = jnp.concatenate(cands, axis=0).astype(BF16)
        return arriving, gbias

    _, gbias = lax.fori_loop(
        0, span // 2, two_steps, (carry_in, jnp.zeros((batch, hidden), F32)), unroll=8
    )
    gbias_ref[...] = jnp.sum(gbias, axis=0, keepdims=True)
    edge_ref[...] = dot_nt(gproj_ref[: edge_ref.shape[0], :], w_in_ref[...]).astype(BF16)
    odd = bit_of("seq", 0) == 1
    wide_gradient(conv_ref, gproj_ref, stay_ref, send_ref, odd)


def deal(tile, shards, first, stay_ref, send_ref, row, odd):
    size = tile.shape[0] // shards
    for even in range(0, shards, 2):
        pair = [tile[(even + k) * size : (even + k + 1) * size].astype(BF16) for k in range(2)]
        index = (first + even) // 2
        stay_ref[index, row : row + size, :] = jnp.where(odd, pair[1], pair[0])
        send_ref[index, row : row + size, :] = jnp.where(odd, pair[0], pair[1])


def wide_gradient(left_ref, right_ref, stay_ref, send_ref, odd):
    shards = 2 * stay_ref.shape[0]
    width = stay_ref.shape[2]
    size = left_ref.shape[1] // shards
    for part in range(right_ref.shape[1] // width):
        tile = dot_tn(left_ref[...], right_ref[:, part * width : (part + 1) * width])
        deal(tile, shards, 0, stay_ref, send_ref, part * size, odd)


def tall_gradient(left_ref, right_ref, stay_ref, send_ref, odd, block=512):
    shards = 2 * stay_ref.shape[0]
    count = left_ref.shape[1] // block
    for part in range(count):
        tile = dot_tn(left_ref[:, part * block : (part + 1) * block], right_ref[...])
        deal(tile, shards // count, part * (shards // count), stay_ref, send_ref, 0, odd)


def weights_kernel(nmid_ref, gup_ref, act_ref, gt_ref, stay_up, send_up, stay_down, send_down):
    odd = bit_of("seq", 0) == 1
    wide_gradient(nmid_ref, gup_ref, stay_up, send_up, odd)
    tall_gradient(act_ref, gt_ref, stay_down, send_down, odd)


def weights_out_kernel(held_ref, gbranch_ref, stay_ref, send_ref):
    tall_gradient(held_ref, gbranch_ref, stay_ref, send_ref, bit_of("seq", 0) == 1)


def bit_of(axis, bit):
    return lax.shift_right_logical(lax.axis_index(axis), bit) & 1


def chunks(count, size, body):
    def step(index, carry):
        body(pl.ds(pl.multiple_of(index * size, size), size))
        return carry

    lax.fori_loop(0, count // size, step, 0)


def core_sum_kernel(*refs, plan):
    sources, (stay_a, send_a, stay_b, send_b) = refs[:-4], refs[-4:]
    base = 0
    for stay_ref, come_ref in zip(sources[::2], sources[1::2]):
        half = stay_ref.shape[1] // 2
        for out_stay, out_send, first, axis in ((stay_a, send_a, 0, plan[0]), (stay_b, send_b, half, plan[1])):
            low = 1 << axis
            for group in range(out_stay.shape[0]):
                fixed = (group >> axis) * 2 * low + (group & (low - 1))
                mine = fixed + low * bit_of("seq", axis + 1)
                other = fixed + low * (1 - bit_of("seq", axis + 1))

                def body(rows):
                    source = pl.ds(pl.multiple_of(rows.start + first, 16), rows.size)
                    goal = pl.ds(pl.multiple_of(rows.start + base, 16), rows.size)
                    out_stay[group, goal, :] = stay_ref[mine, source, :].astype(F32) + come_ref[
                        mine, source, :
                    ].astype(F32)
                    out_send[group, goal, :] = (
                        stay_ref[other, source, :].astype(F32) + come_ref[other, source, :].astype(F32)
                    ).astype(BF16)

                chunks(half, 16, body)
        base += half


def split_sum_kernel(*refs, plan, counts):
    ins = 2 * sum(counts)
    outs = refs[ins:]
    source = 0
    for part, (which, axis) in enumerate(plan):
        out_stay, out_send = outs[2 * part], outs[2 * part + 1]
        low = 1 << axis
        base = 0
        for pair in range(counts[part]):
            stay_ref, come_ref = refs[source], refs[source + 1]
            source += 2
            for group in range(out_stay.shape[0]):
                fixed = (group >> axis) * 2 * low + (group & (low - 1))
                mine = fixed + low * bit_of("seq", which + 1)
                other = fixed + low * (1 - bit_of("seq", which + 1))

                def body(rows):
                    goal = pl.ds(pl.multiple_of(rows.start + base, 16), rows.size)
                    out_stay[group, goal, :] = stay_ref[mine, rows, :].astype(F32) + come_ref[
                        mine, rows, :
                    ].astype(F32)
                    out_send[group, goal, :] = (
                        stay_ref[other, rows, :].astype(F32) + come_ref[other, rows, :].astype(F32)
                    ).astype(BF16)

                chunks(stay_ref.shape[1], 16, body)
            base += stay_ref.shape[1]


def join_sum_kernel(stay_a, come_a, stay_b, come_b, out_stay, out_send):
    width = out_stay.shape[1]
    here = pl.ds(pl.multiple_of(bit_of("dp", 0) * width, width), width)
    there = pl.ds(pl.multiple_of((1 - bit_of("dp", 0)) * width, width), width)
    for stay_ref, come_ref, base in ((stay_a, come_a, 0), (stay_b, come_b, stay_a.shape[1])):

        def body(rows):
            goal = pl.ds(pl.multiple_of(rows.start + base, 16), rows.size)
            out_stay[goal, :] = stay_ref[0, rows, here] + come_ref[0, rows, here].astype(F32)
            out_send[goal, :] = (
                stay_ref[0, rows, there] + come_ref[0, rows, there].astype(F32)
            ).astype(BF16)

        chunks(stay_ref.shape[1], 16, body)


def column_sum_kernel(stay_ref, come_ref, out_stay, out_send, *, bit):
    width = out_stay.shape[1]
    here = pl.ds(pl.multiple_of(bit_of("dp", bit) * width, width), width)
    there = pl.ds(pl.multiple_of((1 - bit_of("dp", bit)) * width, width), width)

    def body(rows):
        out_stay[rows, :] = stay_ref[rows, here] + come_ref[rows, here].astype(F32)
        out_send[rows, :] = (stay_ref[rows, there] + come_ref[rows, there].astype(F32)).astype(BF16)

    chunks(out_stay.shape[0], 16, body)


def round_sum_kernel(stay_ref, come_ref, out_ref):
    def body(rows):
        out_ref[rows, :] = (stay_ref[rows, :].astype(F32) + come_ref[rows, :].astype(F32)).astype(BF16)

    chunks(out_ref.shape[0], 16, body)


def taps_kernel(
    gconv_ref, after_ref, ahead_ref, xt_ref, normed_ref, halo_ref, across_ref, taps_ref, gnorm2_ref, gbias_ref,
    gnormed_ref, stay_ref, send_ref, norm_buf, gconv_buf,
    *, steps,
):
    tokens, width = gconv_ref.shape
    batch = halo_ref.shape[0] // EDGE
    size = steps * batch
    lead = EDGE * batch
    norm_buf[:lead, :] = pick_edge(halo_ref[...], across_ref[...], False)
    gconv_buf[tokens : tokens + after_ref.shape[0], :] = pick_edge(after_ref[...], ahead_ref[...], True)

    def spread(index, carry):
        rows = rows_of(index, size)
        norm_buf[pl.ds(pl.multiple_of(index * size + lead, 8), size), :] = normed_ref[rows, :].astype(F32)
        gconv_buf[rows, :] = gconv_ref[rows, :].astype(F32)
        return carry

    lax.fori_loop(0, tokens // size, spread, 0)

    def chunk(index, carry):
        gnorm1, gtaps = carry
        rows = rows_of(index, size)
        here = gconv_buf[rows, :]
        gnormed = here * taps_ref[0:1, :]
        sums = []
        for tap in range(KW):
            if tap:
                later = pl.ds(pl.multiple_of(index * size + tap * batch, 8), size)
                gnormed = gnormed + gconv_buf[later, :] * taps_ref[tap : tap + 1, :]
            earlier = pl.ds(pl.multiple_of(index * size + lead - tap * batch, 8), size)
            sums.append(gtaps[tap] + jnp.sum(norm_buf[earlier, :] * here, axis=0, keepdims=True))
        gnormed_ref[rows, :] = gnormed
        values = read(xt_ref, rows)
        gnorm1 = gnorm1 + jnp.sum(gnormed * (values * rms(values)), axis=0, keepdims=True)
        return gnorm1, tuple(sums)

    zero = jnp.zeros((1, width), F32)
    gnorm1, gtaps = lax.fori_loop(0, tokens // size, chunk, (zero, (zero,) * KW))
    places = 2 * stay_ref.shape[0]
    odd = bit_of("seq", 0) == 1
    rows = []
    for place in range(places):
        parts = [
            vector[:, place * (vector.shape[1] // places) : (place + 1) * (vector.shape[1] // places)]
            for vector in (gnorm1, gnorm2_ref[...], *gtaps, gbias_ref[...])
        ]
        row = jnp.concatenate(parts, axis=1)
        if row.shape[1] < width:
            row = jnp.concatenate([row, jnp.zeros((1, width - row.shape[1]), F32)], axis=1)
        rows.append(jnp.broadcast_to(row, (stay_ref.shape[1], width)))
    for index in range(places // 2):
        pair = rows[2 * index : 2 * index + 2]
        stay_ref[index] = jnp.where(odd, pair[1], pair[0]).astype(BF16)
        send_ref[index] = jnp.where(odd, pair[0], pair[1]).astype(BF16)


def inputs_kernel(gnormed_ref, xt_ref, gmid_ref, gain_ref, ginput_ref, wide_buf, *, steps):
    batch, span, width = ginput_ref.shape
    gain = gain_ref[...]

    def chunk(index, carry):
        rows = rows_of(index, steps * batch)
        values = read(xt_ref, rows)
        scale = rms(values)
        unit = values * scale
        pulled = gnormed_ref[rows, :] * gain
        ginput = gmid_ref[rows, :] + scale * (
            pulled - unit * jnp.mean(pulled * unit, axis=-1, keepdims=True)
        )
        write(wide_buf, rows, ginput)
        return carry

    lax.fori_loop(0, span // steps, chunk, 0)
    for row in range(batch):
        ginput_ref[row] = deinterleave(wide_buf, row, batch, span)


def finish_kernel(total_ref, come_ref, *outs, sizes):
    wide = total_ref.shape[1]
    width = 2 * wide
    half = sum(sizes) // 2
    if len(outs) > len(sizes):
        low = bit_of("dp", 0) == 0
        mine, other = [ref[half : half + SMALL, :].astype(F32) for ref in (total_ref, come_ref)]
        row = jnp.concatenate([jnp.where(low, mine, other), jnp.where(low, other, mine)], axis=1)
        column = 0
        for out in outs[len(sizes) :]:
            for line in range(out.shape[0]):
                out[line : line + 1, :] = row[0:1, column : column + out.shape[1]]
                column += out.shape[1]
    for source, bit in ((total_ref, bit_of("dp", 0)), (come_ref, 1 - bit_of("dp", 0))):
        for part_b in range(2):
            row = part_b * (total_ref.shape[0] - half)
            for out, rows in zip(outs, sizes):
                size = out.shape[0]
                count = min(size, rows // 2)
                for start in range(part_b * rows // 2, (part_b + 1) * rows // 2, count):
                    part, low_row = start // size, start % size
                    cols = pl.ds(pl.multiple_of(part * width + bit * wide, wide), wide)
                    out[low_row : low_row + count, cols] = source[row : row + count, :].astype(F32)
                    row += count


def call(
    kernel, name, out_shapes, in_specs, args, scratch=(), limit=2, after=(), work=1
):
    ins, outs = len(args), len(out_shapes)

    def body(*refs):
        inner = list(refs[:ins])
        rest = refs[ins:]
        rest = rest[len(after) :]
        inner += rest[:outs]
        rest = rest[outs:]
        if name in FINAL:
            rest[0][...] = jnp.zeros((8, LANES), F32)
            rest = rest[1:]
        kernel(*inner, *rest)

    args, in_specs, out_shapes = list(args), list(in_specs), list(out_shapes)
    if name in FINAL:
        out_shapes.append(((8, LANES), F32))
    args += after
    in_specs += [pl.BlockSpec(memory_space=pl.ANY)] * len(after)
    return pl.pallas_call(
        body,
        name=name,
        out_shape=[
            (pltpu.HBM if name in FINAL and index < outs else jax.ShapeDtypeStruct)(shape, kind)
            for index, (shape, kind) in enumerate(out_shapes)
        ],
        in_specs=in_specs,
        out_specs=[VMEM_SPEC] * len(out_shapes),
        scratch_shapes=list(scratch),
        compiler_params=pltpu.CompilerParams(vmem_limit_bytes=limit * 2**20),
        cost_estimate=pl.CostEstimate(flops=work, bytes_accessed=1, transcendentals=0),
    )(*args)


def neighbour(block, axis):
    count = lax.axis_size(axis)
    inside = swap_by(block, axis, 1)
    across = lax.ppermute(block, axis, [(i, (i + 1 if i % 2 else i - 1) % count) for i in range(count)])
    return inside, across


def pick_edge(inside, across, ahead):
    place = lax.axis_index("seq")
    end = lax.axis_size("seq") - 1 if ahead else 0
    odd = bit_of("seq", 0) == 1
    value = jnp.where(odd != ahead, inside.astype(F32), across.astype(F32))
    return jnp.where(place == end, jnp.zeros_like(value), value)


def swap_by(block, axis, mask):
    return lax.ppermute(block, axis, [(i, i ^ mask) for i in range(lax.axis_size(axis))])


def swap(block, axis, bit):
    return swap_by(block, axis, 1 << bit)


class Order:
    def __init__(self):
        self.last = ()

    def call(self, *args, **kwargs):
        kwargs.setdefault("work", WORK.get(args[1], 1))
        outs = list(call(*args, **kwargs, after=self.last))
        self.last = (min(outs, key=lambda out: out.size * out.dtype.itemsize),)
        if args[1] in FINAL:
            outs.pop()
        return outs


def spread_sum(order, name, sources, out_shapes, late=()):
    places, _, width = sources[0][0].shape
    sizes = tuple(stay.shape[1] for stay, _ in sources)
    rows = sum(sizes)
    levels = places.bit_length() - 1
    order_a = list(range(levels))
    order_b = order_a[::-1]
    half = rows // 2

    def shapes(count, more=0):
        out = []
        for part in (half + more, half):
            out += [((count, part, width), F32), ((count, part, width), BF16)]
        return out

    stay_a, send_a, stay_b, send_b = order.call(
        functools.partial(core_sum_kernel, plan=(order_a[0], order_b[0])), name + "_core",
        shapes(places // 2), [VMEM_SPEC] * (2 * len(sources)), [part for pair in sources for part in pair],
        limit=1,
    )
    for level in range(levels):
        come_a = swap(send_a, "seq", order_a[level] + 1)
        come_b = swap(send_b, "seq", order_b[level] + 1)
        yield None
        if level + 1 == levels:
            break
        plan = []
        for bits in (order_a, order_b):
            bit = bits[level + 1]
            plan.append((bit, bit - sum(done < bit for done in bits[: level + 1])))
        sources = [stay_a, come_a, *(late if level == 0 else ()), stay_b, come_b]
        more = SMALL if late else 0
        stay_a, send_a, stay_b, send_b = order.call(
            functools.partial(
                split_sum_kernel, plan=tuple(plan), counts=(2 if late and level == 0 else 1, 1)
            ),
            name + "_seq", shapes(places // 4 >> level, more), [VMEM_SPEC] * len(sources), sources,
        )
    rows += SMALL if late else 0
    depth = lax.axis_size("dp").bit_length() - 1
    wide = width // 2
    stay, send = order.call(
        join_sum_kernel, name + "_join", [((rows, wide), F32), ((rows, wide), BF16)],
        [VMEM_SPEC] * 4, (stay_a, come_a, stay_b, come_b),
    )
    for bit in range(1, depth - 1):
        wide = wide // 2
        come = swap(send, "dp", bit - 1)
        yield None
        stay, send = order.call(
            functools.partial(column_sum_kernel, bit=bit), name + "_dp",
            [((rows, wide), F32), ((rows, wide), BF16)], [VMEM_SPEC] * 2,
            (stay, come),
        )
    come = swap(send, "dp", depth - 2)
    yield None
    (low,) = order.call(
        round_sum_kernel, name + "_last", [((rows, wide), BF16)], [VMEM_SPEC] * 2, (stay, come)
    )
    come = swap(low, "dp", depth - 1)
    yield None
    (total,) = order.call(
        round_sum_kernel, name + "_total", [((rows, wide), BF16)], [VMEM_SPEC] * 2, (low, come)
    )
    for bit in range(depth - 2, 0, -1):
        come = swap(total, "dp", bit)
        upper = bit_of("dp", bit) == 1
        total = jnp.concatenate(
            [jnp.where(upper, come, total), jnp.where(upper, total, come)], axis=1
        )
    come = swap(total, "dp", 0)
    yield None
    yield order.call(
        functools.partial(finish_kernel, sizes=sizes), name + "_finish", [(shape, F32) for shape in out_shapes],
        [VMEM_SPEC] * 2, (total, come),
    )


def on_device(
    inputs, doc_start, norm1_gain, conv_weight, gate_bias, w_in, w_out, norm2_gain, w_up, w_down, out_grad
):
    batch, span, width = inputs.shape
    hidden = w_out.shape[0]
    inner = w_up.shape[1]
    tokens = batch * span
    lanes = width // LANES
    seq_count, dp_count = lax.axis_size("seq"), lax.axis_size("dp")
    seq_depth, dp_depth = seq_count.bit_length() - 1, dp_count.bit_length() - 1
    pairs = seq_count // 2
    seq_at = lax.axis_index("seq").astype(jnp.int32)
    taps = jnp.transpose(conv_weight)
    gain1, gain2, bias = norm1_gain[None], norm2_gain[None], gate_bias[None]
    order = Order()

    xt, normed, edge, keep = order.call(
        functools.partial(ingest_kernel, steps=span), "ingest",
        [
            ((lanes, tokens, LANES), F32), ((tokens, width), BF16), ((EDGE * batch, width), BF16),
            ((tokens, LANES), F32),
        ],
        [pl.BlockSpec(memory_space=pltpu.HBM)] * 3,
        [pltpu.with_memory_space_constraint(part, pltpu.HBM) for part in (inputs, doc_start, gain1)],
        [
            pltpu.VMEM((batch, span, width), BF16), pltpu.VMEM((batch, span), jnp.int32),
            pltpu.VMEM((1, width), F32), pltpu.SemaphoreType.DMA((batch + 2,)),
        ],
        limit=LIMITS["ingest"],
    )
    halo = neighbour(edge, "seq")
    gt, gact = order.call(
        functools.partial(prepare_kernel, steps=span, block=256), "prepare",
        [((tokens, width), BF16), ((tokens, inner // 2), BF16)],
        [VMEM_SPEC] * 2, (out_grad, w_down), [pltpu.VMEM((lanes, tokens, LANES), F32)],
        limit=LIMITS["prepare"],
    )
    conv_out, gate, cand, totals = order.call(
        functools.partial(front_kernel, steps=span, block=256), "front",
        [
            ((tokens, width), BF16), ((tokens, hidden), F32), ((tokens, hidden), F32),
            ((2, batch, hidden), F32),
        ],
        [VMEM_SPEC] * 7, (normed, *halo, keep, taps, bias, w_in),
        [pltpu.VMEM((tokens + EDGE * batch, width), F32)],
        limit=LIMITS["front"],
    )
    chips = seq_count // 2
    mate_totals = swap(totals, "seq", 0)
    (chip_totals,) = order.call(
        chip_totals_kernel, "chip_totals", [(totals.shape, F32)], [VMEM_SPEC] * 2, (totals, mate_totals)
    )
    all_totals = [swap_by(chip_totals, "seq", 2 * mask) for mask in range(1, chips)]
    (more,) = order.call(
        functools.partial(prepare_rest_kernel, size=tokens, block=256), "prepare_rest",
        [((tokens, inner // 2), BF16)], [VMEM_SPEC] * 2, (gt, w_down), limit=LIMITS["prepare_rest"],
    )
    state_in, held, mid, nmid, act, gup = order.call(
        functools.partial(forward_kernel, chips=chips, steps=span, block=256), "forward",
        [
            ((batch, hidden), F32), ((tokens, hidden), BF16), ((tokens, width), F32),
            ((tokens, width), BF16), ((tokens, inner), BF16), ((tokens, inner), BF16),
        ],
        [VMEM_SPEC] * (9 + chips),
        (mate_totals, *all_totals, xt, keep, gate, cand, gact, more, gain2, w_out, w_up),
        limit=LIMITS["forward"],
    )
    up_rows = inner // seq_count
    stay_up, send_up, stay_down, send_down = order.call(
        weights_kernel, "weights", [((pairs, up_rows, width), BF16)] * 4,
        [VMEM_SPEC] * 4, (nmid, gup, act, gt), limit=LIMITS["weights"],
    )
    come_up, come_down = swap(send_up, "seq", 0), swap(send_down, "seq", 0)
    gmid, gbranch, gheld, outgoing, gnorm2 = order.call(
        functools.partial(reverse_kernel, steps=span), "reverse",
        [
            ((tokens, width), F32), ((tokens, width), BF16), ((tokens, hidden), F32),
            ((batch, hidden), F32), ((1, width), F32),
        ],
        [VMEM_SPEC] * 8, (gup, mid, gt, gain2, keep, gate, w_out, w_up),
        limit=LIMITS["reverse"],
    )
    mate_outgoing = swap(outgoing, "seq", 0)
    out_rows = hidden // seq_count
    in_rows = 2 * hidden // seq_count
    stay_out, send_out = order.call(
        weights_out_kernel, "weights_out", [((pairs, out_rows, width), BF16)] * 2,
        [VMEM_SPEC] * 2, (held, gbranch), limit=LIMITS["weights"],
    )
    come_out = swap(send_out, "seq", 0)
    (chip_outgoing,) = order.call(
        chip_outgoing_kernel, "chip_outgoing", [(outgoing.shape, F32)], [VMEM_SPEC] * 4,
        (outgoing, mate_outgoing, totals, mate_totals),
    )
    all_outgoing = [swap_by(chip_outgoing, "seq", 2 * mask) for mask in range(1, chips)]
    first = spread_sum(
        order, "first", [(stay_up, come_up), (stay_down, come_down)],
        [(width // seq_count, inner), (up_rows, width)],
    )
    next(first)
    gproj, gbias, gconv_edge, stay_in, send_in = order.call(
        functools.partial(back_kernel, chips=chips), "back",
        [((tokens, 2 * hidden), BF16), ((1, hidden), F32), ((EDGE * batch, width), BF16)]
        + [((pairs, in_rows, width), BF16)] * 2,
        [VMEM_SPEC] * (8 + 2 * chips),
        (
            *all_totals, *all_outgoing, mate_totals, mate_outgoing, keep, gate, cand, state_in, held, gheld, conv_out, w_in,
        ),
        limit=LIMITS["back"],
    )
    after = neighbour(gconv_edge, "seq")
    come_in = swap(send_in, "seq", 0)
    (gconv,) = order.call(
        functools.partial(gconv_kernel, steps=span), "gconv", [((tokens, width), BF16)],
        [VMEM_SPEC] * 2, (gproj, w_in), limit=LIMITS["gconv"],
    )
    order.last = (*order.last, after[0])
    late = []
    share = width // seq_count
    second = spread_sum(
        order, "second", [(stay_in, come_in), (stay_out, come_out)],
        [
            (share, 2 * hidden), (out_rows, width), (1, share), (1, share), (KW, share),
            (1, hidden // seq_count),
        ],
        late,
    )
    next(first)
    gnormed, stay_small, send_small = order.call(
        functools.partial(taps_kernel, steps=16), "taps",
        [((tokens, width), F32)] + [((pairs, SMALL, width), BF16)] * 2, [VMEM_SPEC] * 10,
        (gconv, *after, xt, normed, *halo, taps, gnorm2, gbias),
        [
            pltpu.VMEM((tokens + EDGE * batch, width), F32),
            pltpu.VMEM((tokens + EDGE * batch, width), F32),
        ],
        limit=LIMITS["taps"],
    )
    come_small = swap(send_small, "seq", 0)
    next(second)
    next(first)
    stay_small, send_small = order.call(
        functools.partial(split_sum_kernel, plan=((0, 0),), counts=(1,)), "small",
        [((pairs // 2, SMALL, width), F32), ((pairs // 2, SMALL, width), BF16)], [VMEM_SPEC] * 2,
        (stay_small, come_small),
    )
    late += [stay_small, swap(send_small, "seq", 1)]
    (result,) = order.call(
        functools.partial(result_kernel, steps=span), "result", [((batch, span, width), BF16)],
        [VMEM_SPEC] * 3, (act, mid, w_down), [pltpu.VMEM((lanes, tokens, LANES), F32)],
        limit=LIMITS["result"],
    )
    next(second)
    next(first)
    next(second)
    (ginput,) = order.call(
        functools.partial(inputs_kernel, steps=64), "inputs", [((batch, span, width), F32)],
        [VMEM_SPEC] * 4, (gnormed, xt, gmid, gain1), [pltpu.VMEM((lanes, tokens, LANES), F32)],
        limit=LIMITS["inputs"],
    )
    next(first)
    next(second)
    done = {}
    while len(done) < 2:
        for part in (second, first):
            if part not in done:
                outs = next(part)
                if outs is not None:
                    done[part] = outs
    gw_up, gw_down = done[first]
    gw_in, gw_out, gnorm1, gnorm2, gtaps, gbias = done[second]
    return (
        result, ginput, gnorm1[0], jnp.transpose(gtaps), gbias[0], gw_in, gw_out, gnorm2[0], gw_up, gw_down,
    )


def solution(mesh):
    rows, flat = P("dp", "seq", None), P()
    in_specs = (rows, P("dp", "seq")) + (flat,) * 8 + (rows,)
    vec, mat = P("seq"), P("seq", None)
    out_specs = (rows, rows, vec, mat, vec, mat, mat, vec, mat, mat)
    return jax.shard_map(
        on_device, mesh=mesh, in_specs=in_specs, out_specs=out_specs, check_vma=False
    )
```
